32 devices in a mesh: section: 4 (over x, core), dp: 8 (over z, y).
Axes of the slice: x: 2, y: 2, z: 4, core: 2. Of those that a mesh axis runs over, the one named last changes fastest.
Arguments:
- observations: bfloat16 [4, 1024, 39], P(None, 'dp'), may hold values from -6 to 6
- actions: bfloat16 [3, 4, 1024, 6], P(None, None, 'dp'), may hold values from -1 to 1
- action_mask: int32 [80, 6], replicated, may hold values 0 or 1
- task_ids: int32 [4, 1024], P(None, 'dp'), may hold values from 0 to 79
- targets: bfloat16 [3, 4, 1024, 512], P(None, None, 'dp'), may hold values from 0 to 0.25
- bin_low: int32 [3, 4, 1024], P(None, None, 'dp'), may hold values from 0 to 99
- bin_frac: float32 [3, 4, 1024], P(None, None, 'dp'), may hold values from 0 to 1
- task_table: bfloat16 [80, 96], replicated, may hold values from -1.796875 to 1.796875
- encoder_first: bfloat16 [135, 1024], replicated, may hold values from -0.5 to 0.5
- encoder_first_gain: bfloat16 [1024], replicated, may hold values from 0.5 to 1.5
- encoder_first_shift: bfloat16 [1024], replicated, may hold values from -1 to 1
- encoder_second: bfloat16 [1024, 512], replicated, may hold values from -0.1875 to 0.1875
- encoder_second_gain: bfloat16 [512], replicated, may hold values from 0.5 to 1.5
- encoder_second_shift: bfloat16 [512], replicated, may hold values from -1 to 1
- dynamics_first: bfloat16 [614, 1024], replicated, may hold values from -0.25 to 0.25
- dynamics_first_gain: bfloat16 [1024], replicated, may hold values from 0.5 to 1.5
- dynamics_first_shift: bfloat16 [1024], replicated, may hold values from -1 to 1
- dynamics_second: bfloat16 [1024, 1024], replicated, may hold values from -0.1875 to 0.1875
- dynamics_second_gain: bfloat16 [1024], replicated, may hold values from 0.5 to 1.5
- dynamics_second_shift: bfloat16 [1024], replicated, may hold values from -1 to 1
- dynamics_third: bfloat16 [1024, 512], replicated, may hold values from -0.1875 to 0.1875
- dynamics_third_gain: bfloat16 [512], replicated, may hold values from 0.5 to 1.5
- dynamics_third_shift: bfloat16 [512], replicated, may hold values from -1 to 1
- value_first: bfloat16 [5, 614, 1024], replicated, may hold values from -0.25 to 0.25
- value_first_gain: bfloat16 [5, 1024], replicated, may hold values from 0.5 to 1.5
- value_first_shift: bfloat16 [5, 1024], replicated, may hold values from -1 to 1
- value_second: bfloat16 [5, 1024, 1024], replicated, may hold values from -0.1875 to 0.1875
- value_second_gain: bfloat16 [5, 1024], replicated, may hold values from 0.5 to 1.5
- value_second_shift: bfloat16 [5, 1024], replicated, may hold values from -1 to 1
- value_third: bfloat16 [5, 1024, 101], replicated, may hold values from -0.1875 to 0.1875
- value_bias: bfloat16 [5, 101], replicated, may hold values from -3 to 3
Outputs:
- observations_gradient: float32 [4, 1024, 39], P('section', 'dp')
- task_table_gradient: float32 [80, 96], replicated
- encoder_first_gradient: float32 [135, 1024], P(None, 'dp')
- encoder_first_gain_gradient: float32 [1024], replicated
- encoder_first_shift_gradient: float32 [1024], replicated
- encoder_second_gradient: float32 [1024, 512], P('dp')
- encoder_second_gain_gradient: float32 [512], replicated
- encoder_second_shift_gradient: float32 [512], replicated
- dynamics_first_gradient: float32 [614, 1024], P(None, 'dp')
- dynamics_first_gain_gradient: float32 [1024], replicated
- dynamics_first_shift_gradient: float32 [1024], replicated
- dynamics_second_gradient: float32 [1024, 1024], P('dp')
- dynamics_second_gain_gradient: float32 [1024], replicated
- dynamics_second_shift_gradient: float32 [1024], replicated
- dynamics_third_gradient: float32 [1024, 512], P('dp')
- dynamics_third_gain_gradient: float32 [512], replicated
- dynamics_third_shift_gradient: float32 [512], replicated
- value_first_gradient: float32 [5, 614, 1024], P(None, None, 'dp')
- value_first_gain_gradient: float32 [5, 1024], replicated
- value_first_shift_gradient: float32 [5, 1024], replicated
- value_second_gradient: float32 [5, 1024, 1024], P(None, 'dp')
- value_second_gain_gradient: float32 [5, 1024], replicated
- value_second_shift_gradient: float32 [5, 1024], replicated
- value_third_gradient: float32 [5, 1024, 101], P(None, 'dp')
- value_bias_gradient: float32 [5, 101], replicated
The draws below stay inside these ranges and needn't reach their ends.
All inputs are finite; a program needn't handle non-finite values.
Results may differ from the reference program's by a relative error of at most 0.018.
Values may be sent and summed in bfloat16 or wider, within the bound.
A program may use at most 576 MiB of HBM per device.

```python
import jax
import jax.numpy as jnp
from jax import lax

OBS = 39
TASK_DIM = 96
TASKS = 80
ACT = 6
LAT = 512
ENC = 1024
MLP = 1024
NQ = 5
BINS = 101
SIMNORM = 8
HOR = 3
MICRO = 4
BATCH = 1024


def place_ends(values, own_key, least, high):
    index_at = [jax.random.randint(jax.random.fold_in(own_key, axis), (), 0, length) for axis, length in enumerate(values.shape)]
    main_axis = values.shape.index(max(values.shape))
    next_to = index_at[:main_axis] + [(index_at[main_axis] + 1) % values.shape[main_axis]] + index_at[main_axis + 1:]
    return values.at[tuple(index_at)].set(least).at[tuple(next_to)].set(high)


def steps_of(own_key, extent, cuts, least, high):
    def one(axis_at, blocks):
        draws = jax.random.uniform(jax.random.fold_in(jax.random.fold_in(own_key, 6), axis_at), (blocks,), jnp.float32, least / len(cuts), high / len(cuts))
        return jnp.repeat(jnp.exp(draws), extent[axis_at] // blocks).reshape((-1,) + (1,) * (len(extent) - axis_at - 1))

    loudness = one(*cuts[0])
    for cut in cuts[1:]:
        loudness = loudness * one(*cut)
    return loudness


def noise(own_key, shape, deviation, bound, pieces=(), kind=jnp.bfloat16):
    level = steps_of(own_key, shape, pieces, -0.22, 0.18) if pieces else 1.0
    entries = jax.random.normal(own_key, shape, jnp.float32) * deviation * level
    return jnp.minimum(jnp.maximum(entries, -bound), bound).astype(kind)


def setup_inputs(seed: int = 0) -> dict:
    streams_of = jax.random.split(jax.random.key(seed), 32)
    return {
        "observations": noise(streams_of[0], (MICRO, BATCH, OBS), 1.0, 6.0, ((1, 8),)),
        "actions": jnp.clip(jax.random.uniform(streams_of[1], (HOR, MICRO, BATCH, ACT), jnp.float32, -1.0, 1.0) * steps_of(streams_of[1], (HOR, MICRO, BATCH, ACT), ((2, 8),), -0.4, 0.0), -1.0, 1.0).astype(jnp.bfloat16),
        "action_mask": place_ends((jax.random.randint(streams_of[2], (TASKS, ACT), 0, 4) < 3).astype(jnp.int32), jax.random.fold_in(streams_of[2], 1), 0, 1),
        "task_ids": place_ends(jax.random.randint(streams_of[3], (MICRO, BATCH), 0, TASKS), jax.random.fold_in(streams_of[3], 1), 0, TASKS - 1).astype(jnp.int32),
        "targets": jnp.clip(0.25 * jax.random.uniform(streams_of[4], (HOR, MICRO, BATCH, LAT), jnp.float32) ** steps_of(streams_of[4], (HOR, MICRO, BATCH, LAT), ((2, 8),), -0.2, 0.2), 0.0, 0.25).astype(jnp.bfloat16),
        "bin_low": place_ends(jax.random.randint(streams_of[5], (HOR, MICRO, BATCH), 0, BINS - 1), jax.random.fold_in(streams_of[5], 1), 0, (BINS - 1) - 1).astype(jnp.int32),
        "bin_frac": jnp.clip(1.0 * jax.random.uniform(streams_of[6], (HOR, MICRO, BATCH), jnp.float32) ** steps_of(streams_of[6], (HOR, MICRO, BATCH), ((2, 8),), -0.2, 0.2), 0.0, 1.0),
        "task_table": noise(streams_of[7], (TASKS, TASK_DIM), 0.3, 1.796875),
        "encoder_first": noise(streams_of[8], (OBS + TASK_DIM, ENC), (OBS + TASK_DIM) ** -0.5, 0.5),
        "encoder_first_gain": jnp.clip(1.0 + 0.1 * jax.random.normal(streams_of[9], (ENC,), jnp.float32), 0.5, 1.5).astype(jnp.bfloat16),
        "encoder_first_shift": noise(streams_of[10], (ENC,), 0.2, 1.0),
        "encoder_second": noise(streams_of[11], (ENC, LAT), ENC ** -0.5, 0.1875),
        "encoder_second_gain": jnp.clip(1.0 + 0.1 * jax.random.normal(streams_of[12], (LAT,), jnp.float32), 0.5, 1.5).astype(jnp.bfloat16),
        "encoder_second_shift": noise(streams_of[13], (LAT,), 0.2, 1.0),
        "dynamics_first": noise(streams_of[14], (LAT + ACT + TASK_DIM, MLP), (LAT + ACT + TASK_DIM) ** -0.5, 0.25),
        "dynamics_first_gain": jnp.clip(1.0 + 0.1 * jax.random.normal(streams_of[15], (MLP,), jnp.float32), 0.5, 1.5).astype(jnp.bfloat16),
        "dynamics_first_shift": noise(streams_of[16], (MLP,), 0.2, 1.0),
        "dynamics_second": noise(streams_of[17], (MLP, MLP), MLP ** -0.5, 0.1875),
        "dynamics_second_gain": jnp.clip(1.0 + 0.1 * jax.random.normal(streams_of[18], (MLP,), jnp.float32), 0.5, 1.5).astype(jnp.bfloat16),
        "dynamics_second_shift": noise(streams_of[19], (MLP,), 0.2, 1.0),
        "dynamics_third": noise(streams_of[20], (MLP, LAT), MLP ** -0.5, 0.1875),
        "dynamics_third_gain": jnp.clip(1.0 + 0.1 * jax.random.normal(streams_of[21], (LAT,), jnp.float32), 0.5, 1.5).astype(jnp.bfloat16),
        "dynamics_third_shift": noise(streams_of[22], (LAT,), 0.2, 1.0),
        "value_first": noise(streams_of[23], (NQ, LAT + ACT + TASK_DIM, MLP), (LAT + ACT + TASK_DIM) ** -0.5, 0.25),
        "value_first_gain": jnp.clip(1.0 + 0.1 * jax.random.normal(streams_of[24], (NQ, MLP), jnp.float32), 0.5, 1.5).astype(jnp.bfloat16),
        "value_first_shift": noise(streams_of[25], (NQ, MLP), 0.2, 1.0),
        "value_second": noise(streams_of[26], (NQ, MLP, MLP), MLP ** -0.5, 0.1875),
        "value_second_gain": jnp.clip(1.0 + 0.1 * jax.random.normal(streams_of[27], (NQ, MLP), jnp.float32), 0.5, 1.5).astype(jnp.bfloat16),
        "value_second_shift": noise(streams_of[28], (NQ, MLP), 0.2, 1.0),
        "value_third": noise(streams_of[29], (NQ, MLP, BINS), MLP ** -0.5, 0.1875),
        "value_bias": noise(streams_of[30], (NQ, BINS), 0.5, 3.0),
    }


epsilon = 1e-05
discount = 0.5
consistency_weight = 20.0
value_weight = 0.1
highest = lax.Precision.HIGHEST

@jax.custom_vjp
def low(v):
    return lax.optimization_barrier(v.astype(jnp.bfloat16)).astype(jnp.float32)

@jax.custom_vjp
def low_back(v):
    return v

def low_keep(v):
    return (low(v), None)

def low_pass(kept, grad):
    return (grad,)

def back_keep(v):
    return (v, None)

def back_low(kept, grad):
    return (low(grad),)
low.defvjp(low_keep, low_pass)
low_back.defvjp(back_keep, back_low)

def mish_curve(values):
    return values * jnp.tanh(jax.nn.softplus(values))

def layer_norm(before, gain_vec, shift_vec):
    center = before - lax.optimization_barrier(jnp.mean(before, -1, keepdims=True))
    spread = lax.optimization_barrier(jnp.mean(center * center, -1, keepdims=True))
    return center * lax.rsqrt(spread + epsilon) * gain_vec + shift_vec

def sim_norm(values):
    groups = values.reshape(values.shape[:-1] + (values.shape[-1] // SIMNORM, SIMNORM))
    return jax.nn.softmax(groups, -1).reshape(values.shape)

def dense_layer(inputs, weight, gain_vec, shift_vec, after_fn):
    before = low_back(jnp.dot(inputs, weight, precision=highest))
    return after_fn(layer_norm(before, gain_vec, shift_vec))

def value_loss(value_params, inputs, bin_rows, fraction_rows):
    first_matrix, first_gain, first_shift, second_matrix, second_gain, second_shift, third_matrix, bias_vec = value_params
    layer_one = low_back(jnp.einsum('rk,qkn->qrn', inputs, first_matrix, precision=highest))
    layer_one = low(mish_curve(layer_norm(layer_one, first_gain[:, None, :], first_shift[:, None, :])))
    layer_two = low_back(jnp.einsum('qrk,qkn->qrn', layer_one, second_matrix, precision=highest))
    layer_two = low(mish_curve(layer_norm(layer_two, second_gain[:, None, :], second_shift[:, None, :])))
    logits = low_back(jnp.einsum('qrk,qkn->qrn', layer_two, third_matrix, precision=highest)) + bias_vec[:, None, :]
    log_probs = jax.nn.log_softmax(logits, -1)
    columns = jnp.arange(logits.shape[2], dtype=jnp.int32)[None, :]
    lower_bin = bin_rows[:, None]
    target = (1.0 - fraction_rows)[:, None] * (columns == lower_bin).astype(jnp.float32) + fraction_rows[:, None] * (columns == lower_bin + 1).astype(jnp.float32)
    return -jnp.sum(log_probs * target[None]) / logits.shape[0]

def reference(observations, actions, action_mask, task_ids, targets, bin_low, bin_frac, task_table, encoder_first, encoder_first_gain, encoder_first_shift, encoder_second, encoder_second_gain, encoder_second_shift, dynamics_first, dynamics_first_gain, dynamics_first_shift, dynamics_second, dynamics_second_gain, dynamics_second_shift, dynamics_third, dynamics_third_gain, dynamics_third_shift, value_first, value_first_gain, value_first_shift, value_second, value_second_gain, value_second_shift, value_third, value_bias):
    floats = tuple((item.astype(jnp.float32) for item in (observations, task_table, encoder_first, encoder_first_gain, encoder_first_shift, encoder_second, encoder_second_gain, encoder_second_shift, dynamics_first, dynamics_first_gain, dynamics_first_shift, dynamics_second, dynamics_second_gain, dynamics_second_shift, dynamics_third, dynamics_third_gain, dynamics_third_shift, value_first, value_first_gain, value_first_shift, value_second, value_second_gain, value_second_shift, value_third, value_bias)))
    movement = jnp.moveaxis(actions.astype(jnp.float32), 1, 0)
    goals = jnp.moveaxis(targets.astype(jnp.float32), 1, 0)
    bins_all = jnp.moveaxis(bin_low, 1, 0)
    fractions_all = jnp.moveaxis(bin_frac.astype(jnp.float32), 1, 0)
    allowed_table = action_mask.astype(jnp.float32)

    def loss_fn(observed_all, table, *params):
        encoder_params = params[0:6]
        dynamics_params = params[6:15]
        value_params = params[15:23]

        def one_micro(bundle):
            observed, moves_micro, task_rows, goal_rows, bin_rows, fraction_rows = bundle
            onehot = (task_rows[:, None] == jnp.arange(TASKS, dtype=jnp.int32)[None, :]).astype(jnp.float32)
            embedded = jnp.dot(onehot, table, precision=highest)
            allowed = jnp.dot(onehot, allowed_table, precision=highest)
            chosen = moves_micro * allowed[None]
            hidden = low(dense_layer(jnp.concatenate([observed, embedded], 1), encoder_params[0], encoder_params[1], encoder_params[2], mish_curve))
            latent = dense_layer(hidden, encoder_params[3], encoder_params[4], encoder_params[5], sim_norm)
            running = jnp.zeros((), jnp.float32)
            for t in range(HOR):
                latent_low = low(latent)
                value_inputs = jnp.concatenate([latent_low, chosen[t], embedded], 1)
                running = running + value_weight * discount ** t * value_loss(value_params, value_inputs, bin_rows[t], fraction_rows[t])
                inputs = jnp.concatenate([low_back(latent_low), chosen[t], embedded], 1)
                hidden = low(dense_layer(inputs, dynamics_params[0], dynamics_params[1], dynamics_params[2], mish_curve))
                hidden = low(dense_layer(hidden, dynamics_params[3], dynamics_params[4], dynamics_params[5], mish_curve))
                latent = dense_layer(hidden, dynamics_params[6], dynamics_params[7], dynamics_params[8], sim_norm)
                offset = latent - goal_rows[t]
                running = running + consistency_weight * discount ** t * jnp.sum(offset * offset) / latent.shape[1]
            return running
        per_micro = lax.map(jax.checkpoint(one_micro), (observed_all, movement, task_ids, goals, bins_all, fractions_all))
        return jnp.sum(per_micro) / MICRO
    loss_value, puller = jax.vjp(loss_fn, *floats)
    gradients = puller(jnp.ones_like(loss_value))
    return (gradients[0], gradients[1], gradients[2], gradients[3], gradients[4], gradients[5], gradients[6], gradients[7], gradients[8], gradients[9], gradients[10], gradients[11], gradients[12], gradients[13], gradients[14], gradients[15], gradients[16], gradients[17], gradients[18], gradients[19], gradients[20], gradients[21], gradients[22], gradients[23], gradients[24])
```

```python
import jax
import jax.numpy as jnp
from jax import lax
from jax.sharding import PartitionSpec as P

SIMNORM = 8


epsilon = 1e-05
discount = 0.5
consistency_weight = 20.0
value_weight = 0.1


def mish_curve(values):
    return values * jnp.tanh(jax.nn.softplus(values))


def layer_norm(before, gain_vec, shift_vec):
    center = before - jnp.mean(before, -1, keepdims=True)
    spread = jnp.mean(center * center, -1, keepdims=True)
    return center * lax.rsqrt(spread + epsilon) * gain_vec + shift_vec


def sim_norm(values):
    groups = values.reshape(values.shape[:-1] + (values.shape[-1] // SIMNORM, SIMNORM))
    return jax.nn.softmax(groups, -1).reshape(values.shape)


def post_mish(before, gain_vec, shift_vec):
    return mish_curve(layer_norm(before, gain_vec, shift_vec))


def post_simnorm(before, gain_vec, shift_vec):
    return sim_norm(layer_norm(before, gain_vec, shift_vec))


def head_mish(before, gain_vec, shift_vec):
    return post_mish(before, gain_vec[:, None, :], shift_vec[:, None, :])


def matmul(left_side, right_side):
    return jnp.dot(left_side, right_side, preferred_element_type=jnp.float32)


def left_transposed(left_side, right_side):
    return lax.dot_general(
        left_side, right_side, (((0,), (0,)), ((), ())), preferred_element_type=jnp.float32
    )


def right_transposed(left_side, right_side):
    return lax.dot_general(
        left_side, right_side, (((1,), (1,)), ((), ())), preferred_element_type=jnp.float32
    )


def dense_forward(inputs, weight, gain_vec, shift_vec, after_fn):
    before = matmul(inputs, weight)
    return jax.vjp(after_fn, before, gain_vec.astype(jnp.float32), shift_vec.astype(jnp.float32))


def dense_backward(inputs, weight, puller, upstream):
    delta_before, delta_gain, delta_shift = puller(upstream)
    rounded = delta_before.astype(jnp.bfloat16)
    return (
        right_transposed(rounded, weight),
        left_transposed(inputs, rounded),
        delta_gain,
        delta_shift,
    )


def encoder_forward(encoder_params, observed, embedded):
    inputs = jnp.concatenate([observed, embedded], 1)
    hidden, first_pull = dense_forward(
        inputs, encoder_params[0], encoder_params[1], encoder_params[2], post_mish
    )
    hidden_low = hidden.astype(jnp.bfloat16)
    latent, second_pull = dense_forward(
        hidden_low, encoder_params[3], encoder_params[4], encoder_params[5], post_simnorm
    )
    return (latent, (inputs, hidden_low, first_pull, second_pull))


def encoder_backward(encoder_params, retained, upstream):
    inputs, hidden_low, first_pull, second_pull = retained
    delta_hidden, delta_second, second_gain, second_shift = dense_backward(
        hidden_low, encoder_params[3], second_pull, upstream
    )
    delta_inputs, delta_first, first_gain, first_shift = dense_backward(
        inputs, encoder_params[0], first_pull, delta_hidden
    )
    return (
        delta_inputs,
        (delta_first, first_gain, first_shift, delta_second, second_gain, second_shift),
    )


def dynamics_forward(dynamics_params, latent_in, action_low, embedded):
    inputs = jnp.concatenate([latent_in, action_low, embedded], 1)
    layer_one, first_pull = dense_forward(
        inputs, dynamics_params[0], dynamics_params[1], dynamics_params[2], post_mish
    )
    one_low = layer_one.astype(jnp.bfloat16)
    layer_two, second_pull = dense_forward(
        one_low, dynamics_params[3], dynamics_params[4], dynamics_params[5], post_mish
    )
    two_low = layer_two.astype(jnp.bfloat16)
    latent, third_pull = dense_forward(
        two_low, dynamics_params[6], dynamics_params[7], dynamics_params[8], post_simnorm
    )
    return (latent, (inputs, one_low, two_low, first_pull, second_pull, third_pull))


def dynamics_backward(dynamics_params, retained, upstream):
    inputs, one_low, two_low, first_pull, second_pull, third_pull = retained
    delta_two, delta_third, third_gain, third_shift = dense_backward(
        two_low, dynamics_params[6], third_pull, upstream
    )
    delta_one, delta_second, second_gain, second_shift = dense_backward(
        one_low, dynamics_params[3], second_pull, delta_two
    )
    delta_inputs, delta_first, first_gain, first_shift = dense_backward(
        inputs, dynamics_params[0], first_pull, delta_one
    )
    return (
        delta_inputs,
        (
            delta_first,
            first_gain,
            first_shift,
            delta_second,
            second_gain,
            second_shift,
            delta_third,
            third_gain,
            third_shift,
        ),
    )


def value_backward(value_params, inputs, bin_rows, fraction_rows, factor):
    first_before = jnp.einsum(
        "rk,qkn->qrn", inputs, value_params[0], preferred_element_type=jnp.float32
    )
    layer_one, first_pull = jax.vjp(
        head_mish,
        first_before,
        value_params[1].astype(jnp.float32),
        value_params[2].astype(jnp.float32),
    )
    one_low = layer_one.astype(jnp.bfloat16)
    second_before = jnp.einsum(
        "qrk,qkn->qrn", one_low, value_params[3], preferred_element_type=jnp.float32
    )
    layer_two, second_pull = jax.vjp(
        head_mish,
        second_before,
        value_params[4].astype(jnp.float32),
        value_params[5].astype(jnp.float32),
    )
    two_low = layer_two.astype(jnp.bfloat16)
    logits = (
        jnp.einsum("qrk,qkn->qrn", two_low, value_params[6], preferred_element_type=jnp.float32)
        + value_params[7].astype(jnp.float32)[:, None, :]
    )
    chances = jax.nn.softmax(logits, -1)
    columns = lax.broadcasted_iota(jnp.int32, (1, logits.shape[2]), 1)
    lower_bin = bin_rows[:, None]
    target = (1.0 - fraction_rows)[:, None] * (columns == lower_bin).astype(
        jnp.float32
    ) + fraction_rows[:, None] * (columns == lower_bin + 1).astype(jnp.float32)
    delta_logits = factor[None, :, None] * (chances - target[None])
    logit_low = delta_logits.astype(jnp.bfloat16)
    delta_bias = jnp.sum(delta_logits, 1)
    delta_third = jnp.einsum("qrk,qrn->qkn", two_low, logit_low, preferred_element_type=jnp.float32)
    delta_two = jnp.einsum(
        "qrn,qkn->qrk", logit_low, value_params[6], preferred_element_type=jnp.float32
    )
    before_two, second_gain, second_shift = second_pull(delta_two)
    two_round = before_two.astype(jnp.bfloat16)
    delta_second = jnp.einsum(
        "qrk,qrn->qkn", one_low, two_round, preferred_element_type=jnp.float32
    )
    delta_one = jnp.einsum(
        "qrn,qkn->qrk", two_round, value_params[3], preferred_element_type=jnp.float32
    )
    before_one, first_gain, first_shift = first_pull(delta_one)
    one_round = before_one.astype(jnp.bfloat16)
    delta_first = jnp.einsum("rk,qrn->qkn", inputs, one_round, preferred_element_type=jnp.float32)
    delta_inputs = jnp.einsum(
        "qrn,qkn->rk", one_round, value_params[0], preferred_element_type=jnp.float32
    )
    return (
        delta_inputs,
        (
            delta_first,
            first_gain,
            first_shift,
            delta_second,
            second_gain,
            second_shift,
            delta_third,
            delta_bias,
        ),
    )


def reduce_end(gradients):
    def reduced(index, axis):
        shard = lax.psum_scatter(
            gradients[index].astype(jnp.bfloat16), "dp", scatter_dimension=axis, tiled=True
        )
        return lax.psum(shard, "section").astype(jnp.float32)

    return tuple(
        reduced(index, axis)
        for index, axis in ((0, 1), (3, 0), (6, 1), (9, 0), (12, 0), (15, 2), (18, 1), (21, 1))
    )


def on_device(
    observations,
    actions,
    action_mask,
    task_ids,
    targets,
    bin_low,
    bin_frac,
    task_table,
    encoder_first,
    encoder_first_gain,
    encoder_first_shift,
    encoder_second,
    encoder_second_gain,
    encoder_second_shift,
    dynamics_first,
    dynamics_first_gain,
    dynamics_first_shift,
    dynamics_second,
    dynamics_second_gain,
    dynamics_second_shift,
    dynamics_third,
    dynamics_third_gain,
    dynamics_third_shift,
    value_first,
    value_first_gain,
    value_first_shift,
    value_second,
    value_second_gain,
    value_second_shift,
    value_third,
    value_bias,
):
    encoder_params = (
        encoder_first,
        encoder_first_gain,
        encoder_first_shift,
        encoder_second,
        encoder_second_gain,
        encoder_second_shift,
    )
    dynamics_params = (
        dynamics_first,
        dynamics_first_gain,
        dynamics_first_shift,
        dynamics_second,
        dynamics_second_gain,
        dynamics_second_shift,
        dynamics_third,
        dynamics_third_gain,
        dynamics_third_shift,
    )
    value_params = (
        value_first,
        value_first_gain,
        value_first_shift,
        value_second,
        value_second_gain,
        value_second_shift,
        value_third,
        value_bias,
    )
    sections = lax.axis_size("section")
    level_now = lax.axis_index("section")
    micro_total = observations.shape[0]
    share = micro_total // sections
    latent_width = dynamics_third.shape[1]
    action_width = actions.shape[3]
    observed_width = observations.shape[2]
    horizon = actions.shape[0]
    heads = value_first.shape[0]
    task_count = task_table.shape[0]

    def mine(array, axis):
        part = lax.dynamic_slice_in_dim(array, level_now * share, share, axis)
        shape = part.shape
        return part.reshape(shape[:axis] + (shape[axis] * shape[axis + 1],) + shape[axis + 2 :])

    observed = mine(observations, 0)
    movement = mine(actions, 1)
    task_rows = mine(task_ids, 0)
    goals = mine(targets, 1)
    low_bins = mine(bin_low, 1)
    fractions = mine(bin_frac, 1)
    rows = observed.shape[0]
    onehot = (task_rows[:, None] == lax.broadcasted_iota(jnp.int32, (1, task_count), 1)).astype(
        jnp.bfloat16
    )
    embedded = matmul(onehot, task_table).astype(jnp.bfloat16)
    allowed = matmul(onehot, action_mask.astype(jnp.bfloat16))
    chosen = (movement.astype(jnp.float32) * allowed[None]).astype(jnp.bfloat16)

    latent, encoder_kept = encoder_forward(encoder_params, observed, embedded)
    latents = [latent]
    dynamics_kept = []
    for step in range(horizon):
        latent, kept = dynamics_forward(
            dynamics_params, latents[step].astype(jnp.bfloat16), chosen[step], embedded
        )
        latents.append(latent)
        dynamics_kept.append(kept)
    inputs = jnp.concatenate([kept[0] for kept in dynamics_kept], 0)
    step_weight = jnp.asarray(
        [value_weight * discount**step / (heads * micro_total) for step in range(horizon)],
        jnp.float32,
    )
    value_delta, value_grads = value_backward(
        value_params,
        inputs,
        low_bins.reshape(-1),
        fractions.reshape(-1),
        jnp.repeat(step_weight, rows),
    )
    value_delta = value_delta.reshape(horizon, rows, -1)
    upstream = jnp.zeros((rows, latent_width), jnp.float32)
    embed_delta = jnp.sum(value_delta[:, :, latent_width + action_width :], 0)
    dynamics_grads = None
    for step in reversed(range(horizon)):
        factor = 2.0 * consistency_weight * discount**step / (micro_total * latent_width)
        upstream = upstream + factor * (latents[step + 1] - goals[step].astype(jnp.float32))
        inputs_delta, step_grads = dynamics_backward(dynamics_params, dynamics_kept[step], upstream)
        dynamics_grads = (
            step_grads
            if dynamics_grads is None
            else tuple(a + b for a, b in zip(dynamics_grads, step_grads))
        )
        embed_delta = embed_delta + inputs_delta[:, latent_width + action_width :]
        upstream = (
            inputs_delta[:, :latent_width].astype(jnp.bfloat16).astype(jnp.float32)
            + value_delta[step, :, :latent_width]
        )
    inputs_delta, encoder_grads = encoder_backward(encoder_params, encoder_kept, upstream)
    observed_delta = inputs_delta[:, :observed_width]
    embed_delta = embed_delta + inputs_delta[:, observed_width:]
    table_sum = left_transposed(onehot.astype(jnp.float32), embed_delta)
    totals = encoder_grads + dynamics_grads + value_grads
    matrices = reduce_end(totals)
    small_sums = lax.psum(
        tuple(totals[i] for i in (1, 2, 4, 5, 7, 8, 10, 11, 13, 14, 16, 17, 19, 20, 22))
        + (table_sum,),
        ("section", "dp"),
    )
    return (
        observed_delta.reshape(share, rows // share, observed_width),
        small_sums[15],
        matrices[0],
        small_sums[0],
        small_sums[1],
        matrices[1],
        small_sums[2],
        small_sums[3],
        matrices[2],
        small_sums[4],
        small_sums[5],
        matrices[3],
        small_sums[6],
        small_sums[7],
        matrices[4],
        small_sums[8],
        small_sums[9],
        matrices[5],
        small_sums[10],
        small_sums[11],
        matrices[6],
        small_sums[12],
        small_sums[13],
        matrices[7],
        small_sums[14],
    )


def solution(mesh):
    in_specs = (
        P(None, "dp", None),
        P(None, None, "dp", None),
        P(),
        P(None, "dp"),
        P(None, None, "dp", None),
        P(None, None, "dp"),
        P(None, None, "dp"),
        P(),
        P(),
        P(),
        P(),
        P(),
        P(),
        P(),
        P(),
        P(),
        P(),
        P(),
        P(),
        P(),
        P(),
        P(),
        P(),
        P(),
        P(),
        P(),
        P(),
        P(),
        P(),
        P(),
        P(),
    )
    out_specs = (
        P("section", "dp", None),
        P(),
        P(None, "dp"),
        P(),
        P(),
        P("dp", None),
        P(),
        P(),
        P(None, "dp"),
        P(),
        P(),
        P("dp", None),
        P(),
        P(),
        P("dp", None),
        P(),
        P(),
        P(None, None, "dp"),
        P(),
        P(),
        P(None, "dp", None),
        P(),
        P(),
        P(None, "dp", None),
        P(),
    )
    return jax.shard_map(
        on_device, mesh=mesh, in_specs=in_specs, out_specs=out_specs, check_vma=False
    )
```

```python
import functools

import jax
import jax.numpy as jnp
from jax import lax
from jax.experimental import pallas as pl
from jax.experimental.pallas import tpu as pltpu
from jax.sharding import PartitionSpec as P

SIMNORM = 8
epsilon = 1e-05
discount = 0.5
consistency_weight = 20.0
value_weight = 0.1

F32, BF16 = jnp.float32, jnp.bfloat16
TILE = 256
GROUP = 16


def ceil_to(value, unit):
    return -(-value // unit) * unit


def row_sum(values):
    return jnp.sum(values, -1, keepdims=True)


def col_sum(values):
    return jnp.sum(values, 0, keepdims=True)


def dot(a, b):
    return lax.dot_general(a, b, (((1,), (0,)), ((), ())), preferred_element_type=F32)


def dot_left(a, b):
    return lax.dot_general(a, b, (((0,), (0,)), ((), ())), preferred_element_type=F32)


def dot_right(a, b):
    return lax.dot_general(a, b, (((1,), (1,)), ((), ())), preferred_element_type=F32)


def loop(count, body, unroll=1):
    def step(i, carry):
        body(i)
        return carry

    lax.fori_loop(0, count, step, 0, unroll=unroll)


def at(i, size):
    return pl.ds(pl.multiple_of(i * size, size), size)


def forward_dot(out, a, b):
    width = min(TILE, out.shape[1])

    def tile(n):
        out[:, at(n, width)] = dot(a[...], b[:, at(n, width)])

    loop(out.shape[1] // width, tile)


def back_dot(out, a, b, add=False):
    width = 128

    def tile(n):
        part = dot_right(a[...], b[at(n, width), :])
        if add:
            part = part + out[:, at(n, width)]
        out[:, at(n, width)] = part

    loop(out.shape[1] // width, tile)


def norm(values):
    scale = 1.0 / values.shape[1]
    center = values - row_sum(values) * scale
    rstd = lax.rsqrt(row_sum(center * center) * scale + epsilon)
    return center * rstd, rstd


def norm_back(grad, xhat, rstd):
    scale = 1.0 / grad.shape[1]
    mean_grad = row_sum(grad) * scale
    mean_both = row_sum(grad * xhat) * scale
    return rstd * (grad - mean_grad - xhat * mean_both)


def mish_forward(z, rows, gain, shift, hidden, hidden_rows, slope, rstd_ref, unroll):
    def body(i):
        xhat, rstd = norm(z[at(i, GROUP), :])
        v = xhat * gain + shift
        e = jnp.exp(jnp.minimum(v, 30.0))
        n = e * (e + 2.0)
        r = pl.reciprocal(n + 2.0, approx=True)
        t = n * r
        z[at(i, GROUP), :] = xhat
        slope[at(i, GROUP), :] = (t + (4.0 * v) * ((e * r) * ((e + 1.0) * r))).astype(slope.dtype)
        rstd_ref[at(i, GROUP), :] = jnp.broadcast_to(rstd, (GROUP, 128))
        hidden[at(i, GROUP), :] = (v * t).astype(BF16)

    loop(rows // GROUP, body, unroll)


def mish_backward(upstream, rows, gain, xhat_ref, slope, rstd_ref, low, unroll):
    width = upstream.shape[1]

    def body(i, carry):
        gain_sum, shift_sum = carry
        xhat = xhat_ref[at(i, GROUP), :]
        g = upstream[at(i, GROUP), :] * slope[at(i, GROUP), :]
        gx = g * xhat
        low[at(i, GROUP), :] = norm_back(
            g * gain, xhat, rstd_ref[at(i, GROUP), :][:, :1]
        ).astype(BF16)
        return (
            gain_sum + gx.reshape(GROUP // 8, 8, width).sum(0),
            shift_sum + g.reshape(GROUP // 8, 8, width).sum(0),
        )

    zero = jnp.zeros((8, width), F32)
    gain_sum, shift_sum = lax.fori_loop(0, rows // GROUP, body, (zero, zero), unroll=unroll)
    return col_sum(gain_sum), col_sum(shift_sum)


def group_matrix(width):
    return (
        lax.broadcasted_iota(jnp.int32, (width, width), 0) // SIMNORM
        == lax.broadcasted_iota(jnp.int32, (width, width), 1) // SIMNORM
    ).astype(BF16)


def group_sums(values, groups):
    parts = []
    for k in range(values.shape[1] // 128):
        part = values[:, k * 128 : (k + 1) * 128]
        high = part.astype(BF16)
        rest = (part - high.astype(F32)).astype(BF16)
        parts.append(dot(high, groups) + dot(rest, groups))
    return jnp.concatenate(parts, 1)


def simnorm_forward(z, rows, gain, shift, chance, rstd_ref, groups):
    def body(i):
        xhat, rstd = norm(z[at(i, 32), :])
        e = jnp.exp(xhat * gain + shift)
        z[at(i, 32), :] = xhat
        chance[at(i, 32), :] = e / group_sums(e, groups)
        rstd_ref[at(i, 32), :] = jnp.broadcast_to(rstd, (32, 128))

    loop(rows // 32, body, 2)


def simnorm_backward(upstream, rows, gain, xhat_ref, chance, rstd_ref, groups, low):
    width = gain.shape[1]

    def body(i, carry):
        gain_sum, shift_sum = carry
        xhat = xhat_ref[at(i, 32), :]
        p = chance[at(i, 32), :]
        w = upstream[at(i, 32), :] * p
        g = w - p * group_sums(w, groups)
        gx = g * xhat
        low[at(i, 32), :] = norm_back(g * gain, xhat, rstd_ref[at(i, 32), :][:, :1]).astype(BF16)
        return (
            gain_sum + gx.reshape(4, 8, width).sum(0),
            shift_sum + g.reshape(4, 8, width).sum(0),
        )

    zero = jnp.zeros((8, width), F32)
    gain_sum, shift_sum = lax.fori_loop(0, rows // 32, body, (zero, zero), unroll=2)
    return col_sum(gain_sum), col_sum(shift_sum)


ORDERS = (("c", "x", "z0", "z1", "y"), ("c", "y", "z0", "z1", "x"))
STAGES = 5


class Exchange:
    def __init__(self, own, halves, lasts, gathered, outs, send_sem, recv_sem, free_sem, out_sem):
        self.own, self.halves, self.lasts, self.gathered, self.outs = own, halves, lasts, gathered, outs
        self.local = not halves
        self.send_sem, self.recv_sem, self.free_sem, self.out_sem = send_sem, recv_sem, free_sem, out_sem
        section, dp = lax.axis_index("section"), lax.axis_index("dp")
        self.bit = {
            "c": section % 2,
            "x": section // 2,
            "y": dp % 2,
            "z0": (dp // 2) % 2,
            "z1": dp // 4,
        }
        self.partner = {
            "c": {"section": section + 1 - 2 * self.bit["c"]},
            "x": {"section": section + 2 - 4 * self.bit["x"]},
            "y": {"dp": dp + 1 - 2 * self.bit["y"]},
            "z0": {"dp": dp + 2 - 4 * self.bit["z0"]},
            "z1": {"dp": dp + 4 - 8 * self.bit["z1"]},
        }

    def greet(self):
        if self.local:
            return
        barrier = pltpu.get_barrier_semaphore()
        for axis in self.partner:
            pl.semaphore_signal(
                barrier, inc=1, device_id=self.partner[axis], device_id_type=pl.DeviceIdType.MESH
            )
        pl.semaphore_wait(barrier, len(self.partner))

    def place(self, kind, rank, quarter):
        if self.local:
            return rank * 4 + quarter
        bits = {
            "c": quarter // 2,
            "x": quarter % 2,
            "y": rank % 2,
            "z0": (rank // 2) % 2,
            "z1": rank // 4,
        }
        index = 0
        for axis in ORDERS[kind]:
            index = index * 2 + bits[axis]
        return index

    def buffer(self, kind, piece, stage):
        if stage == 0:
            return self.own[kind]
        if stage == 1:
            return self.halves[kind].at[piece % 2]
        return self.lasts[kind][stage - 2].at[piece]

    def copy(self, kind, piece, stage):
        gathered = self.gathered[kind].at[piece]
        if stage < STAGES:
            axis = ORDERS[kind][stage]
            half = 32 >> (stage + 1)
            start = (1 - self.bit[axis]) * half
            source = self.buffer(kind, piece, stage).at[pl.ds(start, half)]
            target = self.buffer(kind, piece, stage + 1)
        elif stage == STAGES:
            axis = "x"
            source = target = gathered.at[self.bit["c"] * 2 + self.bit["x"]]
        else:
            axis = "c"
            source = target = gathered.at[pl.ds(self.bit["c"] * 2, 2)]
        return pltpu.make_async_remote_copy(
            src_ref=source,
            dst_ref=target,
            send_sem=self.send_sem.at[kind, piece, stage],
            recv_sem=self.recv_sem.at[kind, piece, stage],
            device_id=self.partner[axis],
            device_id_type=pl.DeviceIdType.MESH,
        )

    def keep(self, kind, piece):
        copy = pltpu.make_async_copy(self.own[kind], self.outs[kind].at[piece], self.out_sem.at[kind, piece])
        copy.start()
        copy.wait()

    def start(self, kind, piece, stage):
        self.copy(kind, piece, stage).start()

    def free(self, kind):
        pl.semaphore_signal(
            self.free_sem.at[kind],
            inc=1,
            device_id=self.partner["c"],
            device_id_type=pl.DeviceIdType.MESH,
        )

    def finish(self, kind, piece, stage):
        self.copy(kind, piece, stage).wait()
        if stage < STAGES:
            half = 32 >> (stage + 1)
            begin = self.bit[ORDERS[kind][stage]] * half
            kept, total = self.buffer(kind, piece, stage), self.buffer(kind, piece, stage + 1)
            if stage == STAGES - 1:
                self.gathered[kind][piece, self.bit["c"] * 2 + self.bit["x"]] = total[0] + kept[begin]
            else:

                def add(i):
                    total[i] = total[i] + kept[begin + i]

                loop(half, add)
        if stage == STAGES + 1:
            pltpu.make_async_copy(
                self.gathered[kind].at[piece], self.outs[kind].at[piece], self.out_sem.at[kind, piece]
            ).start()

    def advance(self, kind, piece, stage):
        self.finish(kind, piece, stage)
        if stage <= STAGES:
            self.start(kind, piece, stage + 1)

    def small_copy(self, stage):
        parts = self.small
        c, x = self.bit["c"], self.bit["x"]
        if stage == 0:
            axis, source, target = "c", parts[0].at[pl.ds((1 - c) * 2, 2)], parts[1]
        elif stage == 1:
            axis, source, target = "x", parts[1].at[1 - x], parts[2]
        elif stage < STAGES:
            axis, source, target = ("y", "z0", "z1")[stage - 2], parts[stage], parts[stage + 1]
        elif stage == STAGES:
            axis = "x"
            source = target = self.small_all.at[c * 2 + x]
        else:
            axis = "c"
            source = target = self.small_all.at[pl.ds(c * 2, 2)]
        return pltpu.make_async_remote_copy(
            src_ref=source,
            dst_ref=target,
            send_sem=self.small_send.at[stage],
            recv_sem=self.small_recv.at[stage],
            device_id=self.partner[axis],
            device_id_type=pl.DeviceIdType.MESH,
        )

    def small_start(self):
        if not self.local:
            self.small_copy(0).start()

    def small_advance(self, stage):
        parts = self.small
        c, x = self.bit["c"], self.bit["x"]
        self.small_copy(stage).wait()
        if stage == 0:
            parts[1][...] = parts[1][...] + parts[0][pl.ds(c * 2, 2)]
        elif stage == 1:
            parts[2][...] = parts[2][...] + parts[1][x]
        elif stage < STAGES - 1:
            parts[stage + 1][...] = parts[stage + 1][...] + parts[stage][...]
        elif stage == STAGES - 1:
            self.small_all[c * 2 + x] = parts[stage + 1][...] + parts[stage][...]
        if stage <= STAGES:
            self.small_copy(stage + 1).start()

    def finish_out(self, kind, piece):
        pltpu.make_async_copy(
            self.gathered[kind].at[piece], self.outs[kind].at[piece], self.out_sem.at[kind, piece]
        ).wait()


TICKS = {
    1: ((0, 3, 6), (1, 1, 0), (0, 2, 2), (1, 3, 5)),
    2: ((1, 2, 2), (1, 3, 6)),
    3: ((0, 2, 3), (1, 2, 3)),
    4: ((0, 2, 4), (0, 1, 1), (0, 0, -1)),
    5: ((1, 2, 4), (0, 0, 0), (0, 2, 5), (1, 1, 1), (1, 0, -1)),
}


def local_kernel(
    micro_total,
    bins_valid,
    task_columns,
    obs_ref,
    act_ref,
    ids_ref,
    goals_ref,
    low_ref,
    frac_ref,
    lookup_ref,
    we1_ref,
    we2_ref,
    wd1_ref,
    wd2_ref,
    wd3_ref,
    wv1_ref,
    wv1_rest_ref,
    wv2_ref,
    wv3_ref,
    param_ref,
    bias_ref,
    ga_ref,
    gb_ref,
    small_ref,
    obs_grad_ref,
    goals,
    wv1,
    wv2,
    wv3,
    pa,
    pb,
    x_enc,
    x_all,
    onehot,
    target,
    z_chain,
    slope_chain,
    rstd_chain,
    hid_chain,
    z_lat,
    lat,
    rstd_lat,
    dz_lat,
    dz_one,
    dz_two,
    z1,
    s1,
    r1,
    h1,
    z2,
    s2,
    r2,
    h2,
    up,
    dz,
    dlog,
    dx,
    small,
    load_sem,
    goal_sem,
    out_sem,
    half_a=None,
    half_b=None,
    last_a=None,
    last_b=None,
    all_a=None,
    all_b=None,
    small_parts=None,
    small_all=None,
    send_sem=None,
    recv_sem=None,
    small_send=None,
    small_recv=None,
    free_sem=None,
):
    micro = lax.axis_index("section")
    horizon, _, rows, latent_width = goals_ref.shape
    heads = wv1_ref.shape[0]
    hidden = wv2_ref.shape[1]
    observed = obs_ref.shape[2]
    moves = act_ref.shape[3]
    tasks = lookup_ref.shape[0]
    task_width = task_columns
    total = horizon * rows
    ranks = hidden // 128
    exchange = Exchange(
        (pa, pb),
        (half_a, half_b) if half_a is not None else (),
        (last_a, last_b),
        (all_a, all_b),
        (ga_ref, gb_ref),
        send_sem,
        recv_sem,
        free_sem,
        out_sem,
    )
    exchange.small, exchange.small_all = (small, *(small_parts or ())), small_all
    exchange.small_send, exchange.small_recv = small_send, small_recv

    def set_small(index, value):
        small[0, index : index + 1, :] = value

    def tick(point, now):
        for kind, age, stage in TICKS[point]:

            def act(made, kind=kind, stage=stage):
                piece = made
                if kind == 1 and isinstance(made, int):
                    piece = min(made, heads)
                if exchange.local:
                    if stage < 0:
                        exchange.keep(kind, piece)
                    return
                if stage < 0:
                    if isinstance(piece, int):
                        if piece >= 2:
                            pl.semaphore_wait(free_sem.at[kind], 1)
                    else:

                        @pl.when(piece >= 2)
                        def _():
                            pl.semaphore_wait(free_sem.at[kind], 1)

                    exchange.start(kind, piece, 0)
                    return
                exchange.advance(kind, piece, stage)
                if stage == 1:
                    last = heads + 1 if kind == 0 else heads
                    if isinstance(piece, int):
                        if piece + 2 <= last:
                            exchange.free(kind)
                    else:
                        exchange.free(kind)

            made = now - age
            if isinstance(now, int):
                if 0 <= made <= heads + 1 and not (kind == 1 and made == heads):
                    act(made)
            elif age == 0:
                act(made)
            else:
                pl.when(made >= 0)(functools.partial(act, made))


    def weight_copies(q, slot):
        return (
            pltpu.make_async_copy(
                wv1_ref.at[q, pl.ds(0, latent_width)], wv1.at[slot, pl.ds(0, latent_width)], load_sem.at[slot, 0]
            ),
            pltpu.make_async_copy(
                wv1_rest_ref.at[q], wv1.at[slot, pl.ds(latent_width, 128)], load_sem.at[slot, 1]
            ),
            pltpu.make_async_copy(wv2_ref.at[q], wv2.at[slot], load_sem.at[slot, 2]),
            pltpu.make_async_copy(wv3_ref.at[q], wv3.at[slot], load_sem.at[slot, 3]),
        )

    exchange.greet()
    small[...] = jnp.zeros_like(small)
    for copy in weight_copies(0, 0):
        copy.start()
    goal_copies = [
        pltpu.make_async_copy(goals_ref.at[t, micro], goals.at[t], goal_sem.at[t]) for t in range(horizon)
    ]
    for copy in goal_copies:
        copy.start()

    groups = group_matrix(128)
    onehot[...] = (
        lax.broadcasted_iota(jnp.int32, (tasks, rows), 0) == ids_ref[micro]
    ).astype(BF16)
    looked = dot_left(onehot[...], lookup_ref[...])
    x_enc[...] = looked[:, 128:].astype(BF16)
    x_enc[:, :observed] = obs_ref[micro]
    for t in range(horizon):
        x_all[t * rows : (t + 1) * rows, latent_width:] = looked[:, :128].astype(BF16)
        x_all[t * rows : (t + 1) * rows, latent_width : latent_width + moves] = (
            looked[:, :moves] * act_ref[t, micro].astype(F32)
        ).astype(BF16)
        bin_at = lax.broadcasted_iota(jnp.int32, (128, rows), 0)
        lower, upper_part = low_ref[t, micro], frac_ref[t, micro]
        target[t * rows : (t + 1) * rows, :] = (
            jnp.where(bin_at == lower, 1.0 - upper_part, 0.0)
            + jnp.where(bin_at == lower + 1, upper_part, 0.0)
        ).T

    def vec(index):
        return param_ref[index]

    forward_dot(z_chain.at[0], x_enc, we1_ref)
    mish_forward(
        z_chain.at[0], rows, vec(0), vec(1), hid_chain.at[0], None, slope_chain.at[0], rstd_chain.at[0], 2
    )
    forward_dot(z_lat.at[0], hid_chain.at[0], we2_ref)
    simnorm_forward(
        z_lat.at[0],
        rows,
        vec(2)[:, :latent_width],
        vec(2)[:, latent_width:],
        lat.at[0],
        rstd_lat.at[0],
        groups,
    )

    def dynamics_step(t):
        own = x_all.at[at(t, rows), :]
        own[:, :latent_width] = lat[t].astype(BF16)
        one, two = 1 + 2 * t, 2 + 2 * t
        forward_dot(z_chain.at[one], own, wd1_ref)
        mish_forward(
            z_chain.at[one],
            rows,
            vec(3),
            vec(4),
            hid_chain.at[one],
            None,
            slope_chain.at[one],
            rstd_chain.at[one],
            2,
        )
        forward_dot(z_chain.at[two], hid_chain.at[one], wd2_ref)
        mish_forward(
            z_chain.at[two],
            rows,
            vec(5),
            vec(6),
            hid_chain.at[two],
            None,
            slope_chain.at[two],
            rstd_chain.at[two],
            2,
        )
        forward_dot(z_lat.at[t + 1], hid_chain.at[two], wd3_ref)
        simnorm_forward(
            z_lat.at[t + 1],
            rows,
            vec(7)[:, :latent_width],
            vec(7)[:, latent_width:],
            lat.at[t + 1],
            rstd_lat.at[t + 1],
            groups,
        )

    loop(horizon, dynamics_step)

    dx[...] = jnp.zeros_like(dx)
    part_rows, rest_rows = pb.shape[1], pa.shape[1]

    def put(kind, rank, block, quarter_rows, begin):
        low = block.astype(BF16)
        for quarter in range(4):
            exchange.own[kind][
                exchange.place(kind, rank, quarter), begin : begin + quarter_rows, :
            ] = low[quarter * quarter_rows : (quarter + 1) * quarter_rows]


    def head(q):
        slot = lax.rem(q, 2)

        @pl.when(q + 1 < heads)
        def _():
            for copy in weight_copies(q + 1, 1 - slot):
                copy.start()

        for copy in weight_copies(q, slot):
            copy.wait()
        base = 8 + 4 * q
        forward_dot(z1, x_all, wv1.at[slot])
        mish_forward(z1, total, vec(base), vec(base + 1), h1, None, s1, r1, 2)
        tick(1, q)
        forward_dot(z2, h1, wv2.at[slot])
        mish_forward(z2, total, vec(base + 2), vec(base + 3), h2, None, s2, r2, 2)
        tick(2, q)
        bias = bias_ref[q]
        valid = lax.broadcasted_iota(jnp.int32, (1, 128), 1) < bins_valid

        def cross_entropy(t):
            factor = (value_weight / (heads * micro_total)) * jnp.exp2(-t.astype(F32))
            logits = dot(h2[at(t, rows), :], wv3[slot]) + bias
            logits = jnp.where(valid, logits, -1e30)
            e = jnp.exp(logits - jnp.max(logits, -1, keepdims=True))
            delta = factor * (e / row_sum(e) - target[at(t, rows), :])
            dlog[at(t, rows), :] = delta.astype(BF16)
            return col_sum(delta)

        bias_sum = jnp.zeros((1, 128), F32)
        for t in range(horizon):
            bias_sum = bias_sum + cross_entropy(jnp.int32(t))

        def third(d):
            block = dot_left(h2[:, at(d, 128)], dlog[...])
            put(1, d, block, rest_rows, part_rows - rest_rows)

        loop(ranks, third)
        back_dot(up, dlog, wv3.at[slot])
        second_sums = mish_backward(up, total, vec(base + 2), z2, s2, r2, dz, 2)

        tick(3, q)

        def second(d):
            block = dot_left(h1[:, at(d, 128)], dz[...])
            put(0, d, block, rest_rows, 0)

        loop(ranks, second)
        tick(4, q)
        back_dot(up, dz, wv2.at[slot])
        first_sums = mish_backward(up, total, vec(base), z1, s1, r1, dz, 2)
        pad = jnp.zeros((1, hidden - 128), F32)
        small[(q + 1) // 2, pl.ds(pl.multiple_of((q + 1) % 2 * 8, 8), 8), :] = jnp.concatenate(
            [*first_sums, *second_sums, jnp.concatenate([bias_sum, pad], 1), jnp.zeros((3, hidden), F32)], 0
        )

        def first(d):
            block = dot_left(x_all[...], dz[:, at(d, 128)])
            put(1, d, block, part_rows - rest_rows, 0)

        loop(ranks, first)
        back_dot(dx, dz, wv1.at[slot], add=True)
        tick(5, q)

    loop(heads, head)

    for copy in goal_copies:
        copy.wait()
    embed_sum = jnp.zeros((rows, 128), F32)
    for t in range(horizon):
        embed_sum = embed_sum + dx[t * rows : (t + 1) * rows, latent_width:]
    carry_up = up.at[pl.ds(0, rows), pl.ds(0, latent_width)]
    wide_up = up.at[pl.ds(0, rows), :]
    lat_sums = [jnp.zeros((1, latent_width), F32)] * 2
    two_sums = [jnp.zeros((1, hidden), F32)] * 2
    one_sums = [jnp.zeros((1, hidden), F32)] * 2
    gain_lat, shift_lat = vec(7)[:, :latent_width], vec(7)[:, latent_width:]
    carry = None
    for t in reversed(range(horizon)):
        factor = 2.0 * consistency_weight * discount**t / (micro_total * latent_width)
        upstream = factor * (lat[t + 1] - goals[t].astype(F32))
        if carry is not None:
            upstream = upstream + carry
        carry_up[...] = upstream
        own = pl.ds(t * rows, rows)
        sums = simnorm_backward(
            carry_up, rows, gain_lat, z_lat.at[t + 1], lat.at[t + 1], rstd_lat.at[t + 1], groups, dz_lat.at[own, :]
        )
        lat_sums = [a + b for a, b in zip(lat_sums, sums)]
        one, two = 1 + 2 * t, 2 + 2 * t
        back_dot(wide_up, dz_lat.at[own, :], wd3_ref)
        sums = mish_backward(
            wide_up, rows, vec(5), z_chain.at[two], slope_chain.at[two], rstd_chain.at[two], dz_two.at[own, :], 2
        )
        two_sums = [a + b for a, b in zip(two_sums, sums)]
        if t == horizon - 1:
            tick(1, heads)
        back_dot(wide_up, dz_two.at[own, :], wd2_ref)
        sums = mish_backward(
            wide_up, rows, vec(3), z_chain.at[one], slope_chain.at[one], rstd_chain.at[one], dz_one.at[own, :], 2
        )
        one_sums = [a + b for a, b in zip(one_sums, sums)]
        inputs_up = up.at[pl.ds(0, rows), pl.ds(0, latent_width + 128)]
        back_dot(inputs_up, dz_one.at[own, :], wd1_ref)
        carry = (
            inputs_up[:, :latent_width].astype(BF16).astype(F32)
            + dx[t * rows : (t + 1) * rows, :latent_width]
        )
        embed_sum = embed_sum + inputs_up[:, latent_width:]
        if t == horizon - 1:
            tick(2, heads)
        if t == horizon - 2:
            tick(3, heads)
    for index, value in enumerate((*one_sums, *two_sums, jnp.concatenate(lat_sums, 1))):
        set_small(3 + index, value)

    def dynamics_second(d):
        block = dot_left(hid_chain[1, :, at(d, 128)], dz_two[:rows, :])
        for t in range(1, horizon):
            block = block + dot_left(hid_chain[1 + 2 * t, :, at(d, 128)], dz_two[t * rows : (t + 1) * rows, :])
        put(0, d, block, rest_rows, 0)

    loop(ranks, dynamics_second)
    tick(4, heads)

    tick(5, heads)
    first_rows = ceil_to(latent_width + moves + task_width, 16)

    def put_first(rank, block, begin):
        low = block.astype(BF16)
        done = 0
        while done < low.shape[0]:
            quarter, offset = divmod(begin + done, part_rows)
            count = min(part_rows - offset, low.shape[0] - done)
            pb[exchange.place(1, rank, quarter), offset : offset + count, :] = low[done : done + count]
            done += count

    def dynamics_first(d):
        put_first(d, dot_left(x_all[...], dz_one[:, at(d, 128)])[:first_rows], 0)

    loop(ranks, dynamics_first)

    def dynamics_third(d):
        block = dot_left(hid_chain[2, :, at(d, 128)], dz_lat[:rows, :])
        for t in range(1, horizon):
            block = block + dot_left(hid_chain[2 + 2 * t, :, at(d, 128)], dz_lat[t * rows : (t + 1) * rows, :])
        low = block.astype(BF16)
        for quarter in range(4):
            pa[exchange.place(0, d, quarter), :, :latent_width] = low[quarter * rest_rows : (quarter + 1) * rest_rows]

    loop(ranks, dynamics_third)
    tick(1, heads + 1)
    carry_up[...] = carry
    low_lat = dz_lat.at[pl.ds(0, rows), :]
    sums = simnorm_backward(
        carry_up,
        rows,
        vec(2)[:, :latent_width],
        z_lat.at[0],
        lat.at[0],
        rstd_lat.at[0],
        groups,
        low_lat,
    )
    set_small(2, jnp.concatenate(sums, 1))
    tick(2, heads + 1)
    back_dot(wide_up, low_lat, we2_ref)
    low_one = dz_one.at[pl.ds(0, rows), :]
    sums = mish_backward(
        wide_up, rows, vec(0), z_chain.at[0], slope_chain.at[0], rstd_chain.at[0], low_one, 2
    )
    set_small(0, sums[0])
    set_small(1, sums[1])

    def encoder_second(d):
        block = dot_left(hid_chain[0, :, at(d, 128)], low_lat[...])
        low = block.astype(BF16)
        for quarter in range(4):
            pa[exchange.place(0, d, quarter), :, latent_width:] = low[quarter * rest_rows : (quarter + 1) * rest_rows]

    loop(ranks, encoder_second)
    tick(3, heads + 1)
    tick(4, heads + 1)

    enc_up = up.at[pl.ds(0, rows), pl.ds(0, x_enc.shape[1])]
    back_dot(enc_up, low_one, we1_ref)
    obs_grad_ref[...] = enc_up[...]
    grad = embed_sum + pltpu.roll(enc_up[...], x_enc.shape[1] - observed + moves, 1)[:, :128]
    high = grad.astype(BF16)
    table = dot(onehot[...], high) + dot(onehot[...], (grad - high.astype(F32)).astype(BF16))
    for k in range(tasks // 8):
        small[3, (k // 8) * 8 : (k // 8) * 8 + 8, (k % 8) * 128 : (k % 8) * 128 + 128] = table[k * 8 : k * 8 + 8]
    exchange.small_start()

    def encoder_first(d):
        block = dot_left(x_enc[...], low_one[:, at(d, 128)])
        put_first(d, block[: 4 * part_rows - first_rows], first_rows)

    loop(ranks, encoder_first)
    tick(5, heads + 1)
    if exchange.local:
        small_ref[...] = small[...]
        return
    for now in range(heads + 2, heads + 5):
        for point in range(1, 6):
            tick(point, now)
            if now == heads + 2 or point <= 2 and now == heads + 3:
                exchange.small_advance((now - heads - 2) * 5 + point - 1)
    small_ref[...] = small_all[...]
    for piece in range(heads + 2):
        exchange.finish_out(0, piece)
    for piece in range(heads + 1):
        exchange.finish_out(1, piece)


def solution(mesh):
    def on_device(
        observations,
        actions,
        action_mask,
        task_ids,
        targets,
        bin_low,
        bin_frac,
        task_table,
        encoder_first,
        encoder_first_gain,
        encoder_first_shift,
        encoder_second,
        encoder_second_gain,
        encoder_second_shift,
        dynamics_first,
        dynamics_first_gain,
        dynamics_first_shift,
        dynamics_second,
        dynamics_second_gain,
        dynamics_second_shift,
        dynamics_third,
        dynamics_third_gain,
        dynamics_third_shift,
        value_first,
        value_first_gain,
        value_first_shift,
        value_second,
        value_second_gain,
        value_second_shift,
        value_third,
        value_bias,
    ):
        horizon, micro_total, rows, moves = actions.shape
        tasks, task_width = task_table.shape
        heads, inputs, hidden = value_first.shape
        latent_width = dynamics_third.shape[1]
        observed = observations.shape[2]
        bins = value_third.shape[2]
        rest = inputs - latent_width
        enc_rows = ceil_to(observed + task_width, 256)
        in_rows = latent_width + 128
        total = horizon * rows
        ranks = hidden // 128
        lookup = jnp.concatenate(
            [
                action_mask.astype(BF16),
                task_table,
                jnp.zeros((tasks, 128 - rest + observed), BF16),
                task_table,
                jnp.zeros((tasks, enc_rows - observed - task_width), BF16),
            ],
            1,
        )
        we1 = jnp.pad(encoder_first, ((0, enc_rows - observed - task_width), (0, 0)))
        wd1 = jnp.pad(dynamics_first, ((0, in_rows - inputs), (0, 0)))
        wv1_rest = jnp.pad(value_first[:, latent_width:], ((0, 0), (0, 128 - rest), (0, 0)))
        wv3 = jnp.pad(value_third, ((0, 0), (0, 0), (0, 128 - bins)))
        value_vecs = jnp.stack(
            [value_first_gain, value_first_shift, value_second_gain, value_second_shift], 1
        ).reshape(4 * heads, hidden)
        params = (
            jnp.concatenate(
                [
                    jnp.stack(
                        [
                            encoder_first_gain,
                            encoder_first_shift,
                            jnp.concatenate([encoder_second_gain, encoder_second_shift]),
                            dynamics_first_gain,
                            dynamics_first_shift,
                            dynamics_second_gain,
                            dynamics_second_shift,
                            jnp.concatenate([dynamics_third_gain, dynamics_third_shift]),
                        ]
                    ),
                    value_vecs,
                ]
            )
            .astype(F32)
            .reshape(-1, 1, hidden)
        )
        bias = jnp.pad(value_bias.astype(F32), ((0, 0), (0, 128 - bins))).reshape(heads, 1, 128)
        part_rows = (in_rows + 128) // 4
        rest_rows = hidden // (ranks * 4)
        chain = 1 + 2 * horizon
        vmem, anywhere = pl.BlockSpec(memory_space=pltpu.VMEM), pl.BlockSpec(memory_space=pl.ANY)
        local = (lax.axis_size("section"), lax.axis_size("dp")) != (4, 8)
        places = 32 if local else 4
        exchanged = (
            []
            if local
            else [
                pltpu.VMEM((2, 16, rest_rows, hidden), BF16),
                pltpu.VMEM((2, 16, part_rows, 128), BF16),
                [pltpu.VMEM((heads + 2, 8 >> k, rest_rows, hidden), BF16) for k in range(4)],
                [pltpu.VMEM((heads + 1, 8 >> k, part_rows, 128), BF16) for k in range(4)],
                pltpu.VMEM((heads + 2, 4, rest_rows, hidden), BF16),
                pltpu.VMEM((heads + 1, 4, part_rows, 128), BF16),
                [pltpu.VMEM((2, 16, hidden), F32)] + [pltpu.VMEM((16, hidden), F32) for _ in range(4)],
                pltpu.VMEM((4, 16, hidden), F32),
                pltpu.SemaphoreType.DMA((2, heads + 2, 7)),
                pltpu.SemaphoreType.DMA((2, heads + 2, 7)),
                pltpu.SemaphoreType.DMA((7,)),
                pltpu.SemaphoreType.DMA((7,)),
                pltpu.SemaphoreType.REGULAR((2,)),
            ]
        )
        outs = pl.pallas_call(
            functools.partial(local_kernel, micro_total, bins, task_width),
            out_shape=(
                jax.ShapeDtypeStruct((heads + 2, places, rest_rows, hidden), BF16),
                jax.ShapeDtypeStruct((heads + 1, places, part_rows, 128), BF16),
                jax.ShapeDtypeStruct((4, 16, hidden), F32),
                jax.ShapeDtypeStruct((rows, enc_rows), F32),
            ),
            in_specs=[vmem] * 3 + [anywhere] + [vmem] * 8 + [anywhere] * 4 + [vmem] * 2,
            out_specs=[anywhere] * 2 + [vmem] * 2,
            scratch_shapes=[
                pltpu.VMEM((horizon, rows, latent_width), BF16),
                pltpu.VMEM((2, in_rows, hidden), BF16),
                pltpu.VMEM((2, hidden, hidden), BF16),
                pltpu.VMEM((2, hidden, 128), BF16),
                pltpu.VMEM((32, rest_rows, hidden), BF16),
                pltpu.VMEM((32, part_rows, 128), BF16),
                pltpu.VMEM((rows, enc_rows), BF16),
                pltpu.VMEM((total, in_rows), BF16),
                pltpu.VMEM((tasks, rows), BF16),
                pltpu.VMEM((total, 128), F32),
                pltpu.VMEM((chain, rows, hidden), F32),
                pltpu.VMEM((chain, rows, hidden), BF16),
                pltpu.VMEM((chain, rows, 128), F32),
                pltpu.VMEM((chain, rows, hidden), BF16),
                pltpu.VMEM((horizon + 1, rows, latent_width), F32),
                pltpu.VMEM((horizon + 1, rows, latent_width), F32),
                pltpu.VMEM((horizon + 1, rows, 128), F32),
                pltpu.VMEM((total, latent_width), BF16),
                pltpu.VMEM((total, hidden), BF16),
                pltpu.VMEM((total, hidden), BF16),
                pltpu.VMEM((total, hidden), F32),
                pltpu.VMEM((total, hidden), BF16),
                pltpu.VMEM((total, 128), F32),
                pltpu.VMEM((total, hidden), BF16),
                pltpu.VMEM((total, hidden), F32),
                pltpu.VMEM((total, hidden), BF16),
                pltpu.VMEM((total, 128), F32),
                pltpu.VMEM((total, hidden), BF16),
                pltpu.VMEM((total, hidden), F32),
                pltpu.VMEM((total, hidden), BF16),
                pltpu.VMEM((total, 128), BF16),
                pltpu.VMEM((total, in_rows), F32),
                pltpu.VMEM((4, 16, hidden), F32),
                pltpu.SemaphoreType.DMA((2, 4)),
                pltpu.SemaphoreType.DMA((horizon,)),
                pltpu.SemaphoreType.DMA((2, heads + 2)),
            ]
            + exchanged,
            compiler_params=pltpu.CompilerParams(
                collective_id=None if local else 0, has_side_effects=True, vmem_limit_bytes=63 << 20
            ),
        )(
            observations,
            actions,
            task_ids.reshape(micro_total, 1, rows),
            targets,
            bin_low.reshape(horizon, micro_total, 1, rows),
            bin_frac.reshape(horizon, micro_total, 1, rows),
            lookup,
            we1,
            encoder_second,
            wd1,
            dynamics_second,
            dynamics_third,
            value_first,
            wv1_rest,
            value_second,
            wv3,
            params,
            bias,
        )
        ga, gb, small, observed_delta = outs
        first_rows = in_rows // 4
        shard = hidden // lax.axis_size("dp")
        third = gb[:heads, :, first_rows:]
        firsts = gb[:heads, :, :first_rows]
        tall = gb[heads]
        if local:

            def summed(block, axis):
                block = lax.psum_scatter(block, "dp", scatter_dimension=axis, tiled=True)
                return lax.psum(block, "section")

            def lanes(block):
                block = jnp.moveaxis(block.reshape(-1, ranks, 4 * block.shape[-2], 128), 1, 2)
                return block.reshape(block.shape[:2] + (hidden,))

            small = lax.psum(small, ("section", "dp"))
            ga = summed(ga.reshape(heads + 2, hidden, hidden), 1)
            third = summed(third.reshape(heads, hidden, 128), 1)
            firsts = summed(lanes(firsts.reshape(heads, ranks, 4, first_rows, 128)), 2)
            tall = summed(lanes(tall.reshape(1, ranks, 4, part_rows, 128))[0], 1)
        wide = ga.reshape(heads + 2, shard, hidden)
        third = third.reshape(heads, shard, 128)
        firsts = firsts.reshape(heads, in_rows, shard)
        tall = tall.reshape(4 * part_rows, shard)
        small = small.reshape(64, hidden)
        table = jnp.moveaxis(small[48:].reshape(2, 8, ranks, 128), 2, 1).reshape(16 * 8, 128)
        encoder_begin = ceil_to(inputs, 16)

        def vectors(first):
            return jnp.stack([small[8 + 8 * q + first] for q in range(heads)])

        return (
            observed_delta[None, :, :observed],
            table[:tasks, moves : moves + task_width],
            tall[encoder_begin : encoder_begin + observed + task_width].astype(F32),
            small[0],
            small[1],
            wide[heads + 1, :, latent_width:].astype(F32),
            small[2, :latent_width],
            small[2, latent_width:],
            tall[:inputs].astype(F32),
            small[3],
            small[4],
            wide[heads].astype(F32),
            small[5],
            small[6],
            wide[heads + 1, :, :latent_width].astype(F32),
            small[7, :latent_width],
            small[7, latent_width:],
            firsts[:, :inputs].astype(F32),
            vectors(0),
            vectors(1),
            wide[:heads].astype(F32),
            vectors(2),
            vectors(3),
            third[:, :, :bins].astype(F32),
            vectors(4)[:, :bins],
        )

    in_specs = (
        P(None, "dp", None),
        P(None, None, "dp", None),
        P(),
        P(None, "dp"),
        P(None, None, "dp", None),
        P(None, None, "dp"),
        P(None, None, "dp"),
    ) + (P(),) * 24
    out_specs = (
        P("section", "dp", None),
        P(),
        P(None, "dp"),
        P(),
        P(),
        P("dp", None),
        P(),
        P(),
        P(None, "dp"),
        P(),
        P(),
        P("dp", None),
        P(),
        P(),
        P("dp", None),
        P(),
        P(),
        P(None, None, "dp"),
        P(),
        P(),
        P(None, "dp", None),
        P(),
        P(),
        P(None, "dp", None),
        P(),
    )
    return jax.shard_map(
        on_device, mesh=mesh, in_specs=in_specs, out_specs=out_specs, check_vma=False
    )
```

```python
import functools

import jax
import jax.numpy as jnp
from jax import lax
from jax.experimental import pallas as pl
from jax.experimental.pallas import tpu as pltpu
from jax.sharding import PartitionSpec as P

SIMNORM = 8
epsilon = 1e-05
discount = 0.5
consistency_weight = 20.0
value_weight = 0.1

F32, BF16 = jnp.float32, jnp.bfloat16
WIDE_GROUP = 32
GROUP = 16
KERNEL_VMEM = 63 << 20


def ceil_to(value, unit):
    return -(-value // unit) * unit


def row_sum(values):
    return jnp.sum(values, -1, keepdims=True)


def col_sum(values):
    return jnp.sum(values, 0, keepdims=True)


def dot(a, b):
    return lax.dot_general(a, b, (((1,), (0,)), ((), ())), preferred_element_type=F32)


def dot_left(a, b):
    return lax.dot_general(a, b, (((0,), (0,)), ((), ())), preferred_element_type=F32)


def dot_right(a, b):
    return lax.dot_general(a, b, (((1,), (1,)), ((), ())), preferred_element_type=F32)


def loop(count, body, unroll=1):
    def step(i, carry):
        body(i)
        return carry

    lax.fori_loop(0, count, step, 0, unroll=unroll)


def at(i, size):
    return pl.ds(pl.multiple_of(i * size, size), size)


def norm(values):
    scale = 1.0 / values.shape[1]
    center = values - row_sum(values) * scale
    rstd = lax.rsqrt(row_sum(center * center) * scale + epsilon)
    return center * rstd, rstd


def norm_back(grad, xhat, rstd):
    scale = 1.0 / grad.shape[1]
    mean_grad = row_sum(grad) * scale
    mean_both = row_sum(grad * xhat) * scale
    return rstd * (grad - mean_grad - xhat * mean_both)


def mish_forward(z, gain, shift, hidden, xhat_ref, slope, rstd_ref):
    def body(i):
        rows = at(i, WIDE_GROUP)
        xhat, rstd = norm(z[rows, :])
        v = xhat * gain + shift
        e = jnp.exp(jnp.minimum(v, 30.0))
        n = e * (e + 2.0)
        r = pl.reciprocal(n + 2.0, approx=True)
        t = n * r
        xhat_ref[rows, :] = xhat.astype(xhat_ref.dtype)
        slope[rows, :] = (t + (4.0 * v) * ((e * r) * ((e + 1.0) * r))).astype(slope.dtype)
        rstd_ref[rows, :] = jnp.broadcast_to(rstd, (WIDE_GROUP, 128))
        hidden[rows, :] = (v * t).astype(BF16)

    loop(z.shape[0] // WIDE_GROUP, body, 4)


def mish_backward(upstream, gain, xhat_ref, slope, rstd_ref, low):
    rows, width = upstream.shape

    def body(i, carry):
        gain_sum, shift_sum = carry
        xhat = xhat_ref[at(i, GROUP), :].astype(F32)
        g = upstream[at(i, GROUP), :] * slope[at(i, GROUP), :]
        gx = g * xhat
        low[at(i, GROUP), :] = norm_back(
            g * gain, xhat, rstd_ref[at(i, GROUP), :][:, :1]
        ).astype(BF16)
        return (
            gain_sum + gx.reshape(GROUP // 8, 8, width).sum(0),
            shift_sum + g.reshape(GROUP // 8, 8, width).sum(0),
        )

    zero = jnp.zeros((8, width), F32)
    gain_sum, shift_sum = lax.fori_loop(0, rows // GROUP, body, (zero, zero), unroll=8)
    return col_sum(gain_sum), col_sum(shift_sum)


def group_matrix(width):
    return (
        lax.broadcasted_iota(jnp.int32, (width, width), 0) // SIMNORM
        == lax.broadcasted_iota(jnp.int32, (width, width), 1) // SIMNORM
    ).astype(BF16)


def group_sums(values, groups):
    parts = []
    for k in range(values.shape[1] // 128):
        part = values[:, k * 128 : (k + 1) * 128]
        high = part.astype(BF16)
        rest = (part - high.astype(F32)).astype(BF16)
        parts.append(dot(high, groups) + dot(rest, groups))
    return jnp.concatenate(parts, 1)


def simnorm_forward(z, gain, shift, xhat_ref, chance, rstd_ref, groups):
    def body(i):
        xhat, rstd = norm(z[at(i, 32), :])
        e = jnp.exp(xhat * gain + shift)
        xhat_ref[at(i, 32), :] = xhat
        chance[at(i, 32), :] = e / group_sums(e, groups)
        rstd_ref[at(i, 32), :] = jnp.broadcast_to(rstd, (32, 128))

    loop(z.shape[0] // 32, body, 4)


def simnorm_backward(upstream, gain, xhat_ref, chance, rstd_ref, groups, low):
    width = gain.shape[1]

    def body(i, carry):
        gain_sum, shift_sum = carry
        xhat = xhat_ref[at(i, 32), :]
        p = chance[at(i, 32), :]
        w = upstream[at(i, 32), :] * p
        g = w - p * group_sums(w, groups)
        gx = g * xhat
        low[at(i, 32), :] = norm_back(g * gain, xhat, rstd_ref[at(i, 32), :][:, :1]).astype(BF16)
        return (
            gain_sum + gx.reshape(4, 8, width).sum(0),
            shift_sum + g.reshape(4, 8, width).sum(0),
        )

    zero = jnp.zeros((8, width), F32)
    gain_sum, shift_sum = lax.fori_loop(0, upstream.shape[0] // 32, body, (zero, zero), unroll=4)
    return col_sum(gain_sum), col_sum(shift_sum)


ORDERS = {
    "As": ("c", "z0", "y", "z1", "x"),
    "Bs": ("c", "z0", "x", "z1", "y"),
    "D2": ("c", "z0", "x", "y", "z1"),
    "D3": ("c", "x", "y", "z0", "z1"),
    "E2": ("c", "y", "x", "z0", "z1"),
    "D1": ("c", "y", "z0", "z1", "x"),
    "E1": ("c", "x", "z0", "z1", "y"),
    "A0": ("c", "z0", "y", "z1"),
    "B0": ("c", "z0", "y", "z1"),
    "A1": ("c", "z0", "y", "z1"),
    "B1": ("c", "z0", "y", "z1"),
}
SCHEDULE = {
    ("c", 0): [("L0", -1)],
    ("c", 1): [("L1", -1)],
    ("c", 2): [("L2", -1)],
    ("s", 1): [("L0", 0), ("L1", 0), ("L2", 0)],
    ("s", 4): [("As", -1)],
    ("s", 6): [("Bs", -1)],
    ("s", 7): [("As", 0)],
    (0, 1): [("Bs", 0)],
    (0, 4): [("A0", -1), ("As", 1)],
    (0, 5): [("A0", 0)],
    (0, 6): [("Bs", 1), ("B0", -1)],
    (0, 7): [("As", 2)],
    (1, 1): [("B0", 0)],
    (1, 2): [("Bs", 2)],
    (1, 3): [("A0", 1), ("As", 3)],
    (1, 4): [("A1", -1), ("As", 4)],
    (1, 5): [("As", 5), ("A1", 0), ("A0", 2), ("B0", 1)],
    (1, 6): [("B1", -1), ("As", 6), ("Bs", 3)],
    ("t", 0): [("R2", -1), ("R1", -1), ("R0", -1)],
    ("t", 1): [("B1", 0), ("B0", 2)],
    ("t", 2): [("Bs", 4)],
    ("t", 3): [("R2", 0)],
    ("t", 4): [("R1", 0)],
    ("t", 5): [("A1", 1)],
    ("t", 6): [("R0", 0), ("A0", 3), ("Bs", 5)],
    ("t", 8): [("Bs", 6)],
    ("t", 9): [("A0", 4), ("A1", 2)],
    ("t", 10): [("D2", -1)],
    ("t", 11): [("B1", 1), ("D1", -1), ("A0", 5), ("D2", 0)],
    ("t", 12): [("D3", -1), ("B0", 3), ("D1", 0)],
    ("t", 13): [("A1", 3), ("B1", 2), ("D3", 0), ("B0", 4)],
    ("t", 14): [("E2", -1)],
    ("t", 15): [("E1", -1)],
    ("t", 16): [("S", -1)],
    ("t", 17): [("B0", 5), ("E2", 0), ("E1", 0), ("S", 0), ("A1", 4), ("D1", 1), ("A1", 5), ("D2", 1), ("D3", 1), ("B1", 3), ("E2", 1), ("E1", 1), ("S", 1), ("D1", 2), ("D3", 2), ("E1", 2), ("S", 2), ("D3", 3), ("D2", 2), ("D1", 3), ("E1", 3), ("S", 3), ("B1", 4), ("D3", 4), ("B1", 5), ("E2", 2), ("D2", 3), ("E1", 4), ("D1", 4), ("D3", 5), ("S", 4), ("E1", 5), ("E2", 3), ("D3", 6), ("D1", 5), ("E1", 6), ("D2", 4), ("S", 5), ("D1", 6), ("E2", 4), ("S", 6), ("D2", 5), ("E2", 5), ("D2", 6), ("E2", 6)],
}


class Piece:
    def __init__(self, index, order, buffers, gathered, credit=None, gives=False):
        self.index, self.order, self.buffers, self.gathered = index, order, buffers, gathered
        self.credit, self.gives = credit, gives
        self.stages = len(order) + 2


class Exchange:
    def __init__(self, send_sem, recv_sem, free_sem):
        self.send_sem, self.recv_sem, self.free_sem = send_sem, recv_sem, free_sem
        section, dp = lax.axis_index("section"), lax.axis_index("dp")
        self.bit = {
            "c": section % 2,
            "x": section // 2,
            "y": dp % 2,
            "z0": (dp // 2) % 2,
            "z1": dp // 4,
        }
        self.partner = {
            "c": {"section": section + 1 - 2 * self.bit["c"]},
            "x": {"section": section + 2 - 4 * self.bit["x"]},
            "y": {"dp": dp + 1 - 2 * self.bit["y"]},
            "z0": {"dp": dp + 2 - 4 * self.bit["z0"]},
            "z1": {"dp": dp + 4 - 8 * self.bit["z1"]},
        }

    def greet(self):
        barrier = pltpu.get_barrier_semaphore()
        for axis in self.partner:
            self.signal(barrier, axis)
        pl.semaphore_wait(barrier, len(self.partner))

    def signal(self, sem, axis):
        pl.semaphore_signal(
            sem, inc=1, device_id=self.partner[axis], device_id_type=pl.DeviceIdType.MESH
        )

    def remote(self, source, target, index, stage, axis):
        return pltpu.make_async_remote_copy(
            src_ref=source,
            dst_ref=target,
            send_sem=self.send_sem.at[index, stage],
            recv_sem=self.recv_sem.at[index, stage],
            device_id=self.partner[axis],
            device_id_type=pl.DeviceIdType.MESH,
        )

    def place(self, order, rank, quarter):
        bits = {
            "c": quarter // 2,
            "x": quarter % 2,
            "y": rank % 2,
            "z0": (rank // 2) % 2,
            "z1": rank // 4,
        }
        index = 0
        for axis in order if len(order) == 5 else order + ("x",):
            index = index * 2 + bits[axis]
        return index

    def copy(self, piece, stage):
        c, x = self.bit["c"], self.bit["x"]
        count = len(piece.order)
        if stage < count:
            axis = piece.order[stage]
            half = 32 >> (stage + 1)
            source = piece.buffers[stage].at[pl.ds((1 - self.bit[axis]) * half, half)]
            target = piece.buffers[stage + 1]
        elif stage == count:
            axis = "x"
            source = target = piece.gathered.at[c, x]
        else:
            axis = "c"
            source = target = piece.gathered.at[c]
        return self.remote(source, target, piece.index, stage, axis)

    def begin(self, piece):
        if piece.credit is not None:
            pl.semaphore_wait(self.free_sem.at[piece.credit], 1)
        self.copy(piece, 0).start()

    def advance(self, piece, stage):
        self.copy(piece, stage).wait()
        count = len(piece.order)
        if stage < count:
            half = 32 >> (stage + 1)
            first = self.bit[piece.order[stage]] * half
            kept, total = piece.buffers[stage], piece.buffers[stage + 1]
            if stage < count - 1:

                def add(i):
                    total[i] = total[i] + kept[first + i]

                loop(half, add)
            else:
                for i in range(half):
                    piece.gathered[self.bit["c"], self.bit["x"], i] = total[i] + kept[first + i]
        if stage == 1 and piece.gives is not False:
            self.signal(self.free_sem.at[piece.gives], "c")
        if stage + 1 < piece.stages:
            self.copy(piece, stage + 1).start()


class Sums:
    def __init__(self, index, parts, gathered, exchange):
        self.index, self.parts, self.gathered, self.exchange = index, parts, gathered, exchange
        self.stages = 7

    def copy(self, stage):
        parts = self.parts
        c, x = self.exchange.bit["c"], self.exchange.bit["x"]
        if stage == 0:
            axis, source, target = "c", parts[0].at[pl.ds((1 - c) * 2, 2)], parts[1]
        elif stage == 1:
            axis, source, target = "x", parts[1].at[1 - x], parts[2]
        elif stage < 5:
            axis, source, target = ("y", "z0", "z1")[stage - 2], parts[stage], parts[stage + 1]
        elif stage == 5:
            axis = "x"
            source = target = self.gathered.at[c * 2 + x]
        else:
            axis = "c"
            source = target = self.gathered.at[pl.ds(c * 2, 2)]
        return self.exchange.remote(source, target, self.index, stage, axis)

    def begin(self):
        self.copy(0).start()

    def advance(self, stage):
        parts = self.parts
        c, x = self.exchange.bit["c"], self.exchange.bit["x"]
        self.copy(stage).wait()
        if stage == 0:
            parts[1][...] = parts[1][...] + parts[0][pl.ds(c * 2, 2)]
        elif stage == 1:
            parts[2][...] = parts[2][...] + parts[1][x]
        elif stage < 4:
            parts[stage + 1][...] = parts[stage + 1][...] + parts[stage][...]
        elif stage == 4:
            self.gathered[c * 2 + x] = parts[5][...] + parts[4][...]
        if stage + 1 < self.stages:
            self.copy(stage + 1).start()


def step_kernel(
    sizes,
    feat_ref,
    ids_ref,
    low_ref,
    frac_ref,
    mask_ref,
    task_ref,
    param_ref,
    goals_ref,
    we1_ref,
    we2_ref,
    wd1_ref,
    wd2_ref,
    wd3_ref,
    wv1_ref,
    wv2_ref,
    wv3_ref,
    ga_ref,
    ga_pair_ref,
    gb_ref,
    gb_pair_ref,
    ge_ref,
    small_ref,
    obs_grad_ref,
    goals,
    we1_raw,
    we1,
    we2,
    wd1,
    wd1_rest,
    wd2,
    wd3,
    wv1,
    wv1_rest,
    wv2,
    wv3_raw,
    wv3,
    x_enc,
    x_all,
    x_turned,
    turned,
    onehot,
    target,
    z_chain,
    slope_chain,
    rstd_chain,
    hid_chain,
    z_lat,
    lat,
    rstd_lat,
    dz_lat,
    z1,
    s1,
    r1,
    h1,
    z2,
    s2,
    r2,
    h2,
    up,
    dz,
    dlog,
    dx,
    lat_in,
    dx_out,
    dx_in,
    pa,
    pb,
    pe,
    half_a,
    half_b,
    half_e,
    last_a,
    last_b,
    last_e,
    all_a,
    all_a_pair,
    all_b,
    all_b_pair,
    all_e,
    small,
    small_parts,
    small_all,
    chain_sem,
    goal_sem,
    value_sem,
    out_sem,
    send_sem,
    recv_sem,
    free_sem,
):
    micro_total, observed, moves, task_width, bins, heads = sizes
    horizon, _, rows, latent_width = goals_ref.shape
    tasks = task_ref.shape[0]
    hidden = wv2_ref.shape[1]
    inputs = wv1_ref.shape[1]
    rest = inputs - latent_width
    total = horizon * rows
    ranks = hidden // 128
    part_rows, rest_rows = pb.shape[1], pa.shape[1]
    section = lax.axis_index("section")
    exchange = Exchange(send_sem, recv_sem, free_sem)
    x_bit = exchange.bit["x"]
    micros = (section, section + 2 - 4 * x_bit)
    own_heads = heads // 2
    shared = heads - 1

    pieces = {}

    def piece(name, own, half, last, gathered, credit=None, gives=False):
        order = ORDERS[name]
        buffers = [own, half] + last
        pieces[name] = Piece(len(pieces), order, buffers, gathered, credit, gives)

    def lasts(refs, k, lanes=None):
        views = [ref.at[k] for ref in refs]
        return views if lanes is None else [view.at[:, :, lanes] for view in views]

    left, right = pl.ds(0, latent_width), pl.ds(latent_width, latent_width)
    piece("As", pa, half_a.at[0], lasts(last_a, 0), all_a.at[0], None, 0)
    piece("A0", pa, half_a.at[1], lasts(last_a, 1), all_a_pair.at[0], None, 1)
    piece("A1", pa, half_a.at[0], lasts(last_a, 2), all_a_pair.at[1], 0, 0)
    piece("D2", pa, half_a.at[1], lasts(last_a, 3), all_a.at[1], 1)
    piece("D3", pa.at[:, :, left], half_a.at[0, :, :, left], lasts(last_a, 4, left), all_a.at[2, :, :, :, :, left], 0)
    piece("E2", pa.at[:, :, right], half_a.at[0, :, :, right], lasts(last_a, 4, right), all_a.at[2, :, :, :, :, right])
    piece("Bs", pb, half_b, lasts(last_b, 0), all_b.at[0], None, 2)
    piece("B0", pb, half_b, lasts(last_b, 1), all_b_pair.at[0], 2, 2)
    piece("B1", pb, half_b, lasts(last_b, 2), all_b_pair.at[1], 2, 2)
    piece("D1", pb, half_b, lasts(last_b, 3), all_b.at[1], 2)
    piece("E1", pe, half_e, list(last_e), all_e)
    sums = Sums(len(pieces), [small, *small_parts], small_all, exchange)
    swaps = len(pieces) + 1

    def swap(name):
        t = int(name[1])
        if name[0] == "L":
            source, target_ref, stage = x_all.at[pl.ds(t * rows, rows), pl.ds(0, latent_width)], lat_in.at[t], t
        else:
            source, target_ref, stage = dx_out.at[t], dx_in.at[t], horizon + t
        return exchange.remote(source, target_ref, swaps, stage, "x")

    def act(name, stage):
        if name[0] in "LR":
            if stage < 0:
                swap(name).start()
            else:
                swap(name).wait()
        elif name == "S":
            if stage < 0:
                sums.begin()
            else:
                sums.advance(stage)
        elif stage < 0:
            exchange.begin(pieces[name])
        else:
            exchange.advance(pieces[name], stage)

    def tick(*key):
        for name, stage in SCHEDULE.get(key, ()):
            act(name, stage)

    def pair_tick(k, point):
        for own in range(own_heads):
            if (own, point) in SCHEDULE:
                pl.when(k == own)(functools.partial(tick, own, point))

    def chain_copies():
        return [
            pltpu.make_async_copy(source, place, chain_sem.at[k])
            for k, (source, place) in enumerate(
                (
                    (we1_ref, we1_raw),
                    (we2_ref, we2),
                    (wd1_ref, wd1),
                    (wd2_ref, wd2),
                    (wd3_ref, wd3),
                )
            )
        ]

    def value_copy(q, index):
        source, place = ((wv1_ref, wv1), (wv2_ref, wv2), (wv3_ref, wv3_raw))[index]
        return pltpu.make_async_copy(source.at[q], place, value_sem.at[index])

    for copy in chain_copies():
        copy.start()
    for index in range(3):
        value_copy(shared, index).start()
    goal_copies = [
        pltpu.make_async_copy(goals_ref.at[t, section], goals.at[t], goal_sem.at[t]) for t in range(horizon)
    ]
    for copy in goal_copies:
        copy.start()

    small[...] = jnp.zeros_like(small)
    we1[...] = jnp.zeros_like(we1)
    wd1_rest[...] = jnp.zeros_like(wd1_rest)
    wv1_rest[...] = jnp.zeros_like(wv1_rest)
    wv3[...] = jnp.zeros_like(wv3)
    turned[...] = jnp.zeros_like(turned)
    groups = group_matrix(128)

    def pick(ref, micro):
        out = jnp.zeros((1, rows), ref.dtype)
        for m in range(micro_total):
            out = out + jnp.where(micro == m, ref[m : m + 1, :], jnp.zeros((1, rows), ref.dtype))
        return out

    mask = mask_ref[...].astype(F32).astype(BF16)
    for j, micro in enumerate(micros):
        hot = (lax.broadcasted_iota(jnp.int32, (tasks, rows), 0) == pick(ids_ref, micro)).astype(BF16)
        onehot[j] = hot
        embedded = dot_left(task_ref[...], hot)
        allowed = dot(mask, hot)
        feats = feat_ref[:, pl.ds(pl.multiple_of(micro * rows, rows), rows)].astype(F32)
        turned[moves:rest, :] = embedded
        for t in range(horizon):
            start = observed + moves * t
            turned[0:moves, :] = feats[start : start + moves, :] * allowed
            at_rows = slice((j * horizon + t) * rows, (j * horizon + t + 1) * rows)
            x_turned[latent_width:, at_rows] = turned[:128, :].astype(BF16)
            x_all[at_rows, latent_width:] = turned[:128, :].T.astype(BF16)
            bin_at = lax.broadcasted_iota(jnp.int32, (128, rows), 0)
            lower, upper_part = pick(low_ref.at[t], micro), pick(frac_ref.at[t], micro)
            target[at_rows, :] = (
                jnp.where(bin_at == lower, 1.0 - upper_part, 0.0) + jnp.where(bin_at == lower + 1, upper_part, 0.0)
            ).T
        if j == 0:
            turned[0:observed, :] = feats[0:observed, :]
            turned[observed : observed + task_width, :] = embedded
            x_enc[:, :128] = turned[:128, :].T.astype(BF16)
            x_enc[:, 128:] = turned[128:, :].T.astype(BF16)
            turned[...] = jnp.zeros_like(turned)

    def vec(index):
        return param_ref[index : index + 1, :]

    wide_up = up.at[pl.ds(0, rows), :]
    carry_up = up.at[pl.ds(0, rows), pl.ds(0, latent_width)]

    def mish_layer(index, slot):
        mish_forward(
            wide_up,
            vec(index),
            vec(index + 1),
            hid_chain.at[slot],
            z_chain.at[slot],
            slope_chain.at[slot],
            rstd_chain.at[slot],
        )

    def latent_layer(weight, hidden_slot, index, slot):
        carry_up[...] = dot(hid_chain[hidden_slot], weight[...])
        simnorm_forward(
            carry_up,
            vec(index)[:, :latent_width],
            vec(index)[:, latent_width:],
            z_lat.at[slot],
            lat.at[slot],
            rstd_lat.at[slot],
            groups,
        )

    copies = chain_copies()
    copies[0].wait()
    we1[: observed + task_width, :] = we1_raw[...]
    wide_up[...] = dot(x_enc[...], we1[...])
    mish_layer(0, 0)
    copies[1].wait()
    latent_layer(we2, 0, 2, 0)
    copies[2].wait()
    copies[3].wait()
    copies[4].wait()
    wd1_rest[:rest, :] = wd1[latent_width:, :]
    exchange.greet()
    for t in range(horizon):
        own = slice(t * rows, (t + 1) * rows)
        x_all[own, :latent_width] = lat[t].astype(BF16)
        tick("c", t)
        wide_up[...] = dot(x_all[own, :latent_width], wd1[:latent_width, :]) + dot(
            x_all[own, latent_width:], wd1_rest[...]
        )
        mish_layer(3, 1 + 2 * t)
        wide_up[...] = dot(hid_chain[1 + 2 * t], wd2[...])
        mish_layer(5, 2 + 2 * t)
        latent_layer(wd3, 2 + 2 * t, 7, t + 1)
    x_turned[:latent_width, :total] = x_all[:total, :latent_width].T

    def put_rows(order, own, rank, block, lanes=slice(None)):
        low = block.astype(BF16)
        for k in range(low.shape[0] // rest_rows):
            place = exchange.place(order, rank + k // 4, k % 4)
            own[place, :, lanes] = low[k * rest_rows : (k + 1) * rest_rows]

    def put_lanes(order, own, rank, block, begin=0):
        low = block.astype(BF16)
        quarter_rows = own.shape[1]
        for k in range(low.shape[1] // 128):
            done = 0
            while done < low.shape[0]:
                quarter, offset = divmod(begin + done, quarter_rows)
                count = min(quarter_rows - offset, low.shape[0] - done)
                place = exchange.place(order, rank + k, quarter)
                own[place, offset : offset + count, :] = low[done : done + count, k * 128 : (k + 1) * 128]
                done += count

    def head(q, count, order_a, order_b, after, following, fresh):
        block = param_ref[pl.ds(pl.multiple_of(8 * (q + 1), 8), 8), :]
        first_gain, first_shift, second_gain, second_shift, bias = (block[k : k + 1, :] for k in range(5))
        here = pl.ds(0, count)

        def prefetch(index):
            if following is not None:
                nxt, condition = following
                if condition is None:
                    value_copy(nxt, index).start()
                else:
                    pl.when(condition)(lambda: value_copy(nxt, index).start())

        value_copy(q, 0).wait()
        wv1_rest[:rest, :] = wv1[latent_width:, :]
        up[here, :] = dot(x_all[here, :latent_width], wv1[:latent_width, :]) + dot(
            x_all[here, latent_width:], wv1_rest[...]
        )
        mish_forward(up.at[here, :], first_gain, first_shift, h1.at[here, :], z1.at[here, :], s1.at[here, :], r1.at[here, :])
        after(1)
        value_copy(q, 1).wait()
        up[here, :] = dot(h1[here, :], wv2[...])
        mish_forward(up.at[here, :], second_gain, second_shift, h2.at[here, :], z2.at[here, :], s2.at[here, :], r2.at[here, :])
        after(2)
        value_copy(q, 2).wait()
        wv3[:bins, :] = wv3_raw[...]
        prefetch(2)
        valid = lax.broadcasted_iota(jnp.int32, (1, 128), 1) < bins
        bias_sum = jnp.zeros((1, 128), F32)
        for k in range(count // rows):
            factor = value_weight * discount ** (k % horizon) / (heads * micro_total)
            own = slice(k * rows, (k + 1) * rows)
            logits = jnp.where(valid, dot_right(h2[own, :], wv3[...]) + bias[:, :128], -1e30)
            e = jnp.exp(logits - jnp.max(logits, -1, keepdims=True))
            delta = factor * (e / row_sum(e) - target[own, :])
            dlog[own, :] = delta.astype(BF16)
            bias_sum = bias_sum + col_sum(delta)
        up[here, :] = dot(dlog[here, :], wv3[...])
        second_sums = mish_backward(
            up.at[here, :], second_gain, z2.at[here, :], s2.at[here, :], r2.at[here, :], dz.at[here, :]
        )
        after(3)
        for part in range(2):
            columns = pl.ds(part * (hidden // 2), hidden // 2)
            put_rows(order_a, pa, part * (ranks // 2), dot_left(h1[here, columns], dz[here, :]))
        after(4)
        up[here, :] = dot_right(dz[here, :], wv2[...])
        prefetch(1)
        first_sums = mish_backward(
            up.at[here, :], first_gain, z1.at[here, :], s1.at[here, :], r1.at[here, :], dz.at[here, :]
        )
        after(5)
        for part in range(2):
            columns = pl.ds(part * (hidden // 2), hidden // 2)
            put_lanes(order_b, pb, part * (ranks // 2), dot(x_turned[:, here], dz[here, columns]))
        put_lanes(order_b, pb, 0, dot_left(dlog[here, :], h2[here, :]), latent_width + 128)
        after(6)
        main = dot_right(dz[here, :], wv1[:latent_width, :])
        tail = dot_right(dz[here, :], wv1_rest[...])
        prefetch(0)
        if fresh:
            dx[:fresh, :latent_width] = dx[:fresh, :latent_width] + main[:fresh]
            dx[:fresh, latent_width:] = dx[:fresh, latent_width:] + tail[:fresh]
        if fresh < count:
            dx[fresh:count, :latent_width] = main[fresh:]
            dx[fresh:count, latent_width:] = tail[fresh:]
        pad = jnp.zeros((1, hidden - 128), F32)
        small[(q + 1) // 2, pl.ds(pl.multiple_of((q + 1) % 2 * 8, 8), 8), :] = jnp.concatenate(
            [*first_sums, *second_sums, jnp.concatenate([bias_sum, pad], 1), jnp.zeros((3, hidden), F32)], 0
        )
        after(7)

    head(
        jnp.int32(shared),
        total,
        ORDERS["As"],
        ORDERS["Bs"],
        functools.partial(tick, "s"),
        (x_bit * own_heads, None),
        0,
    )
    tick("s", 8)
    for t in range(horizon):
        x_all[total + t * rows : total + (t + 1) * rows, :latent_width] = lat_in[t]
    x_turned[:latent_width, total:] = x_all[total:, :latent_width].T
    dx[total:, :] = jnp.zeros_like(dx[total:, :])

    def pair_head(k):
        q = x_bit * own_heads + k
        head(
            q,
            2 * total,
            ORDERS["A0"],
            ORDERS["B0"],
            functools.partial(pair_tick, k),
            (q + 1, k + 1 < own_heads),
            2 * total,
        )

    loop(own_heads, pair_head)

    for t in range(horizon):
        dx_out[t] = dx[total + t * rows : total + (t + 1) * rows, :latent_width].astype(BF16)
    tick("t", 0)
    for copy in goal_copies:
        copy.wait()
    embed_sums = []
    for j in range(2):
        parts = [dx[(j * horizon + t) * rows : (j * horizon + t + 1) * rows, latent_width:] for t in range(horizon)]
        embed_sums.append(sum(parts[1:], parts[0]))
    dz_one, dz_two = dz.at[pl.ds(0, total), :], dz.at[pl.ds(total, total), :]
    lat_sums = two_sums = one_sums = None

    def added(old, new):
        return new if old is None else [a + b for a, b in zip(old, new)]

    gain_lat = vec(7)[:, :latent_width]
    carry = None
    point = 1
    for t in reversed(range(horizon)):
        factor = 2.0 * consistency_weight * discount**t / (micro_total * latent_width)
        upstream = factor * (lat[t + 1] - goals[t].astype(F32))
        if carry is not None:
            upstream = upstream + carry
        carry_up[...] = upstream
        own = pl.ds(t * rows, rows)
        one, two = 1 + 2 * t, 2 + 2 * t
        lat_sums = added(
            lat_sums,
            simnorm_backward(
                carry_up, gain_lat, z_lat.at[t + 1], lat.at[t + 1], rstd_lat.at[t + 1], groups, dz_lat.at[own, :]
            ),
        )
        wide_up[...] = dot_right(dz_lat[own, :], wd3[...])
        two_sums = added(
            two_sums,
            mish_backward(
                wide_up, vec(5), z_chain.at[two], slope_chain.at[two], rstd_chain.at[two], dz_two.at[own, :]
            ),
        )
        tick("t", point)
        wide_up[...] = dot_right(dz_two[own, :], wd2[...])
        one_sums = added(
            one_sums,
            mish_backward(
                wide_up, vec(3), z_chain.at[one], slope_chain.at[one], rstd_chain.at[one], dz_one.at[own, :]
            ),
        )
        tick("t", point + 1)
        latent_delta = dot_right(dz_one[own, :], wd1[:latent_width, :])
        embed_sums[0] = embed_sums[0] + dot_right(dz_one[own, :], wd1_rest[...])
        tick("t", point + 2)
        carry = (
            latent_delta.astype(BF16).astype(F32)
            + dx[t * rows : (t + 1) * rows, :latent_width]
            + dx_in[t].astype(F32)
        )
        point += 3
    small[0, 3:8, :] = jnp.concatenate([*one_sums, *two_sums, jnp.concatenate(lat_sums, 1)], 0)

    def put_chain(order, grad, first, lanes=slice(None)):
        for part in range(2):
            columns = pl.ds(part * (hidden // 2), hidden // 2)
            block = None
            for t in range(horizon):
                product = dot_left(hid_chain[first + 2 * t, :, columns], grad[t * rows : (t + 1) * rows, :])
                block = product if block is None else block + product
            put_rows(order, pa, part * (ranks // 2), block, lanes)

    put_chain(ORDERS["D2"], dz_two, 1)
    tick("t", 10)
    for part in range(2):
        columns = pl.ds(part * (hidden // 2), hidden // 2)
        put_lanes(ORDERS["D1"], pb, part * (ranks // 2), dot(x_turned[:, :total], dz_one[:, columns]))
    tick("t", 11)
    put_chain(ORDERS["D3"], dz_lat, 2, slice(0, latent_width))
    tick("t", 12)

    carry_up[...] = carry
    low_lat = dz_lat.at[pl.ds(0, rows), :]
    encoder_lat = simnorm_backward(
        carry_up, vec(2)[:, :latent_width], z_lat.at[0], lat.at[0], rstd_lat.at[0], groups, low_lat
    )
    wide_up[...] = dot_right(low_lat[...], we2[...])
    low_one = dz_one.at[pl.ds(0, rows), :]
    encoder_one = mish_backward(wide_up, vec(0), z_chain.at[0], slope_chain.at[0], rstd_chain.at[0], low_one)
    small[0, 0:3, :] = jnp.concatenate([*encoder_one, jnp.concatenate(encoder_lat, 1)], 0)
    tick("t", 13)
    put_rows(
        ORDERS["E2"], pa, 0, dot_left(hid_chain[0], low_lat[...]), slice(latent_width, 2 * latent_width)
    )
    tick("t", 14)
    put_lanes(ORDERS["E1"], pe, 0, dot_left(x_enc[...], low_one[...])[: 4 * pe.shape[1]])
    tick("t", 15)
    enc_up = dot_right(low_one[...], we1[...])
    obs_grad_ref[...] = enc_up[:, :128].T[:observed, :]
    embed_sums[0] = embed_sums[0] + pltpu.roll(enc_up, x_enc.shape[1] - observed + moves, 1)[:, :128]
    table = None
    for j in range(2):
        high = embed_sums[j].astype(BF16)
        low = (embed_sums[j] - high.astype(F32)).astype(BF16)
        part = dot(onehot[j], high) + dot(onehot[j], low)
        table = part if table is None else table + part
    for k in range(tasks // 8):
        small[3, (k // 8) * 8 : (k // 8) * 8 + 8, (k % 8) * 128 : (k % 8) * 128 + 128] = table[k * 8 : k * 8 + 8]
    tick("t", 16)
    tick("t", 17)
    outs = [
        pltpu.make_async_copy(source, place, out_sem.at[k])
        for k, (source, place) in enumerate(
            (
                (all_a, ga_ref),
                (all_a_pair, ga_pair_ref),
                (all_b, gb_ref),
                (all_b_pair, gb_pair_ref),
                (all_e, ge_ref),
            )
        )
    ]
    for copy in outs:
        copy.start()
    small_ref[...] = small_all[...]
    for copy in outs:
        copy.wait()


def finish_kernel(
    sizes,
    ga_from,
    ga_pair_from,
    gb_from,
    gb_pair_from,
    ge_from,
    small_from,
    table_ref,
    encoder_first,
    encoder_first_gain,
    encoder_first_shift,
    encoder_second,
    encoder_second_gain,
    encoder_second_shift,
    dynamics_first,
    dynamics_first_gain,
    dynamics_first_shift,
    dynamics_second,
    dynamics_second_gain,
    dynamics_second_shift,
    dynamics_third,
    dynamics_third_gain,
    dynamics_third_shift,
    value_first,
    value_first_gain,
    value_first_shift,
    value_second,
    value_second_gain,
    value_second_shift,
    value_third,
    value_bias,
    ga_ref,
    ga_pair_ref,
    gb_ref,
    gb_pair_ref,
    ge_ref,
    small_ref,
    sem,
):
    copies = [
        pltpu.make_async_copy(source, place, sem.at[k])
        for k, (source, place) in enumerate(
            (
                (ga_from, ga_ref),
                (ga_pair_from, ga_pair_ref),
                (gb_from, gb_ref),
                (gb_pair_from, gb_pair_ref),
                (ge_from, ge_ref),
                (small_from, small_ref),
            )
        )
    ]
    for copy in copies:
        copy.start()
    for copy in copies:
        copy.wait()
    _, _, moves, task_width, bins, heads = sizes
    rest_rows, part_rows = ga_ref.shape[4], gb_ref.shape[4]
    inputs = dynamics_first.shape[0]
    latent_width = dynamics_third.shape[1]
    encoder_rows = encoder_first.shape[0]
    third_at = 4 * part_rows - 128
    own_heads = heads // 2

    def move(target, first_row, block):
        count = min(target.shape[0] - first_row, block.shape[0])
        if count > 0:
            target[first_row : first_row + count, :] = block[:count].astype(F32)

    for c in range(2):
        for x in range(2):
            quarter = c * 2 + x
            move(value_second.at[heads - 1], quarter * rest_rows, ga_ref[0, c, x, 0])
            move(dynamics_second, quarter * rest_rows, ga_ref[1, c, x, 0])
            move(dynamics_third, quarter * rest_rows, ga_ref[2, c, x, 0, :, :latent_width])
            move(encoder_second, quarter * rest_rows, ga_ref[2, c, x, 0, :, latent_width:])
            move(encoder_first, quarter * ge_ref.shape[3], ge_ref[c, x, 0])
            move(dynamics_first, quarter * part_rows, gb_ref[1, c, x, 0])
            for k in range(own_heads):
                for i in range(2):
                    move(value_second.at[x * own_heads + k], (c * 2 + i) * rest_rows, ga_pair_ref[k, c, x, i])

    def lanes(head, quarter, block):
        first = quarter * part_rows
        move(value_first.at[head], first, block)
        if first + part_rows > third_at:
            move(value_third.at[head], 0, block[third_at - first :])

    for quarter in range(4):
        lanes(heads - 1, quarter, gb_ref[0, quarter // 2, quarter % 2, 0])
        for x in range(2):
            for k in range(own_heads):
                lanes(x * own_heads + k, quarter, gb_pair_ref[k, quarter // 2, x, quarter % 2])

    def row(index):
        return small_ref[index // 16, index % 16 : index % 16 + 1, :]

    encoder_first_gain[...] = row(0)
    encoder_first_shift[...] = row(1)
    encoder_second_gain[...] = row(2)[:, :latent_width]
    encoder_second_shift[...] = row(2)[:, latent_width:]
    dynamics_first_gain[...] = row(3)
    dynamics_first_shift[...] = row(4)
    dynamics_second_gain[...] = row(5)
    dynamics_second_shift[...] = row(6)
    dynamics_third_gain[...] = row(7)[:, :latent_width]
    dynamics_third_shift[...] = row(7)[:, latent_width:]
    for q in range(heads):
        for k, target in enumerate((value_first_gain, value_first_shift, value_second_gain, value_second_shift)):
            target[q : q + 1, :] = row(8 + 8 * q + k)
        value_bias[q : q + 1, :] = row(8 + 8 * q + 4)[:, :bins]
    for k in range(table_ref.shape[0] // 8):
        block = small_ref[3, (k // 8) * 8 : (k // 8) * 8 + 8, (k % 8) * 128 : (k % 8) * 128 + 128]
        table_ref[k * 8 : k * 8 + 8, :] = block[:, moves : moves + task_width]


def mish_curve(values):
    return values * jnp.tanh(jax.nn.softplus(values))


def layer_norm(before, gain_vec, shift_vec):
    center = before - jnp.mean(before, -1, keepdims=True)
    spread = jnp.mean(center * center, -1, keepdims=True)
    return center * lax.rsqrt(spread + epsilon) * gain_vec + shift_vec


def sim_norm(values):
    groups = values.reshape(values.shape[:-1] + (values.shape[-1] // SIMNORM, SIMNORM))
    return jax.nn.softmax(groups, -1).reshape(values.shape)


def post_mish(before, gain_vec, shift_vec):
    return mish_curve(layer_norm(before, gain_vec, shift_vec))


def post_simnorm(before, gain_vec, shift_vec):
    return sim_norm(layer_norm(before, gain_vec, shift_vec))


def head_mish(before, gain_vec, shift_vec):
    return post_mish(before, gain_vec[:, None, :], shift_vec[:, None, :])


def matmul(left_side, right_side):
    return jnp.dot(left_side, right_side, preferred_element_type=jnp.float32)


def left_transposed(left_side, right_side):
    return lax.dot_general(
        left_side, right_side, (((0,), (0,)), ((), ())), preferred_element_type=jnp.float32
    )


def right_transposed(left_side, right_side):
    return lax.dot_general(
        left_side, right_side, (((1,), (1,)), ((), ())), preferred_element_type=jnp.float32
    )


def dense_forward(inputs, weight, gain_vec, shift_vec, after_fn):
    before = matmul(inputs, weight)
    return jax.vjp(after_fn, before, gain_vec.astype(jnp.float32), shift_vec.astype(jnp.float32))


def dense_backward(inputs, weight, puller, upstream):
    delta_before, delta_gain, delta_shift = puller(upstream)
    rounded = delta_before.astype(jnp.bfloat16)
    return (
        right_transposed(rounded, weight),
        left_transposed(inputs, rounded),
        delta_gain,
        delta_shift,
    )


def encoder_forward(encoder_params, observed, embedded):
    inputs = jnp.concatenate([observed, embedded], 1)
    hidden, first_pull = dense_forward(
        inputs, encoder_params[0], encoder_params[1], encoder_params[2], post_mish
    )
    hidden_low = hidden.astype(jnp.bfloat16)
    latent, second_pull = dense_forward(
        hidden_low, encoder_params[3], encoder_params[4], encoder_params[5], post_simnorm
    )
    return (latent, (inputs, hidden_low, first_pull, second_pull))


def encoder_backward(encoder_params, retained, upstream):
    inputs, hidden_low, first_pull, second_pull = retained
    delta_hidden, delta_second, second_gain, second_shift = dense_backward(
        hidden_low, encoder_params[3], second_pull, upstream
    )
    delta_inputs, delta_first, first_gain, first_shift = dense_backward(
        inputs, encoder_params[0], first_pull, delta_hidden
    )
    return (
        delta_inputs,
        (delta_first, first_gain, first_shift, delta_second, second_gain, second_shift),
    )


def dynamics_forward(dynamics_params, latent_in, action_low, embedded):
    inputs = jnp.concatenate([latent_in, action_low, embedded], 1)
    layer_one, first_pull = dense_forward(
        inputs, dynamics_params[0], dynamics_params[1], dynamics_params[2], post_mish
    )
    one_low = layer_one.astype(jnp.bfloat16)
    layer_two, second_pull = dense_forward(
        one_low, dynamics_params[3], dynamics_params[4], dynamics_params[5], post_mish
    )
    two_low = layer_two.astype(jnp.bfloat16)
    latent, third_pull = dense_forward(
        two_low, dynamics_params[6], dynamics_params[7], dynamics_params[8], post_simnorm
    )
    return (latent, (inputs, one_low, two_low, first_pull, second_pull, third_pull))


def dynamics_backward(dynamics_params, retained, upstream):
    inputs, one_low, two_low, first_pull, second_pull, third_pull = retained
    delta_two, delta_third, third_gain, third_shift = dense_backward(
        two_low, dynamics_params[6], third_pull, upstream
    )
    delta_one, delta_second, second_gain, second_shift = dense_backward(
        one_low, dynamics_params[3], second_pull, delta_two
    )
    delta_inputs, delta_first, first_gain, first_shift = dense_backward(
        inputs, dynamics_params[0], first_pull, delta_one
    )
    return (
        delta_inputs,
        (
            delta_first,
            first_gain,
            first_shift,
            delta_second,
            second_gain,
            second_shift,
            delta_third,
            third_gain,
            third_shift,
        ),
    )


def value_backward(value_params, inputs, bin_rows, fraction_rows, factor):
    first_before = jnp.einsum(
        "rk,qkn->qrn", inputs, value_params[0], preferred_element_type=jnp.float32
    )
    layer_one, first_pull = jax.vjp(
        head_mish,
        first_before,
        value_params[1].astype(jnp.float32),
        value_params[2].astype(jnp.float32),
    )
    one_low = layer_one.astype(jnp.bfloat16)
    second_before = jnp.einsum(
        "qrk,qkn->qrn", one_low, value_params[3], preferred_element_type=jnp.float32
    )
    layer_two, second_pull = jax.vjp(
        head_mish,
        second_before,
        value_params[4].astype(jnp.float32),
        value_params[5].astype(jnp.float32),
    )
    two_low = layer_two.astype(jnp.bfloat16)
    logits = (
        jnp.einsum("qrk,qkn->qrn", two_low, value_params[6], preferred_element_type=jnp.float32)
        + value_params[7].astype(jnp.float32)[:, None, :]
    )
    chances = jax.nn.softmax(logits, -1)
    columns = lax.broadcasted_iota(jnp.int32, (1, logits.shape[2]), 1)
    lower_bin = bin_rows[:, None]
    target = (1.0 - fraction_rows)[:, None] * (columns == lower_bin).astype(
        jnp.float32
    ) + fraction_rows[:, None] * (columns == lower_bin + 1).astype(jnp.float32)
    delta_logits = factor[None, :, None] * (chances - target[None])
    logit_low = delta_logits.astype(jnp.bfloat16)
    delta_bias = jnp.sum(delta_logits, 1)
    delta_third = jnp.einsum("qrk,qrn->qkn", two_low, logit_low, preferred_element_type=jnp.float32)
    delta_two = jnp.einsum(
        "qrn,qkn->qrk", logit_low, value_params[6], preferred_element_type=jnp.float32
    )
    before_two, second_gain, second_shift = second_pull(delta_two)
    two_round = before_two.astype(jnp.bfloat16)
    delta_second = jnp.einsum(
        "qrk,qrn->qkn", one_low, two_round, preferred_element_type=jnp.float32
    )
    delta_one = jnp.einsum(
        "qrn,qkn->qrk", two_round, value_params[3], preferred_element_type=jnp.float32
    )
    before_one, first_gain, first_shift = first_pull(delta_one)
    one_round = before_one.astype(jnp.bfloat16)
    delta_first = jnp.einsum("rk,qrn->qkn", inputs, one_round, preferred_element_type=jnp.float32)
    delta_inputs = jnp.einsum(
        "qrn,qkn->rk", one_round, value_params[0], preferred_element_type=jnp.float32
    )
    return (
        delta_inputs,
        (
            delta_first,
            first_gain,
            first_shift,
            delta_second,
            second_gain,
            second_shift,
            delta_third,
            delta_bias,
        ),
    )


def reduce_end(gradients):
    def reduced(index, axis):
        shard = lax.psum_scatter(
            gradients[index].astype(jnp.bfloat16), "dp", scatter_dimension=axis, tiled=True
        )
        return lax.psum(shard, "section").astype(jnp.float32)

    return tuple(
        reduced(index, axis)
        for index, axis in ((0, 1), (3, 0), (6, 1), (9, 0), (12, 0), (15, 2), (18, 1), (21, 1))
    )


def plain_device(
    observations,
    actions,
    action_mask,
    task_ids,
    targets,
    bin_low,
    bin_frac,
    task_table,
    encoder_first,
    encoder_first_gain,
    encoder_first_shift,
    encoder_second,
    encoder_second_gain,
    encoder_second_shift,
    dynamics_first,
    dynamics_first_gain,
    dynamics_first_shift,
    dynamics_second,
    dynamics_second_gain,
    dynamics_second_shift,
    dynamics_third,
    dynamics_third_gain,
    dynamics_third_shift,
    value_first,
    value_first_gain,
    value_first_shift,
    value_second,
    value_second_gain,
    value_second_shift,
    value_third,
    value_bias,
):
    encoder_params = (
        encoder_first,
        encoder_first_gain,
        encoder_first_shift,
        encoder_second,
        encoder_second_gain,
        encoder_second_shift,
    )
    dynamics_params = (
        dynamics_first,
        dynamics_first_gain,
        dynamics_first_shift,
        dynamics_second,
        dynamics_second_gain,
        dynamics_second_shift,
        dynamics_third,
        dynamics_third_gain,
        dynamics_third_shift,
    )
    value_params = (
        value_first,
        value_first_gain,
        value_first_shift,
        value_second,
        value_second_gain,
        value_second_shift,
        value_third,
        value_bias,
    )
    sections = lax.axis_size("section")
    level_now = lax.axis_index("section")
    micro_total = observations.shape[0]
    share = micro_total // sections
    latent_width = dynamics_third.shape[1]
    action_width = actions.shape[3]
    observed_width = observations.shape[2]
    horizon = actions.shape[0]
    heads = value_first.shape[0]
    task_count = task_table.shape[0]

    def mine(array, axis):
        part = lax.dynamic_slice_in_dim(array, level_now * share, share, axis)
        shape = part.shape
        return part.reshape(shape[:axis] + (shape[axis] * shape[axis + 1],) + shape[axis + 2 :])

    observed = mine(observations, 0)
    movement = mine(actions, 1)
    task_rows = mine(task_ids, 0)
    goals = mine(targets, 1)
    low_bins = mine(bin_low, 1)
    fractions = mine(bin_frac, 1)
    rows = observed.shape[0]
    onehot = (task_rows[:, None] == lax.broadcasted_iota(jnp.int32, (1, task_count), 1)).astype(
        jnp.bfloat16
    )
    embedded = matmul(onehot, task_table).astype(jnp.bfloat16)
    allowed = matmul(onehot, action_mask.astype(jnp.bfloat16))
    chosen = (movement.astype(jnp.float32) * allowed[None]).astype(jnp.bfloat16)

    latent, encoder_kept = encoder_forward(encoder_params, observed, embedded)
    latents = [latent]
    dynamics_kept = []
    for step in range(horizon):
        latent, kept = dynamics_forward(
            dynamics_params, latents[step].astype(jnp.bfloat16), chosen[step], embedded
        )
        latents.append(latent)
        dynamics_kept.append(kept)
    inputs = jnp.concatenate([kept[0] for kept in dynamics_kept], 0)
    step_weight = jnp.asarray(
        [value_weight * discount**step / (heads * micro_total) for step in range(horizon)],
        jnp.float32,
    )
    value_delta, value_grads = value_backward(
        value_params,
        inputs,
        low_bins.reshape(-1),
        fractions.reshape(-1),
        jnp.repeat(step_weight, rows),
    )
    value_delta = value_delta.reshape(horizon, rows, -1)
    upstream = jnp.zeros((rows, latent_width), jnp.float32)
    embed_delta = jnp.sum(value_delta[:, :, latent_width + action_width :], 0)
    dynamics_grads = None
    for step in reversed(range(horizon)):
        factor = 2.0 * consistency_weight * discount**step / (micro_total * latent_width)
        upstream = upstream + factor * (latents[step + 1] - goals[step].astype(jnp.float32))
        inputs_delta, step_grads = dynamics_backward(dynamics_params, dynamics_kept[step], upstream)
        dynamics_grads = (
            step_grads
            if dynamics_grads is None
            else tuple(a + b for a, b in zip(dynamics_grads, step_grads))
        )
        embed_delta = embed_delta + inputs_delta[:, latent_width + action_width :]
        upstream = (
            inputs_delta[:, :latent_width].astype(jnp.bfloat16).astype(jnp.float32)
            + value_delta[step, :, :latent_width]
        )
    inputs_delta, encoder_grads = encoder_backward(encoder_params, encoder_kept, upstream)
    observed_delta = inputs_delta[:, :observed_width]
    embed_delta = embed_delta + inputs_delta[:, observed_width:]
    table_sum = left_transposed(onehot.astype(jnp.float32), embed_delta)
    totals = encoder_grads + dynamics_grads + value_grads
    matrices = reduce_end(totals)
    small_sums = lax.psum(
        tuple(totals[i] for i in (1, 2, 4, 5, 7, 8, 10, 11, 13, 14, 16, 17, 19, 20, 22))
        + (table_sum,),
        ("section", "dp"),
    )
    return (
        observed_delta.reshape(share, rows // share, observed_width),
        small_sums[15],
        matrices[0],
        small_sums[0],
        small_sums[1],
        matrices[1],
        small_sums[2],
        small_sums[3],
        matrices[2],
        small_sums[4],
        small_sums[5],
        matrices[3],
        small_sums[6],
        small_sums[7],
        matrices[4],
        small_sums[8],
        small_sums[9],
        matrices[5],
        small_sums[10],
        small_sums[11],
        matrices[6],
        small_sums[12],
        small_sums[13],
        matrices[7],
        small_sums[14],
    )


def step_device(
    observations,
    actions,
    action_mask,
    task_ids,
    targets,
    bin_low,
    bin_frac,
    task_table,
    encoder_first,
    encoder_first_gain,
    encoder_first_shift,
    encoder_second,
    encoder_second_gain,
    encoder_second_shift,
    dynamics_first,
    dynamics_first_gain,
    dynamics_first_shift,
    dynamics_second,
    dynamics_second_gain,
    dynamics_second_shift,
    dynamics_third,
    dynamics_third_gain,
    dynamics_third_shift,
    value_first,
    value_first_gain,
    value_first_shift,
    value_second,
    value_second_gain,
    value_second_shift,
    value_third,
    value_bias,
):
    horizon, micro_total, rows, moves = actions.shape
    tasks, task_width = task_table.shape
    heads, inputs, hidden = value_first.shape
    latent_width = dynamics_third.shape[1]
    observed = observations.shape[2]
    bins = value_third.shape[2]
    enc_rows = ceil_to(observed + task_width, 256)
    in_rows = latent_width + 128
    total = horizon * rows
    ranks = hidden // 128
    sizes = (micro_total, observed, moves, task_width, bins, heads)
    feats = jnp.concatenate(
        [observations.transpose(2, 0, 1), actions.transpose(0, 3, 1, 2).reshape(horizon * moves, micro_total, rows)]
    ).reshape(-1, micro_total * rows)

    def joined(a, b):
        return jnp.pad(a, (0, hidden - a.shape[0])) + jnp.pad(b, (hidden - b.shape[0], 0))

    row_at = lax.broadcasted_iota(jnp.int32, (heads + 1, 8, hidden), 1)
    head_at = lax.broadcasted_iota(jnp.int32, (heads + 1, 8, hidden), 0)
    params = jnp.zeros((heads + 1, 8, hidden), BF16)
    for k, vector in enumerate(
        (
            encoder_first_gain,
            encoder_first_shift,
            joined(encoder_second_gain, encoder_second_shift),
            dynamics_first_gain,
            dynamics_first_shift,
            dynamics_second_gain,
            dynamics_second_shift,
            joined(dynamics_third_gain, dynamics_third_shift),
        )
    ):
        params = jnp.where((head_at == 0) & (row_at == k), vector[None, None, :], params)
    for k, vectors in enumerate(
        (
            value_first_gain,
            value_first_shift,
            value_second_gain,
            value_second_shift,
            jnp.pad(value_bias, ((0, 0), (0, hidden - bins))),
        )
    ):
        params = jnp.where((head_at > 0) & (row_at == k), jnp.pad(vectors, ((1, 0), (0, 0)))[:, None, :], params)
    params = params.astype(F32).reshape(-1, hidden)
    part_rows = (in_rows + 128) // 4
    rest_rows = hidden // (ranks * 4)
    enc_part = ceil_to(observed + task_width, 64) // 4
    chain = 1 + 2 * horizon
    pair = heads // 2
    vmem, anywhere = pl.BlockSpec(memory_space=pltpu.VMEM), pl.BlockSpec(memory_space=pl.ANY)
    names = len(ORDERS) + 2

    def gathered(count, blocks, block_rows, width):
        return (count, 2, 2, blocks, block_rows, width)

    shapes = (
        gathered(3, 1, rest_rows, hidden),
        gathered(pair, 2, rest_rows, hidden),
        gathered(2, 1, part_rows, 128),
        gathered(pair, 2, part_rows, 128),
        gathered(1, 1, enc_part, 128)[1:],
    )
    f32, bf16 = (lambda *shape: pltpu.VMEM(shape, F32)), (lambda *shape: pltpu.VMEM(shape, BF16))
    outs = pl.pallas_call(
        functools.partial(step_kernel, sizes),
        out_shape=tuple(jax.ShapeDtypeStruct(shape, BF16) for shape in shapes)
        + (
            jax.ShapeDtypeStruct((4, 16, hidden), F32),
            jax.ShapeDtypeStruct((observed, rows), F32),
        ),
        in_specs=[vmem] * 7 + [anywhere] * 9,
        out_specs=[anywhere] * 5 + [vmem] * 2,
        scratch_shapes=[
            bf16(horizon, rows, latent_width),
            bf16(observed + task_width, hidden),
            bf16(enc_rows, hidden),
            bf16(hidden, latent_width),
            bf16(inputs, hidden),
            bf16(128, hidden),
            bf16(hidden, hidden),
            bf16(hidden, latent_width),
            bf16(inputs, hidden),
            bf16(128, hidden),
            bf16(hidden, hidden),
            bf16(bins, hidden),
            bf16(128, hidden),
            bf16(rows, enc_rows),
            bf16(2 * total, in_rows),
            bf16(in_rows, 2 * total),
            f32(enc_rows, rows),
            bf16(2, tasks, rows),
            f32(2 * total, 128),
            bf16(chain, rows, hidden),
            bf16(chain, rows, hidden),
            f32(chain, rows, 128),
            bf16(chain, rows, hidden),
            f32(horizon + 1, rows, latent_width),
            f32(horizon + 1, rows, latent_width),
            f32(horizon + 1, rows, 128),
            bf16(total, latent_width),
        ]
        + [bf16(2 * total, hidden), bf16(2 * total, hidden), f32(2 * total, 128), bf16(2 * total, hidden)] * 2
        + [
            f32(2 * total, hidden),
            bf16(2 * total, hidden),
            bf16(2 * total, 128),
            f32(2 * total, in_rows),
            bf16(horizon, rows, latent_width),
            bf16(horizon, rows, latent_width),
            bf16(horizon, rows, latent_width),
            bf16(32, rest_rows, hidden),
            bf16(32, part_rows, 128),
            bf16(32, enc_part, 128),
            bf16(2, 16, rest_rows, hidden),
            bf16(16, part_rows, 128),
            bf16(16, enc_part, 128),
            [bf16(5, 8 >> k, rest_rows, hidden) for k in range(4)],
            [bf16(4, 8 >> k, part_rows, 128) for k in range(4)],
            [bf16(8 >> k, enc_part, 128) for k in range(4)],
            *(bf16(*shape) for shape in shapes),
            f32(4, 16, hidden),
            [f32(2, 16, hidden)] + [f32(16, hidden)] * 4,
            f32(4, 16, hidden),
            pltpu.SemaphoreType.DMA((5,)),
            pltpu.SemaphoreType.DMA((horizon,)),
            pltpu.SemaphoreType.DMA((3,)),
            pltpu.SemaphoreType.DMA((5,)),
            pltpu.SemaphoreType.DMA((names, 7)),
            pltpu.SemaphoreType.DMA((names, 7)),
            pltpu.SemaphoreType.REGULAR((3,)),
        ],
        compiler_params=pltpu.CompilerParams(
            collective_id=0, has_side_effects=True, vmem_limit_bytes=KERNEL_VMEM
        ),
    )(
        feats,
        task_ids,
        bin_low,
        bin_frac,
        action_mask.T,
        task_table,
        params,
        targets,
        encoder_first,
        encoder_second,
        dynamics_first,
        dynamics_second,
        dynamics_third,
        value_first,
        value_second,
        value_third.transpose(0, 2, 1),
    )

    def like(*shape):
        return jax.ShapeDtypeStruct(shape, F32)

    done = pl.pallas_call(
        functools.partial(finish_kernel, sizes),
        out_shape=(
            like(tasks, task_width),
            like(observed + task_width, 128),
            like(1, hidden),
            like(1, hidden),
            like(128, latent_width),
            like(1, latent_width),
            like(1, latent_width),
            like(inputs, 128),
            like(1, hidden),
            like(1, hidden),
            like(128, hidden),
            like(1, hidden),
            like(1, hidden),
            like(128, latent_width),
            like(1, latent_width),
            like(1, latent_width),
            like(heads, inputs, 128),
            like(heads, hidden),
            like(heads, hidden),
            like(heads, 128, hidden),
            like(heads, hidden),
            like(heads, hidden),
            like(heads, bins, 128),
            like(heads, bins),
        ),
        in_specs=[anywhere] * 6,
        out_specs=[vmem] * 24,
        scratch_shapes=[*(bf16(*shape) for shape in shapes), f32(4, 16, hidden), pltpu.SemaphoreType.DMA((6,))],
        compiler_params=pltpu.CompilerParams(vmem_limit_bytes=32 << 20),
    )(*outs[:6])
    observed_delta = outs[6].T.reshape(1, rows, observed)
    done = [item.reshape(-1) if item.shape[0] == 1 else item for item in done]
    done[22] = done[22].transpose(0, 2, 1)
    return (observed_delta, *done)


def solution(mesh):
    in_specs = (
        P(None, "dp", None),
        P(None, None, "dp", None),
        P(),
        P(None, "dp"),
        P(None, None, "dp", None),
        P(None, None, "dp"),
        P(None, None, "dp"),
    ) + (P(),) * 24
    out_specs = (
        P("section", "dp", None),
        P(),
        P(None, "dp"),
        P(),
        P(),
        P("dp", None),
        P(),
        P(),
        P(None, "dp"),
        P(),
        P(),
        P("dp", None),
        P(),
        P(),
        P("dp", None),
        P(),
        P(),
        P(None, None, "dp"),
        P(),
        P(),
        P(None, "dp", None),
        P(),
        P(),
        P(None, "dp", None),
        P(),
    )
    paired = (mesh.shape["section"], mesh.shape["dp"]) == (4, 8)
    return jax.shard_map(
        step_device if paired else plain_device,
        mesh=mesh,
        in_specs=in_specs,
        out_specs=out_specs,
        check_vma=False,
    )
```

```python
import functools

import jax
import jax.numpy as jnp
from jax import lax
from jax.experimental import pallas as pl
from jax.experimental.pallas import tpu as pltpu
from jax.sharding import PartitionSpec as P

SIMNORM = 8
epsilon = 1e-05
discount = 0.5
consistency_weight = 20.0
value_weight = 0.1

F32, BF16 = jnp.float32, jnp.bfloat16
WIDE_GROUP = 16
GROUP = 16
KERNEL_VMEM = 63 << 20
FINISH_VMEM = 63 << 20


def ceil_to(value, unit):
    return -(-value // unit) * unit


def row_sum(values):
    return jnp.sum(values, -1, keepdims=True)


def col_sum(values):
    return jnp.sum(values, 0, keepdims=True)


def dot(a, b):
    return lax.dot_general(a, b, (((1,), (0,)), ((), ())), preferred_element_type=F32)


def dot_left(a, b):
    return lax.dot_general(a, b, (((0,), (0,)), ((), ())), preferred_element_type=F32)


def dot_right(a, b):
    return lax.dot_general(a, b, (((1,), (1,)), ((), ())), preferred_element_type=F32)


def loop(count, body, unroll=1):
    def step(i, carry):
        body(i)
        return carry

    lax.fori_loop(0, count, step, 0, unroll=unroll)


def at(i, size):
    return pl.ds(pl.multiple_of(i * size, size), size)


def norm(values):
    scale = 1.0 / values.shape[1]
    center = values - row_sum(values) * scale
    rstd = lax.rsqrt(row_sum(center * center) * scale + epsilon)
    return center * rstd, rstd


def norm_back(grad, xhat, rstd):
    scale = 1.0 / grad.shape[1]
    mean_grad = row_sum(grad) * scale
    mean_both = row_sum(grad * xhat) * scale
    return rstd * (grad - mean_grad - xhat * mean_both)


def mish_forward(z, first, count, gain, shift, hidden, xhat_ref, slope, rstd_ref):
    for i in range(0, count, WIDE_GROUP):
        rows = pl.ds(first + i, WIDE_GROUP)
        xhat, rstd = norm(z[pl.ds(i, WIDE_GROUP), :])
        v = xhat * gain + shift
        e = jnp.exp(jnp.minimum(v, 30.0))
        n = e * (e + 2.0)
        r = pl.reciprocal(n + 2.0, approx=True)
        t = n * r
        xhat_ref[rows, :] = xhat.astype(xhat_ref.dtype)
        slope[rows, :] = (t + (4.0 * v) * ((e * r) * ((e + 1.0) * r))).astype(slope.dtype)
        rstd_ref[0][rows, rstd_ref[1] : rstd_ref[1] + 1] = rstd
        hidden[rows, :] = (v * t).astype(BF16)


def mish_backward(upstream, first, count, gain, xhat_ref, slope, rstd_ref, low, both_sums):
    width = upstream.shape[1]
    for i in range(0, count, GROUP):
        rows = pl.ds(first + i, GROUP)
        xhat = xhat_ref[rows, :].astype(F32)
        g = upstream[pl.ds(i, GROUP), :] * slope[rows, :]
        low[rows, :] = norm_back(g * gain, xhat, rstd_ref[0][rows, rstd_ref[1] : rstd_ref[1] + 1]).astype(BF16)
        both_sums[0] = both_sums[0] + (g * xhat).reshape(GROUP // 8, 8, width).sum(0)
        both_sums[1] = both_sums[1] + g.reshape(GROUP // 8, 8, width).sum(0)


def group_matrix(width):
    return (
        lax.broadcasted_iota(jnp.int32, (width, width), 0) // SIMNORM
        == lax.broadcasted_iota(jnp.int32, (width, width), 1) // SIMNORM
    ).astype(BF16)


def group_sums(values, groups):
    parts = []
    for k in range(values.shape[1] // 128):
        part = values[:, k * 128 : (k + 1) * 128]
        high = part.astype(BF16)
        rest = (part - high.astype(F32)).astype(BF16)
        parts.append(dot(high, groups) + dot(rest, groups))
    return jnp.concatenate(parts, 1)


def simnorm_forward(z, gain, shift, xhat_ref, chance, rstd_ref, groups):
    def body(i):
        xhat, rstd = norm(z[at(i, 32), :])
        e = jnp.exp(xhat * gain + shift)
        xhat_ref[at(i, 32), :] = xhat.astype(xhat_ref.dtype)
        chance[at(i, 32), :] = e / group_sums(e, groups)
        rstd_ref[0][at(i, 32), rstd_ref[1] : rstd_ref[1] + 1] = rstd

    loop(z.shape[0] // 32, body, 4)


def simnorm_backward(upstream, gain, xhat_ref, chance, rstd_ref, groups, low):
    width = gain.shape[1]

    def body(i, carry):
        gain_sum, shift_sum = carry
        xhat = xhat_ref[at(i, 32), :].astype(F32)
        p = chance[at(i, 32), :]
        w = upstream[at(i, 32), :] * p
        g = w - p * group_sums(w, groups)
        gx = g * xhat
        low[at(i, 32), :] = norm_back(g * gain, xhat, rstd_ref[0][at(i, 32), rstd_ref[1] : rstd_ref[1] + 1]).astype(BF16)
        return (
            gain_sum + gx.reshape(4, 8, width).sum(0),
            shift_sum + g.reshape(4, 8, width).sum(0),
        )

    zero = jnp.zeros((8, width), F32)
    gain_sum, shift_sum = lax.fori_loop(0, upstream.shape[0] // 32, body, (zero, zero), unroll=4)
    return col_sum(gain_sum), col_sum(shift_sum)


ORDERS = {
    "As": ("c", "y", "x", "z0", "z1"),
    "Bs": ("c", "x", "y", "z0", "z1"),
    "A0": ("c", "z0", "y", "z1"),
    "B0": ("c", "y", "z0", "z1"),
    "A1": ("c", "z0", "y", "z1"),
    "B1": ("c", "y", "z0", "z1"),
    "D2": ("c", "y", "z0", "z1", "x"),
    "F2": ("c", "z0", "x", "y", "z1"),
    "D1": ("c", "x", "z0", "z1", "y"),
    "G1": ("c", "y", "z0", "z1", "x"),
    "D3": ("c", "x", "y", "z0", "z1"),
    "E2": ("c", "y", "x", "z0", "z1"),
    "E1": ("c", "y", "x", "z0", "z1"),
}
SCHEDULE = {
    ("c", 0): [("L0", -1)],
    ("c", 1): [("L1", -1)],
    ("c", 2): [("L2", -1)],
    ("h", 0, 1): [("L0", 0), ("L1", 0)],
    ("h", 0, 3): [("L2", 0)],
    ("h", 0, 4): [("As", -1)],
    ("h", 0, 6): [("Bs", -1), ("As", 0)],
    ("h", 1, 2): [("Bs", 0)],
    ("h", 2, 2): [("As", 1), ("Bs", 1)],
    ("h", 2, 4): [("A0", -1)],
    ("h", 2, 6): [("Bs", 2), ("B0", -1), ("A0", 0)],
    ("h", 2, 7): [("As", 2)],
    ("h", 3, 2): [("B0", 0), ("Bs", 3)],
    ("h", 4, 2): [("A0", 1), ("B0", 1)],
    ("h", 4, 4): [("A1", -1), ("As", 3), ("Bs", 4)],
    ("h", 4, 6): [("B0", 2), ("B1", -1), ("Bs", 5), ("A1", 0), ("A0", 2), ("As", 4)],
    ("t", 0): [("R2", -1), ("R1", -1), ("R0", -1), ("T", -1)],
    ("b", 0, 1): [("B1", 0), ("Bs", 6)],
    ("b", 0, 2): [("T", 0), ("As", 5)],
    ("b", 0, 3): [("B0", 3), ("R2", 0)],
    ("b", 1, 1): [("As", 6)],
    ("b", 1, 3): [("R1", 0)],
    ("b", 2, 2): [("R0", 0)],
    ("t", 10): [("D2", -1), ("F2", -1), ("B1", 1), ("T", 1), ("A1", 1)],
    ("t", 11): [("B1", 2), ("D1", -1), ("G1", -1), ("B0", 4), ("A0", 3), ("D2", 0), ("F2", 0), ("T", 2)],
    ("t", 12): [("A1", 2), ("D3", -1), ("D1", 0), ("G1", 0), ("B0", 5)],
    ("t", 13): [("A0", 4), ("D3", 0), ("B1", 3)],
    ("t", 14): [("E2", -1)],
    ("t", 15): [("E1", -1)],
    ("t", 16): [("S", -1), ("D2", 1), ("A0", 5), ("D1", 1), ("F2", 1)],
    ("t", 17): [("E2", 0), ("E1", 0), ("S", 0), ("T", 3), ("G1", 1), ("A1", 3), ("D3", 1), ("D2", 2), ("B1", 4), ("E2", 1), ("D1", 2), ("B1", 5), ("F2", 2), ("T", 4), ("E1", 1), ("S", 1), ("G1", 2), ("D3", 2), ("A1", 4), ("D2", 3), ("F2", 3), ("D1", 3), ("S", 2), ("A1", 5), ("E2", 2), ("G1", 3), ("D3", 3), ("D1", 4), ("T", 5), ("F2", 4), ("S", 3), ("E1", 2), ("D2", 4), ("G1", 4), ("E2", 3), ("T", 6), ("D1", 5), ("D3", 4), ("F2", 5), ("E1", 3), ("S", 4), ("D2", 5), ("G1", 5), ("D1", 6), ("F2", 6), ("E2", 4), ("D3", 5), ("E1", 4), ("D2", 6), ("G1", 6), ("S", 5), ("D3", 6), ("E2", 5), ("E1", 5), ("S", 6), ("E2", 6), ("E1", 6)],
}


class Piece:
    def __init__(self, index, order, buffers, gathered, credit=None, gives=False):
        self.index, self.order, self.buffers, self.gathered = index, order, buffers, gathered
        self.credit, self.gives = credit, gives
        self.stages = len(order) + 2


class Exchange:
    def __init__(self, send_sem, recv_sem, free_sem):
        self.send_sem, self.recv_sem, self.free_sem = send_sem, recv_sem, free_sem
        section, dp = lax.axis_index("section"), lax.axis_index("dp")
        self.bit = {
            "c": section % 2,
            "x": section // 2,
            "y": dp % 2,
            "z0": (dp // 2) % 2,
            "z1": dp // 4,
        }
        self.partner = {
            "c": {"section": section + 1 - 2 * self.bit["c"]},
            "x": {"section": section + 2 - 4 * self.bit["x"]},
            "y": {"dp": dp + 1 - 2 * self.bit["y"]},
            "z0": {"dp": dp + 2 - 4 * self.bit["z0"]},
            "z1": {"dp": dp + 4 - 8 * self.bit["z1"]},
        }

    def greet(self):
        barrier = pltpu.get_barrier_semaphore()
        for axis in self.partner:
            self.signal(barrier, axis)
        pl.semaphore_wait(barrier, len(self.partner))

    def signal(self, sem, axis):
        pl.semaphore_signal(
            sem, inc=1, device_id=self.partner[axis], device_id_type=pl.DeviceIdType.MESH
        )

    def remote(self, source, target, index, stage, axis):
        return pltpu.make_async_remote_copy(
            src_ref=source,
            dst_ref=target,
            send_sem=self.send_sem.at[index, stage],
            recv_sem=self.recv_sem.at[index, stage],
            device_id=self.partner[axis],
            device_id_type=pl.DeviceIdType.MESH,
        )

    def place(self, order, rank, quarter):
        bits = {
            "c": quarter // 2,
            "x": quarter % 2,
            "y": rank % 2,
            "z0": (rank // 2) % 2,
            "z1": rank // 4,
        }
        index = 0
        for axis in order if len(order) == 5 else order + ("x",):
            index = index * 2 + bits[axis]
        return index

    def copy(self, piece, stage):
        c, x = self.bit["c"], self.bit["x"]
        count = len(piece.order)
        if stage < count:
            axis = piece.order[stage]
            half = 32 >> (stage + 1)
            source = piece.buffers[stage].at[pl.ds((1 - self.bit[axis]) * half, half)]
            target = piece.buffers[stage + 1]
        elif stage == count:
            axis = "x"
            source = target = piece.gathered.at[c, x]
        else:
            axis = "c"
            source = target = piece.gathered.at[c]
        return self.remote(source, target, piece.index, stage, axis)

    def begin(self, piece):
        if piece.credit is not None:
            pl.semaphore_wait(self.free_sem.at[piece.credit], 1)
        self.copy(piece, 0).start()

    def advance(self, piece, stage):
        last = stage + 1 == piece.stages
        self.copy(piece, stage).wait_recv()
        if stage == 0 or last:
            self.copy(piece, stage).wait_send()
        if stage > 1:
            self.copy(piece, stage - 1).wait_send()
        if stage == 2 and piece.gives is not False:
            self.signal(self.free_sem.at[piece.gives], "c")
        count = len(piece.order)
        if stage < count:
            half = 32 >> (stage + 1)
            first = self.bit[piece.order[stage]] * half
            kept, total = piece.buffers[stage], piece.buffers[stage + 1]
            if stage < count - 1:

                def add(i):
                    total[i] = total[i] + kept[first + i]

                loop(half, add, min(half, 4))
            else:
                for i in range(half):
                    piece.gathered[self.bit["c"], self.bit["x"], i] = total[i] + kept[first + i]
        if not last:
            self.copy(piece, stage + 1).start()


class Sums:
    def __init__(self, index, parts, gathered, exchange):
        self.index, self.parts, self.gathered, self.exchange = index, parts, gathered, exchange
        self.stages = 7

    def copy(self, stage):
        parts = self.parts
        c, x = self.exchange.bit["c"], self.exchange.bit["x"]
        if stage == 0:
            axis, source, target = "c", parts[0].at[pl.ds((1 - c) * 2, 2)], parts[1]
        elif stage == 1:
            axis, source, target = "x", parts[1].at[1 - x], parts[2]
        elif stage < 5:
            axis, source, target = ("y", "z0", "z1")[stage - 2], parts[stage], parts[stage + 1]
        elif stage == 5:
            axis = "x"
            source = target = self.gathered.at[c * 2 + x]
        else:
            axis = "c"
            source = target = self.gathered.at[pl.ds(c * 2, 2)]
        return self.exchange.remote(source, target, self.index, stage, axis)

    def begin(self):
        self.copy(0).start()

    def advance(self, stage):
        parts = self.parts
        c, x = self.exchange.bit["c"], self.exchange.bit["x"]
        self.copy(stage).wait()
        if stage == 0:
            parts[1][...] = parts[1][...] + parts[0][pl.ds(c * 2, 2)]
        elif stage == 1:
            parts[2][...] = parts[2][...] + parts[1][x]
        elif stage < 4:
            parts[stage + 1][...] = parts[stage + 1][...] + parts[stage][...]
        elif stage == 4:
            self.gathered[c * 2 + x] = parts[5][...] + parts[4][...]
        if stage + 1 < self.stages:
            self.copy(stage + 1).start()


def step_kernel(
    sizes,
    obs_ref,
    act_ref,
    ids_ref,
    low_ref,
    frac_ref,
    mask_ref,
    task_ref,
    enc_one_gain,
    enc_one_shift,
    enc_two_gain,
    enc_two_shift,
    dyn_one_gain,
    dyn_one_shift,
    dyn_two_gain,
    dyn_two_shift,
    dyn_three_gain,
    dyn_three_shift,
    value_one_gain,
    value_one_shift,
    value_two_gain,
    value_two_shift,
    value_bias,
    goals_ref,
    we1_ref,
    we2_ref,
    wd1_ref,
    wd2_ref,
    wd3_ref,
    wv1_ref,
    wv2_ref,
    wv3_ref,
    ga_ref,
    ga_pair_ref,
    gb_ref,
    gb_pair_ref,
    ge_ref,
    small_ref,
    heads_ref,
    obs_grad_ref,
    goals,
    we1_raw,
    we1,
    we2,
    wd1,
    wd1_rest,
    wd2,
    wd3,
    wv1,
    wv1_rest,
    wv2,
    wv3_raw,
    wv3,
    x_enc,
    x_all,
    x_now,
    turned,
    onehot,
    target,
    param_ref,
    z_chain,
    slope_chain,
    rstd_chain,
    hid_chain,
    z_lat,
    lat,
    rstd_lat,
    dz_lat,
    z1,
    s1,
    r_both,
    h1,
    z2,
    s2,
    h2,
    up_a,
    up_b,
    up,
    carry,
    both_sums,
    dz,
    dlog,
    dx,
    lat_in,
    dx_in,
    pa,
    pb,
    pe,
    half_a,
    half_b,
    half_e,
    last_a,
    last_b,
    last_e,
    all_a,
    all_a_pair,
    all_b,
    all_b_pair,
    all_e,
    small,
    small_parts,
    small_all,
    heads_small,
    heads_parts,
    heads_all,
    chain_sem,
    goal_sem,
    value_sem,
    out_sem,
    send_sem,
    recv_sem,
    free_sem,
):
    micro_total, observed, moves, task_width, bins, heads = sizes
    horizon, _, rows, latent_width = goals_ref.shape
    tasks = task_ref.shape[0]
    hidden = wv2_ref.shape[1]
    inputs = wv1_ref.shape[1]
    rest = inputs - latent_width
    total = horizon * rows
    ranks = hidden // 128
    part_rows, rest_rows = pb.shape[1], pa.shape[1]
    section = lax.axis_index("section")
    exchange = Exchange(send_sem, recv_sem, free_sem)
    x_bit = exchange.bit["x"]
    micros = (section, section + 2 - 4 * x_bit)
    own_heads = heads // 2
    shared = heads - 1

    pieces = {}

    def piece(name, own, half, last, gathered, credit=None, gives=False):
        order = ORDERS[name]
        buffers = [own, half] + last
        pieces[name] = Piece(len(pieces), order, buffers, gathered, credit, gives)

    def lasts(refs, k, lanes=None):
        views = [ref.at[k] for ref in refs]
        return views if lanes is None else [view.at[:, :, lanes] for view in views]

    left, right = pl.ds(0, latent_width), pl.ds(latent_width, latent_width)
    piece("As", pa, half_a.at[0], lasts(last_a, 0), all_a.at[0], None, 0)
    piece("A0", pa, half_a.at[1], lasts(last_a, 1), all_a_pair.at[0], None, 1)
    piece("A1", pa, half_a.at[0], lasts(last_a, 2), all_a_pair.at[1], 0, 0)
    for name, lanes, k, slot, final, credit in (
        ("D2", left, 3, 1, 1, 1),
        ("F2", right, 3, 1, 1, None),
        ("D3", left, 4, 0, 2, 0),
        ("E2", right, 4, 0, 2, None),
    ):
        piece(
            name,
            pa.at[:, :, lanes],
            half_a.at[slot, :, :, lanes],
            lasts(last_a, k, lanes),
            all_a.at[final, :, :, :, :, lanes],
            credit,
        )
    piece("Bs", pb, half_b, lasts(last_b, 0), all_b.at[0], None, 4)
    piece("B0", pb, half_b, lasts(last_b, 1), all_b_pair.at[0], 4, 4)
    piece("B1", pb, half_b, lasts(last_b, 2), all_b_pair.at[1], 4, 4)
    half_rows = part_rows // 2
    for name, first, credit in (("D1", 0, 4), ("G1", half_rows, None)):
        those = pl.ds(first, half_rows)
        piece(
            name,
            pb.at[:, those],
            half_b.at[:, those],
            [ref.at[3, :, those] for ref in last_b],
            all_b.at[1, :, :, :, those],
            credit,
        )
    piece("E1", pe, half_e, list(last_e), all_e)
    sums = {
        "S": Sums(len(pieces), [small, *small_parts], small_all, exchange),
        "T": Sums(len(pieces) + 1, [heads_small, *heads_parts], heads_all, exchange),
    }
    swaps = len(pieces) + 2

    def swap(name):
        t = int(name[1])
        if name[0] == "L":
            source, target_ref, stage = x_all.at[pl.ds(t * rows, rows), pl.ds(0, latent_width)], lat_in.at[t], t
        else:
            source, target_ref, stage = lat_in.at[t], dx_in.at[t], horizon + t
        return exchange.remote(source, target_ref, swaps, stage, "x")

    def act(name, stage):
        if name[0] in "LR":
            if stage < 0:
                swap(name).start()
            else:
                swap(name).wait()
        elif name in sums:
            if stage < 0:
                sums[name].begin()
            else:
                sums[name].advance(stage)
        elif stage < 0:
            exchange.begin(pieces[name])
        else:
            exchange.advance(pieces[name], stage)

    def tick(*key):
        for name, stage in SCHEDULE.get(key, ()):
            act(name, stage)

    def loop_tick(group, index, point=None):
        for key in SCHEDULE:
            if key[0] == group and key[2:] == (() if point is None else (point,)):
                pl.when(index == key[1])(functools.partial(tick, *key))

    def chain_copies():
        return [
            pltpu.make_async_copy(source, place, chain_sem.at[k])
            for k, (source, place) in enumerate(
                (
                    (we1_ref, we1_raw),
                    (we2_ref, we2),
                    (wd1_ref, wd1),
                    (wd2_ref, wd2),
                    (wd3_ref, wd3),
                )
            )
        ]

    def value_copy(q, index):
        source, place = ((wv1_ref, wv1), (wv2_ref, wv2), (wv3_ref, wv3_raw))[index]
        return pltpu.make_async_copy(source.at[q], place, value_sem.at[index])

    for copy in chain_copies():
        copy.start()
    for index in range(3):
        value_copy(shared, index).start()
    goal_copies = [
        pltpu.make_async_copy(goals_ref.at[t, section], goals.at[t], goal_sem.at[t]) for t in range(horizon)
    ]
    for copy in goal_copies:
        copy.start()

    small[...] = jnp.zeros_like(small)
    heads_small[...] = jnp.zeros_like(heads_small)
    dx[...] = jnp.zeros_like(dx)
    param_ref[...] = jnp.zeros_like(param_ref)
    we1[...] = jnp.zeros_like(we1)
    wd1_rest[...] = jnp.zeros_like(wd1_rest)
    wv1_rest[...] = jnp.zeros_like(wv1_rest)
    wv3[...] = jnp.zeros_like(wv3)
    turned[...] = jnp.zeros_like(turned)
    groups = group_matrix(128)

    def pick(ref, micro):
        out = jnp.zeros((1, rows), ref.dtype)
        for m in range(micro_total):
            out = out + jnp.where(micro == m, ref[m : m + 1, :], jnp.zeros((1, rows), ref.dtype))
        return out

    def line(ref):
        return ref[...].astype(F32).reshape(1, ref.shape[0])

    for index, vector in enumerate(
        (
            line(enc_one_gain),
            line(enc_one_shift),
            jnp.concatenate([line(enc_two_gain), line(enc_two_shift)], 1),
            line(dyn_one_gain),
            line(dyn_one_shift),
            line(dyn_two_gain),
            line(dyn_two_shift),
            jnp.concatenate([line(dyn_three_gain), line(dyn_three_shift)], 1),
        )
    ):
        param_ref[index : index + 1, :] = vector
    for index, ref in enumerate((value_one_gain, value_one_shift, value_two_gain, value_two_shift, value_bias)):
        for q in range(heads):
            at_row = 8 * (q + 1) + index
            param_ref[at_row : at_row + 1, : ref.shape[1]] = ref[q : q + 1, :].astype(F32)

    def pick_micro(values, micro):
        out = None
        for m in range(micro_total):
            part = jnp.where(micro == m, values[..., m, :], 0.0)
            out = part if out is None else out + part
        return out

    mask = mask_ref[...].astype(F32).astype(BF16)
    all_obs, all_act = obs_ref[...].astype(F32), act_ref[...].astype(F32)
    for j, micro in enumerate(micros):
        hot = (lax.broadcasted_iota(jnp.int32, (tasks, rows), 0) == pick(ids_ref, micro)).astype(BF16)
        onehot[j] = hot
        embedded = dot_left(task_ref[...], hot)
        allowed = dot(mask, hot)
        acts = pick_micro(all_act, micro)
        turned[moves:rest, :] = embedded
        for t in range(horizon):
            turned[0:moves, :] = acts[t] * allowed
            at_rows = slice((j * horizon + t) * rows, (j * horizon + t + 1) * rows)
            x_all[at_rows, latent_width:] = turned[:128, :].T.astype(BF16)
            bin_at = lax.broadcasted_iota(jnp.int32, (128, rows), 0)
            lower, upper_part = pick(low_ref.at[t], micro), pick(frac_ref.at[t], micro)
            target[at_rows, :] = (
                jnp.where(bin_at == lower, 1.0 - upper_part, 0.0) + jnp.where(bin_at == lower + 1, upper_part, 0.0)
            ).T
        if j == 0:
            turned[0:observed, :] = pick_micro(all_obs, micro)
            turned[observed : observed + task_width, :] = embedded
            x_enc[:, :128] = turned[:128, :].T.astype(BF16)
            x_enc[:, 128:] = turned[128:, :].T.astype(BF16)
            turned[...] = jnp.zeros_like(turned)

    def vec(index):
        return param_ref[index : index + 1, :]

    ups = (up_a, up_b)
    wide_up = up_a.at[pl.ds(0, rows), :]
    carry_up = up_a.at[pl.ds(0, rows), pl.ds(0, latent_width)]
    lat_up = up_b.at[pl.ds(0, rows), pl.ds(0, latent_width)]

    def in_blocks(count, product, after):
        size = up_a.shape[0] if count % up_a.shape[0] == 0 else rows
        blocks = [pl.ds(k * size, size) for k in range(count // size)]
        ups[0][:size, :] = product(blocks[0])
        for k, block in enumerate(blocks):
            if k + 1 < len(blocks):
                ups[(k + 1) % 2][:size, :] = product(blocks[k + 1])
            after(ups[k % 2], k * size, size)

    def forward_blocks(count, product, gain, shift, hidden_ref, xhat_ref, slope, rstd_ref):
        def after(z, first, size):
            mish_forward(z, first, size, gain, shift, hidden_ref, xhat_ref, slope, rstd_ref)

        in_blocks(count, product, after)

    def backward_blocks(count, product, gain, xhat_ref, slope, rstd_ref, low):
        both_sums[...] = jnp.zeros_like(both_sums)

        def after(upstream, first, size):
            mish_backward(upstream, first, size, gain, xhat_ref, slope, rstd_ref, low, both_sums)

        in_blocks(count, product, after)
        return col_sum(both_sums[0]), col_sum(both_sums[1])


    def mish_layer(product, index, slot):
        forward_blocks(
            rows,
            product,
            vec(index),
            vec(index + 1),
            hid_chain.at[at(slot, rows), :],
            z_chain.at[slot],
            slope_chain.at[slot],
            (rstd_chain.at[slot], 0),
        )

    def latent_layer(weight, hidden_slot, index, slot):
        carry_up[...] = dot(hid_chain[at(hidden_slot, rows), :], weight[...])
        simnorm_forward(
            carry_up,
            vec(index)[:, :latent_width],
            vec(index)[:, latent_width:],
            z_lat.at[slot],
            lat.at[slot],
            (rstd_lat.at[slot], 0),
            groups,
        )

    copies = chain_copies()
    copies[0].wait()
    we1[: observed + task_width, :] = we1_raw[...]
    mish_layer(lambda block: dot(x_enc[block, :], we1[...]), 0, 0)
    copies[1].wait()
    latent_layer(we2, 0, 2, 0)
    copies[2].wait()
    copies[3].wait()
    copies[4].wait()
    wd1_rest[:rest, :] = wd1[latent_width:, :]
    exchange.greet()
    def dynamics_step(t):
        own = at(t, rows)
        x_all[own, :latent_width] = lat[t].astype(BF16)
        loop_tick("c", t)
        mish_layer(
            lambda block: dot(x_all[own, :latent_width], wd1[:latent_width, :])
            + dot(x_all[own, latent_width:], wd1_rest[...]),
            3,
            1 + t,
        )
        mish_layer(lambda block: dot(hid_chain[at(1 + t, rows), :], wd2[...]), 5, 1 + horizon + t)
        latent_layer(wd3, 1 + horizon + t, 7, t + 1)

    loop(horizon, dynamics_step)

    def placed(name):
        return lambda rank, quarter: exchange.place(ORDERS[name], rank, quarter)

    def put_rows(place_of, own, rank, block, lanes=slice(None), more=None):
        low = block.astype(BF16)
        for k in range(low.shape[0] // rest_rows):
            place = place_of(rank + k // 4, k % 4)
            part = low[k * rest_rows : (k + 1) * rest_rows]
            own[place, :, lanes] = part if more is None else jnp.where(more, part + own[place, :, lanes], part)

    def put_lanes(places, own, rank, block, begin=0, more=None):
        low = block.astype(BF16)
        quarter_rows = own.shape[1]
        part_size = quarter_rows // len(places)
        for k in range(low.shape[1] // 128):
            done = 0
            while done < low.shape[0]:
                quarter, offset = divmod(begin + done, quarter_rows)
                which, inside = divmod(offset, part_size)
                count = min(part_size - inside, low.shape[0] - done)
                place = places[which](rank + k, quarter)
                part = low[done : done + count, k * 128 : (k + 1) * 128]
                own[place, offset : offset + count, :] = (
                    part if more is None else jnp.where(more, part + own[place, offset : offset + count, :], part)
                )
                done += count

    def head_pass(j):
        fifth = 1 - (j + 2 * own_heads) // (2 * own_heads + 1)
        q = fifth * shared + (1 - fifth) * (x_bit * own_heads + (j - 1) // 2)
        others = (1 - fifth) * (1 - j % 2)

        def mixed(first_name, other_name):
            def place_of(rank, quarter):
                first = exchange.place(ORDERS[first_name], rank, quarter)
                other = exchange.place(ORDERS[other_name], rank, quarter)
                return other + fifth * (first - other)

            return place_of

        more = others == 1
        block = param_ref[pl.ds(pl.multiple_of(8 * (q + 1), 8), 8), :]
        first_gain, first_shift, second_gain, second_shift, bias = (block[k : k + 1, :] for k in range(5))
        offset = others * total

        def arrived(index):
            pl.when(others == 0)(lambda: value_copy(q, index).wait())

        def prefetch(index):
            nxt = x_bit * own_heads + j // 2
            pl.when((j % 2 == 0) & (j < 2 * own_heads))(lambda: value_copy(nxt, index).start())

        @pl.when(j == 2)
        def _():
            for t in range(horizon):
                x_all[total + t * rows : total + (t + 1) * rows, :latent_width] = lat_in[t]

        x_now[...] = x_all[pl.ds(pl.multiple_of(offset, total), total), :]
        arrived(0)
        wv1_rest[:rest, :] = wv1[latent_width:, :]
        forward_blocks(
            total,
            lambda block: dot(x_now[block, :latent_width], wv1[:latent_width, :])
            + dot(x_now[block, latent_width:], wv1_rest[...]),
            first_gain,
            first_shift,
            h1,
            z1,
            s1,
            (r_both, 0),
        )
        loop_tick("h", j, 1)
        arrived(1)
        forward_blocks(total, lambda block: dot(h1[block, :], wv2[...]), second_gain, second_shift, h2, z2, s2, (r_both, 1))
        loop_tick("h", j, 2)
        arrived(2)
        wv3[:bins, :] = wv3_raw[...]
        prefetch(2)
        valid = lax.broadcasted_iota(jnp.int32, (1, 128), 1) < bins
        bias_sum = jnp.zeros((1, 128), F32)
        for t in range(horizon):
            factor = value_weight * discount**t / (heads * micro_total)
            own = slice(t * rows, (t + 1) * rows)
            logits = jnp.where(valid, dot_right(h2[own, :], wv3[...]) + bias[:, :128], -1e30)
            e = jnp.exp(logits - jnp.max(logits, -1, keepdims=True))
            goal = target[pl.ds(pl.multiple_of(offset + t * rows, rows), rows), :]
            delta = factor * (e / row_sum(e) - goal)
            dlog[own, :] = delta.astype(BF16)
            bias_sum = bias_sum + col_sum(delta)
        second_sums = backward_blocks(
            total, lambda block: dot(dlog[block, :], wv3[...]), second_gain, z2, s2, (r_both, 1), dz
        )
        loop_tick("h", j, 3)
        for part in range(2):
            columns = pl.ds(part * (hidden // 2), hidden // 2)
            product = dot_left(h1[:, columns], dz[...])
            put_rows(mixed("As", "A0"), pa, part * (ranks // 2), product, slice(None), more)
        loop_tick("h", j, 4)
        both_sums[...] = jnp.zeros_like(both_sums)
        up[...] = dot_right(dz[...], wv2[...])
        mish_backward(up, 0, total, first_gain, z1, s1, (r_both, 0), dz, both_sums)
        prefetch(1)
        loop_tick("h", j, 5)
        for part in range(2):
            columns = pl.ds(part * (hidden // 2), hidden // 2)
            put_lanes([mixed("Bs", "B0")], pb, part * (ranks // 2), dot_left(x_now[...], dz[:, columns]), 0, more)
        put_lanes([mixed("Bs", "B0")], pb, 0, dot_left(dlog[...], h2[...]), latent_width + 128, more)
        loop_tick("h", j, 6)
        here = pl.ds(pl.multiple_of(offset, total), total)
        dx[here, :latent_width] = dx[here, :latent_width] + dot_right(dz[...], wv1[:latent_width, :])
        dx[here, latent_width:] = dx[here, latent_width:] + dot_right(dz[...], wv1_rest[...])
        prefetch(0)
        pad = jnp.zeros((1, hidden - 128), F32)
        place = pl.ds(pl.multiple_of(q % 2 * 8, 8), 8)
        heads_small[q // 2, place, :] = heads_small[q // 2, place, :] + jnp.concatenate(
            [
                col_sum(both_sums[0]),
                col_sum(both_sums[1]),
                *second_sums,
                jnp.concatenate([bias_sum, pad], 1),
                jnp.zeros((3, hidden), F32),
            ],
            0,
        )
        loop_tick("h", j, 7)

    loop(1 + 2 * own_heads, head_pass)

    for t in range(horizon):
        lat_in[t] = dx[total + t * rows : total + (t + 1) * rows, :latent_width].astype(BF16)
    tick("t", 0)
    for copy in goal_copies:
        copy.wait()
    embed_sums = []
    for j in range(2):
        parts = [dx[(j * horizon + t) * rows : (j * horizon + t + 1) * rows, latent_width:] for t in range(horizon)]
        embed_sums.append(sum(parts[1:], parts[0]))
    dz_one, dz_two = h1, dz
    gain_lat = vec(7)[:, :latent_width]
    carry[...] = jnp.zeros_like(carry)

    def step_backward(i, sums):
        t = horizon - 1 - i
        factor = 0.0
        for k in range(horizon):
            factor = jnp.where(t == k, 2.0 * consistency_weight * discount**k / (micro_total * latent_width), factor)
        lat_up[...] = factor * (lat[t + 1] - goals[t].astype(F32)) + carry[...]
        own = at(t, rows)
        one, two = 1 + t, 1 + horizon + t
        lat_sums = simnorm_backward(
            lat_up, gain_lat, z_lat.at[t + 1], lat.at[t + 1], (rstd_lat.at[t + 1], 0), groups, dz_lat.at[own, :]
        )
        two_sums = backward_blocks(
            rows,
            lambda block: dot_right(dz_lat[own, :], wd3[...]),
            vec(5),
            z_chain.at[two],
            slope_chain.at[two],
            (rstd_chain.at[two], 0),
            dz_two.at[own, :],
        )
        loop_tick("b", i, 1)
        one_sums = backward_blocks(
            rows,
            lambda block: dot_right(dz_two[own, :], wd2[...]),
            vec(3),
            z_chain.at[one],
            slope_chain.at[one],
            (rstd_chain.at[one], 0),
            dz_one.at[own, :],
        )
        loop_tick("b", i, 2)
        latent_delta = dot_right(dz_one[own, :], wd1[:latent_width, :])
        rest_delta = dot_right(dz_one[own, :], wd1_rest[...])
        loop_tick("b", i, 3)
        carry[...] = latent_delta.astype(BF16).astype(F32) + dx[own, :latent_width] + dx_in[t].astype(F32)
        return tuple(a + b for a, b in zip(sums, (rest_delta, *one_sums, *two_sums, *lat_sums)))

    zero, zero_lat = jnp.zeros((1, hidden), F32), jnp.zeros((1, latent_width), F32)
    totals = lax.fori_loop(
        0, horizon, step_backward, (embed_sums[0], zero, zero, zero, zero, zero_lat, zero_lat)
    )
    embed_sums[0] = totals[0]
    small[0, 3:8, :] = jnp.concatenate([*totals[1:5], jnp.concatenate(totals[5:], 1)], 0)

    def put_chain(name, grad, first, lanes=slice(None), second_name=None):
        for part in range(2):
            columns = pl.ds(part * (hidden // 2), hidden // 2)
            block = dot_left(hid_chain[first * rows : (first + horizon) * rows, columns], grad[...])
            if second_name is None:
                put_rows(placed(name), pa, part * (ranks // 2), block, lanes)
            else:
                put_rows(placed(name), pa, part * (ranks // 2), block[:, :latent_width], slice(0, latent_width))
                put_rows(
                    placed(second_name),
                    pa,
                    part * (ranks // 2),
                    block[:, latent_width:],
                    slice(latent_width, 2 * latent_width),
                )

    put_chain("D2", dz_two, 1, second_name="F2")
    tick("t", 10)
    for part in range(2):
        columns = pl.ds(part * (hidden // 2), hidden // 2)
        put_lanes([placed("D1"), placed("G1")], pb, part * (ranks // 2), dot_left(x_all[:total, :], dz_one[:, columns]))
    tick("t", 11)
    put_chain("D3", dz_lat, 1 + horizon, slice(0, latent_width))
    tick("t", 12)

    lat_up[...] = carry[...]
    low_lat = dz_lat.at[pl.ds(0, rows), :]
    encoder_lat = simnorm_backward(
        lat_up, vec(2)[:, :latent_width], z_lat.at[0], lat.at[0], (rstd_lat.at[0], 0), groups, low_lat
    )
    low_one = dz_one.at[pl.ds(0, rows), :]
    encoder_one = backward_blocks(
        rows,
        lambda block: dot_right(low_lat[...], we2[...]),
        vec(0),
        z_chain.at[0],
        slope_chain.at[0],
        (rstd_chain.at[0], 0),
        low_one,
    )
    small[0, 0:3, :] = jnp.concatenate([*encoder_one, jnp.concatenate(encoder_lat, 1)], 0)
    tick("t", 13)
    put_rows(
        placed("E2"), pa, 0, dot_left(hid_chain[:rows, :], low_lat[...]), slice(latent_width, 2 * latent_width)
    )
    tick("t", 14)
    put_lanes([placed("E1")], pe, 0, dot_left(x_enc[...], low_one[...])[: 4 * pe.shape[1]])
    tick("t", 15)
    enc_up = dot_right(low_one[...], we1[...])
    obs_grad_ref[...] = enc_up[:, :128].T[:observed, :]
    embed_sums[0] = embed_sums[0] + pltpu.roll(enc_up, x_enc.shape[1] - observed + moves, 1)[:, :128]
    table = None
    for j in range(2):
        high = embed_sums[j].astype(BF16)
        low = (embed_sums[j] - high.astype(F32)).astype(BF16)
        part = dot(onehot[j], high) + dot(onehot[j], low)
        table = part if table is None else table + part
    for k in range(tasks // 8):
        small[1 + k // 8, :, (k % 8) * 128 : (k % 8) * 128 + 128] = table[k * 8 : k * 8 + 8]
    tick("t", 16)
    tick("t", 17)
    outs = [
        pltpu.make_async_copy(source, place, out_sem.at[k])
        for k, (source, place) in enumerate(
            (
                (all_a, ga_ref),
                (all_a_pair, ga_pair_ref),
                (all_b, gb_ref),
                (all_b_pair, gb_pair_ref),
                (all_e, ge_ref),
            )
        )
    ]
    for copy in outs:
        copy.start()
    small_ref[...] = small_all[...]
    heads_ref[...] = heads_all[...]
    for copy in outs:
        copy.wait()


def finish_kernel(
    sizes,
    ga_from,
    ga_pair_from,
    gb_from,
    gb_pair_from,
    ge_from,
    small_from,
    heads_from,
    obs_from,
    obs_out,
    table_ref,
    encoder_first,
    encoder_first_gain,
    encoder_first_shift,
    encoder_second,
    encoder_second_gain,
    encoder_second_shift,
    dynamics_first,
    dynamics_first_gain,
    dynamics_first_shift,
    dynamics_second,
    dynamics_second_gain,
    dynamics_second_shift,
    dynamics_third,
    dynamics_third_gain,
    dynamics_third_shift,
    value_first,
    value_first_gain,
    value_first_shift,
    value_second,
    value_second_gain,
    value_second_shift,
    value_third,
    value_bias,
    ga_ref,
    ga_pair_ref,
    gb_ref,
    gb_pair_ref,
    ge_ref,
    small_ref,
    heads_ref,
    obs_ref,
    sem,
):
    copies = [
        pltpu.make_async_copy(source, place, sem.at[k])
        for k, (source, place) in enumerate(
            (
                (ga_from, ga_ref),
                (ga_pair_from, ga_pair_ref),
                (gb_from, gb_ref),
                (gb_pair_from, gb_pair_ref),
                (ge_from, ge_ref),
                (small_from, small_ref),
                (heads_from, heads_ref),
                (obs_from, obs_ref),
            )
        )
    ]
    for copy in copies:
        copy.start()
    for copy in copies:
        copy.wait()
    _, _, moves, task_width, bins, heads = sizes
    rest_rows, part_rows = ga_ref.shape[4], gb_ref.shape[4]
    obs_out[:, 0, :] = obs_ref[...]
    inputs = dynamics_first.shape[0]
    latent_width = dynamics_third.shape[1]
    encoder_rows = encoder_first.shape[0]
    third_at = 4 * part_rows - 128
    own_heads = heads // 2

    def move(target, first_row, block):
        count = min(target.shape[0] - first_row, block.shape[0])
        if count > 0:
            target[first_row : first_row + count, :] = block[:count].astype(F32)

    for c in range(2):
        for x in range(2):
            quarter = c * 2 + x
            move(value_second.at[heads - 1], quarter * rest_rows, ga_ref[0, c, x, 0])
            move(dynamics_second, quarter * rest_rows, ga_ref[1, c, x, 0])
            move(dynamics_third, quarter * rest_rows, ga_ref[2, c, x, 0, :, :latent_width])
            move(encoder_second, quarter * rest_rows, ga_ref[2, c, x, 0, :, latent_width:])
            move(encoder_first, quarter * ge_ref.shape[3], ge_ref[c, x, 0])
            move(dynamics_first, quarter * part_rows, gb_ref[1, c, x, 0])
            for k in range(own_heads):
                for i in range(2):
                    move(value_second.at[x * own_heads + k], (c * 2 + i) * rest_rows, ga_pair_ref[k, c, x, i])

    def lanes(head, quarter, block):
        first = quarter * part_rows
        move(value_first.at[head], first, block)
        if first + part_rows > third_at:
            move(value_third.at[head], 0, block[third_at - first :])

    for quarter in range(4):
        lanes(heads - 1, quarter, gb_ref[0, quarter // 2, quarter % 2, 0])
        for x in range(2):
            for k in range(own_heads):
                lanes(x * own_heads + k, quarter, gb_pair_ref[k, quarter // 2, x, quarter % 2])

    def row(index):
        return small_ref[0, index : index + 1, :]

    def head_row(q, k):
        return heads_ref[q // 2, q % 2 * 8 + k : q % 2 * 8 + k + 1, :]

    encoder_first_gain[...] = row(0)
    encoder_first_shift[...] = row(1)
    encoder_second_gain[...] = row(2)[:, :latent_width]
    encoder_second_shift[...] = row(2)[:, latent_width:]
    dynamics_first_gain[...] = row(3)
    dynamics_first_shift[...] = row(4)
    dynamics_second_gain[...] = row(5)
    dynamics_second_shift[...] = row(6)
    dynamics_third_gain[...] = row(7)[:, :latent_width]
    dynamics_third_shift[...] = row(7)[:, latent_width:]
    for q in range(heads):
        for k, target in enumerate((value_first_gain, value_first_shift, value_second_gain, value_second_shift)):
            target[q : q + 1, :] = head_row(q, k)
        value_bias[q : q + 1, :] = head_row(q, 4)[:, :bins]
    for k in range(table_ref.shape[0] // 8):
        block = small_ref[1 + k // 8, :, (k % 8) * 128 : (k % 8) * 128 + 128]
        table_ref[k * 8 : k * 8 + 8, :] = block[:, moves : moves + task_width]


def mish_curve(values):
    return values * jnp.tanh(jax.nn.softplus(values))


def layer_norm(before, gain_vec, shift_vec):
    center = before - jnp.mean(before, -1, keepdims=True)
    spread = jnp.mean(center * center, -1, keepdims=True)
    return center * lax.rsqrt(spread + epsilon) * gain_vec + shift_vec


def sim_norm(values):
    groups = values.reshape(values.shape[:-1] + (values.shape[-1] // SIMNORM, SIMNORM))
    return jax.nn.softmax(groups, -1).reshape(values.shape)


def post_mish(before, gain_vec, shift_vec):
    return mish_curve(layer_norm(before, gain_vec, shift_vec))


def post_simnorm(before, gain_vec, shift_vec):
    return sim_norm(layer_norm(before, gain_vec, shift_vec))


def head_mish(before, gain_vec, shift_vec):
    return post_mish(before, gain_vec[:, None, :], shift_vec[:, None, :])


def matmul(left_side, right_side):
    return jnp.dot(left_side, right_side, preferred_element_type=jnp.float32)


def left_transposed(left_side, right_side):
    return lax.dot_general(
        left_side, right_side, (((0,), (0,)), ((), ())), preferred_element_type=jnp.float32
    )


def right_transposed(left_side, right_side):
    return lax.dot_general(
        left_side, right_side, (((1,), (1,)), ((), ())), preferred_element_type=jnp.float32
    )


def dense_forward(inputs, weight, gain_vec, shift_vec, after_fn):
    before = matmul(inputs, weight)
    return jax.vjp(after_fn, before, gain_vec.astype(jnp.float32), shift_vec.astype(jnp.float32))


def dense_backward(inputs, weight, puller, upstream):
    delta_before, delta_gain, delta_shift = puller(upstream)
    rounded = delta_before.astype(jnp.bfloat16)
    return (
        right_transposed(rounded, weight),
        left_transposed(inputs, rounded),
        delta_gain,
        delta_shift,
    )


def encoder_forward(encoder_params, observed, embedded):
    inputs = jnp.concatenate([observed, embedded], 1)
    hidden, first_pull = dense_forward(
        inputs, encoder_params[0], encoder_params[1], encoder_params[2], post_mish
    )
    hidden_low = hidden.astype(jnp.bfloat16)
    latent, second_pull = dense_forward(
        hidden_low, encoder_params[3], encoder_params[4], encoder_params[5], post_simnorm
    )
    return (latent, (inputs, hidden_low, first_pull, second_pull))


def encoder_backward(encoder_params, retained, upstream):
    inputs, hidden_low, first_pull, second_pull = retained
    delta_hidden, delta_second, second_gain, second_shift = dense_backward(
        hidden_low, encoder_params[3], second_pull, upstream
    )
    delta_inputs, delta_first, first_gain, first_shift = dense_backward(
        inputs, encoder_params[0], first_pull, delta_hidden
    )
    return (
        delta_inputs,
        (delta_first, first_gain, first_shift, delta_second, second_gain, second_shift),
    )


def dynamics_forward(dynamics_params, latent_in, action_low, embedded):
    inputs = jnp.concatenate([latent_in, action_low, embedded], 1)
    layer_one, first_pull = dense_forward(
        inputs, dynamics_params[0], dynamics_params[1], dynamics_params[2], post_mish
    )
    one_low = layer_one.astype(jnp.bfloat16)
    layer_two, second_pull = dense_forward(
        one_low, dynamics_params[3], dynamics_params[4], dynamics_params[5], post_mish
    )
    two_low = layer_two.astype(jnp.bfloat16)
    latent, third_pull = dense_forward(
        two_low, dynamics_params[6], dynamics_params[7], dynamics_params[8], post_simnorm
    )
    return (latent, (inputs, one_low, two_low, first_pull, second_pull, third_pull))


def dynamics_backward(dynamics_params, retained, upstream):
    inputs, one_low, two_low, first_pull, second_pull, third_pull = retained
    delta_two, delta_third, third_gain, third_shift = dense_backward(
        two_low, dynamics_params[6], third_pull, upstream
    )
    delta_one, delta_second, second_gain, second_shift = dense_backward(
        one_low, dynamics_params[3], second_pull, delta_two
    )
    delta_inputs, delta_first, first_gain, first_shift = dense_backward(
        inputs, dynamics_params[0], first_pull, delta_one
    )
    return (
        delta_inputs,
        (
            delta_first,
            first_gain,
            first_shift,
            delta_second,
            second_gain,
            second_shift,
            delta_third,
            third_gain,
            third_shift,
        ),
    )


def value_backward(value_params, inputs, bin_rows, fraction_rows, factor):
    first_before = jnp.einsum(
        "rk,qkn->qrn", inputs, value_params[0], preferred_element_type=jnp.float32
    )
    layer_one, first_pull = jax.vjp(
        head_mish,
        first_before,
        value_params[1].astype(jnp.float32),
        value_params[2].astype(jnp.float32),
    )
    one_low = layer_one.astype(jnp.bfloat16)
    second_before = jnp.einsum(
        "qrk,qkn->qrn", one_low, value_params[3], preferred_element_type=jnp.float32
    )
    layer_two, second_pull = jax.vjp(
        head_mish,
        second_before,
        value_params[4].astype(jnp.float32),
        value_params[5].astype(jnp.float32),
    )
    two_low = layer_two.astype(jnp.bfloat16)
    logits = (
        jnp.einsum("qrk,qkn->qrn", two_low, value_params[6], preferred_element_type=jnp.float32)
        + value_params[7].astype(jnp.float32)[:, None, :]
    )
    chances = jax.nn.softmax(logits, -1)
    columns = lax.broadcasted_iota(jnp.int32, (1, logits.shape[2]), 1)
    lower_bin = bin_rows[:, None]
    target = (1.0 - fraction_rows)[:, None] * (columns == lower_bin).astype(
        jnp.float32
    ) + fraction_rows[:, None] * (columns == lower_bin + 1).astype(jnp.float32)
    delta_logits = factor[None, :, None] * (chances - target[None])
    logit_low = delta_logits.astype(jnp.bfloat16)
    delta_bias = jnp.sum(delta_logits, 1)
    delta_third = jnp.einsum("qrk,qrn->qkn", two_low, logit_low, preferred_element_type=jnp.float32)
    delta_two = jnp.einsum(
        "qrn,qkn->qrk", logit_low, value_params[6], preferred_element_type=jnp.float32
    )
    before_two, second_gain, second_shift = second_pull(delta_two)
    two_round = before_two.astype(jnp.bfloat16)
    delta_second = jnp.einsum(
        "qrk,qrn->qkn", one_low, two_round, preferred_element_type=jnp.float32
    )
    delta_one = jnp.einsum(
        "qrn,qkn->qrk", two_round, value_params[3], preferred_element_type=jnp.float32
    )
    before_one, first_gain, first_shift = first_pull(delta_one)
    one_round = before_one.astype(jnp.bfloat16)
    delta_first = jnp.einsum("rk,qrn->qkn", inputs, one_round, preferred_element_type=jnp.float32)
    delta_inputs = jnp.einsum(
        "qrn,qkn->rk", one_round, value_params[0], preferred_element_type=jnp.float32
    )
    return (
        delta_inputs,
        (
            delta_first,
            first_gain,
            first_shift,
            delta_second,
            second_gain,
            second_shift,
            delta_third,
            delta_bias,
        ),
    )


def reduce_end(gradients):
    def reduced(index, axis):
        shard = lax.psum_scatter(
            gradients[index].astype(jnp.bfloat16), "dp", scatter_dimension=axis, tiled=True
        )
        return lax.psum(shard, "section").astype(jnp.float32)

    return tuple(
        reduced(index, axis)
        for index, axis in ((0, 1), (3, 0), (6, 1), (9, 0), (12, 0), (15, 2), (18, 1), (21, 1))
    )


def plain_device(
    observations,
    actions,
    action_mask,
    task_ids,
    targets,
    bin_low,
    bin_frac,
    task_table,
    encoder_first,
    encoder_first_gain,
    encoder_first_shift,
    encoder_second,
    encoder_second_gain,
    encoder_second_shift,
    dynamics_first,
    dynamics_first_gain,
    dynamics_first_shift,
    dynamics_second,
    dynamics_second_gain,
    dynamics_second_shift,
    dynamics_third,
    dynamics_third_gain,
    dynamics_third_shift,
    value_first,
    value_first_gain,
    value_first_shift,
    value_second,
    value_second_gain,
    value_second_shift,
    value_third,
    value_bias,
):
    encoder_params = (
        encoder_first,
        encoder_first_gain,
        encoder_first_shift,
        encoder_second,
        encoder_second_gain,
        encoder_second_shift,
    )
    dynamics_params = (
        dynamics_first,
        dynamics_first_gain,
        dynamics_first_shift,
        dynamics_second,
        dynamics_second_gain,
        dynamics_second_shift,
        dynamics_third,
        dynamics_third_gain,
        dynamics_third_shift,
    )
    value_params = (
        value_first,
        value_first_gain,
        value_first_shift,
        value_second,
        value_second_gain,
        value_second_shift,
        value_third,
        value_bias,
    )
    sections = lax.axis_size("section")
    level_now = lax.axis_index("section")
    micro_total = observations.shape[0]
    share = micro_total // sections
    latent_width = dynamics_third.shape[1]
    action_width = actions.shape[3]
    observed_width = observations.shape[2]
    horizon = actions.shape[0]
    heads = value_first.shape[0]
    task_count = task_table.shape[0]

    def mine(array, axis):
        part = lax.dynamic_slice_in_dim(array, level_now * share, share, axis)
        shape = part.shape
        return part.reshape(shape[:axis] + (shape[axis] * shape[axis + 1],) + shape[axis + 2 :])

    observed = mine(observations, 0)
    movement = mine(actions, 1)
    task_rows = mine(task_ids, 0)
    goals = mine(targets, 1)
    low_bins = mine(bin_low, 1)
    fractions = mine(bin_frac, 1)
    rows = observed.shape[0]
    onehot = (task_rows[:, None] == lax.broadcasted_iota(jnp.int32, (1, task_count), 1)).astype(
        jnp.bfloat16
    )
    embedded = matmul(onehot, task_table).astype(jnp.bfloat16)
    allowed = matmul(onehot, action_mask.astype(jnp.bfloat16))
    chosen = (movement.astype(jnp.float32) * allowed[None]).astype(jnp.bfloat16)

    latent, encoder_kept = encoder_forward(encoder_params, observed, embedded)
    latents = [latent]
    dynamics_kept = []
    for step in range(horizon):
        latent, kept = dynamics_forward(
            dynamics_params, latents[step].astype(jnp.bfloat16), chosen[step], embedded
        )
        latents.append(latent)
        dynamics_kept.append(kept)
    inputs = jnp.concatenate([kept[0] for kept in dynamics_kept], 0)
    step_weight = jnp.asarray(
        [value_weight * discount**step / (heads * micro_total) for step in range(horizon)],
        jnp.float32,
    )
    value_delta, value_grads = value_backward(
        value_params,
        inputs,
        low_bins.reshape(-1),
        fractions.reshape(-1),
        jnp.repeat(step_weight, rows),
    )
    value_delta = value_delta.reshape(horizon, rows, -1)
    upstream = jnp.zeros((rows, latent_width), jnp.float32)
    embed_delta = jnp.sum(value_delta[:, :, latent_width + action_width :], 0)
    dynamics_grads = None
    for step in reversed(range(horizon)):
        factor = 2.0 * consistency_weight * discount**step / (micro_total * latent_width)
        upstream = upstream + factor * (latents[step + 1] - goals[step].astype(jnp.float32))
        inputs_delta, step_grads = dynamics_backward(dynamics_params, dynamics_kept[step], upstream)
        dynamics_grads = (
            step_grads
            if dynamics_grads is None
            else tuple(a + b for a, b in zip(dynamics_grads, step_grads))
        )
        embed_delta = embed_delta + inputs_delta[:, latent_width + action_width :]
        upstream = (
            inputs_delta[:, :latent_width].astype(jnp.bfloat16).astype(jnp.float32)
            + value_delta[step, :, :latent_width]
        )
    inputs_delta, encoder_grads = encoder_backward(encoder_params, encoder_kept, upstream)
    observed_delta = inputs_delta[:, :observed_width]
    embed_delta = embed_delta + inputs_delta[:, observed_width:]
    table_sum = left_transposed(onehot.astype(jnp.float32), embed_delta)
    totals = encoder_grads + dynamics_grads + value_grads
    matrices = reduce_end(totals)
    small_sums = lax.psum(
        tuple(totals[i] for i in (1, 2, 4, 5, 7, 8, 10, 11, 13, 14, 16, 17, 19, 20, 22))
        + (table_sum,),
        ("section", "dp"),
    )
    return (
        observed_delta.reshape(share, rows // share, observed_width),
        small_sums[15],
        matrices[0],
        small_sums[0],
        small_sums[1],
        matrices[1],
        small_sums[2],
        small_sums[3],
        matrices[2],
        small_sums[4],
        small_sums[5],
        matrices[3],
        small_sums[6],
        small_sums[7],
        matrices[4],
        small_sums[8],
        small_sums[9],
        matrices[5],
        small_sums[10],
        small_sums[11],
        matrices[6],
        small_sums[12],
        small_sums[13],
        matrices[7],
        small_sums[14],
    )


def step_device(
    observations,
    actions,
    action_mask,
    task_ids,
    targets,
    bin_low,
    bin_frac,
    task_table,
    encoder_first,
    encoder_first_gain,
    encoder_first_shift,
    encoder_second,
    encoder_second_gain,
    encoder_second_shift,
    dynamics_first,
    dynamics_first_gain,
    dynamics_first_shift,
    dynamics_second,
    dynamics_second_gain,
    dynamics_second_shift,
    dynamics_third,
    dynamics_third_gain,
    dynamics_third_shift,
    value_first,
    value_first_gain,
    value_first_shift,
    value_second,
    value_second_gain,
    value_second_shift,
    value_third,
    value_bias,
):
    horizon, micro_total, rows, moves = actions.shape
    tasks, task_width = task_table.shape
    heads, inputs, hidden = value_first.shape
    latent_width = dynamics_third.shape[1]
    observed = observations.shape[2]
    bins = value_third.shape[2]
    enc_rows = ceil_to(observed + task_width, 256)
    in_rows = latent_width + 128
    total = horizon * rows
    ranks = hidden // 128
    sizes = (micro_total, observed, moves, task_width, bins, heads)
    part_rows = (in_rows + 128) // 4
    rest_rows = hidden // (ranks * 4)
    enc_part = ceil_to(observed + task_width, 64) // 4
    chain = 1 + 2 * horizon
    pair = heads // 2
    vmem, anywhere = pl.BlockSpec(memory_space=pltpu.VMEM), pl.BlockSpec(memory_space=pl.ANY)
    names = len(ORDERS) + 3

    def gathered(count, blocks, block_rows, width):
        return (count, 2, 2, blocks, block_rows, width)

    shapes = (
        gathered(3, 1, rest_rows, hidden),
        gathered(pair, 2, rest_rows, hidden),
        gathered(2, 1, part_rows, 128),
        gathered(pair, 2, part_rows, 128),
        gathered(1, 1, enc_part, 128)[1:],
    )
    f32, bf16 = (lambda *shape: pltpu.VMEM(shape, F32)), (lambda *shape: pltpu.VMEM(shape, BF16))
    outs = pl.pallas_call(
        functools.partial(step_kernel, sizes),
        out_shape=tuple(jax.ShapeDtypeStruct(shape, BF16) for shape in shapes)
        + (
            jax.ShapeDtypeStruct((4, 8, hidden), F32),
            jax.ShapeDtypeStruct((4, 16, hidden), F32),
            jax.ShapeDtypeStruct((observed, rows), F32),
        ),
        in_specs=[vmem] * 22 + [anywhere] * 9,
        out_specs=[anywhere] * 5 + [vmem] * 3,
        scratch_shapes=[
            bf16(horizon, rows, latent_width),
            bf16(observed + task_width, hidden),
            bf16(enc_rows, hidden),
            bf16(hidden, latent_width),
            bf16(inputs, hidden),
            bf16(128, hidden),
            bf16(hidden, hidden),
            bf16(hidden, latent_width),
            bf16(inputs, hidden),
            bf16(128, hidden),
            bf16(hidden, hidden),
            bf16(bins, hidden),
            bf16(128, hidden),
            bf16(rows, enc_rows),
            bf16(2 * total, in_rows),
            bf16(total, in_rows),
            f32(enc_rows, rows),
            bf16(2, tasks, rows),
            f32(2 * total, 128),
            f32(8 * (heads + 1), hidden),
            bf16(chain, rows, hidden),
            bf16(chain, rows, hidden),
            f32(chain, rows, 128),
            bf16(chain * rows, hidden),
            bf16(horizon + 1, rows, latent_width),
            f32(horizon + 1, rows, latent_width),
            f32(horizon + 1, rows, 128),
            bf16(total, latent_width),
        ]
        + [bf16(total, hidden), bf16(total, hidden), f32(total, 128)]
        + [bf16(total, hidden)] * 4
        + [
            f32(rows, hidden),
            f32(rows, hidden),
            f32(total, hidden),
            f32(rows, latent_width),
            f32(2, 8, hidden),
            bf16(total, hidden),
            bf16(total, 128),
            f32(2 * total, in_rows),
            bf16(horizon, rows, latent_width),
            bf16(horizon, rows, latent_width),
            bf16(32, rest_rows, hidden),
            bf16(32, part_rows, 128),
            bf16(32, enc_part, 128),
            bf16(2, 16, rest_rows, hidden),
            bf16(16, part_rows, 128),
            bf16(16, enc_part, 128),
            [bf16(5, 8 >> k, rest_rows, hidden) for k in range(4)],
            [bf16(4, 8 >> k, part_rows, 128) for k in range(4)],
            [bf16(8 >> k, enc_part, 128) for k in range(4)],
            *(bf16(*shape) for shape in shapes),
            f32(4, 8, hidden),
            [f32(2, 8, hidden)] + [f32(8, hidden)] * 4,
            f32(4, 8, hidden),
            f32(4, 16, hidden),
            [f32(2, 16, hidden)] + [f32(16, hidden)] * 4,
            f32(4, 16, hidden),
            pltpu.SemaphoreType.DMA((5,)),
            pltpu.SemaphoreType.DMA((horizon,)),
            pltpu.SemaphoreType.DMA((3,)),
            pltpu.SemaphoreType.DMA((5,)),
            pltpu.SemaphoreType.DMA((names, 7)),
            pltpu.SemaphoreType.DMA((names, 7)),
            pltpu.SemaphoreType.REGULAR((5,)),
        ],
        compiler_params=pltpu.CompilerParams(
            collective_id=0, has_side_effects=True, vmem_limit_bytes=KERNEL_VMEM
        ),
    )(
        observations.transpose(2, 0, 1),
        actions.transpose(0, 3, 1, 2),
        task_ids,
        bin_low,
        bin_frac,
        action_mask.T,
        task_table,
        encoder_first_gain,
        encoder_first_shift,
        encoder_second_gain,
        encoder_second_shift,
        dynamics_first_gain,
        dynamics_first_shift,
        dynamics_second_gain,
        dynamics_second_shift,
        dynamics_third_gain,
        dynamics_third_shift,
        value_first_gain,
        value_first_shift,
        value_second_gain,
        value_second_shift,
        value_bias,
        targets,
        encoder_first,
        encoder_second,
        dynamics_first,
        dynamics_second,
        dynamics_third,
        value_first,
        value_second,
        value_third.transpose(0, 2, 1),
    )

    def like(*shape):
        return jax.ShapeDtypeStruct(shape, F32)

    done = pl.pallas_call(
        functools.partial(finish_kernel, sizes),
        out_shape=(
            like(observed, 1, rows),
            like(tasks, task_width),
            like(observed + task_width, 128),
            like(1, hidden),
            like(1, hidden),
            like(128, latent_width),
            like(1, latent_width),
            like(1, latent_width),
            like(inputs, 128),
            like(1, hidden),
            like(1, hidden),
            like(128, hidden),
            like(1, hidden),
            like(1, hidden),
            like(128, latent_width),
            like(1, latent_width),
            like(1, latent_width),
            like(heads, inputs, 128),
            like(heads, hidden),
            like(heads, hidden),
            like(heads, 128, hidden),
            like(heads, hidden),
            like(heads, hidden),
            like(heads, bins, 128),
            like(heads, bins),
        ),
        in_specs=[anywhere] * 8,
        out_specs=[vmem] * 25,
        scratch_shapes=[
            *(bf16(*shape) for shape in shapes),
            f32(4, 8, hidden),
            f32(4, 16, hidden),
            f32(observed, rows),
            pltpu.SemaphoreType.DMA((8,)),
        ],
        compiler_params=pltpu.CompilerParams(vmem_limit_bytes=FINISH_VMEM),
    )(*outs)
    done = [item.reshape(-1) if item.shape[0] == 1 else item for item in done]
    done[0] = done[0].transpose(1, 2, 0)
    done[23] = done[23].transpose(0, 2, 1)
    return tuple(done)


def solution(mesh):
    in_specs = (
        P(None, "dp", None),
        P(None, None, "dp", None),
        P(),
        P(None, "dp"),
        P(None, None, "dp", None),
        P(None, None, "dp"),
        P(None, None, "dp"),
    ) + (P(),) * 24
    out_specs = (
        P("section", "dp", None),
        P(),
        P(None, "dp"),
        P(),
        P(),
        P("dp", None),
        P(),
        P(),
        P(None, "dp"),
        P(),
        P(),
        P("dp", None),
        P(),
        P(),
        P("dp", None),
        P(),
        P(),
        P(None, None, "dp"),
        P(),
        P(),
        P(None, "dp", None),
        P(),
        P(),
        P(None, "dp", None),
        P(),
    )
    paired = (mesh.shape["section"], mesh.shape["dp"]) == (4, 8)
    return jax.shard_map(
        step_device if paired else plain_device,
        mesh=mesh,
        in_specs=in_specs,
        out_specs=out_specs,
        check_vma=False,
    )
```

```python
import functools

import jax
import jax.numpy as jnp
from jax import lax
from jax.experimental import pallas as pl
from jax.experimental.pallas import tpu as pltpu
from jax.sharding import PartitionSpec as P

SIMNORM = 8
epsilon = 1e-05
discount = 0.5
consistency_weight = 20.0
value_weight = 0.1

F32, BF16 = jnp.float32, jnp.bfloat16
WIDE_GROUP = 16
GROUP = 16
KERNEL_VMEM = 63 << 20
FINISH_VMEM = 63 << 20


def ceil_to(value, unit):
    return -(-value // unit) * unit


def row_sum(values):
    return jnp.sum(values, -1, keepdims=True)


def col_sum(values):
    return jnp.sum(values, 0, keepdims=True)


def dot(a, b):
    return lax.dot_general(a, b, (((1,), (0,)), ((), ())), preferred_element_type=F32)


def dot_left(a, b):
    return lax.dot_general(a, b, (((0,), (0,)), ((), ())), preferred_element_type=F32)


def dot_right(a, b):
    return lax.dot_general(a, b, (((1,), (1,)), ((), ())), preferred_element_type=F32)


def loop(count, body, unroll=1):
    def step(i, carry):
        body(i)
        return carry

    lax.fori_loop(0, count, step, 0, unroll=unroll)


def at(i, size):
    return pl.ds(pl.multiple_of(i * size, size), size)


def norm(values):
    scale = 1.0 / values.shape[1]
    center = values - row_sum(values) * scale
    rstd = lax.rsqrt(row_sum(center * center) * scale + epsilon)
    return center * rstd, rstd


def norm_back(grad, xhat, rstd):
    scale = 1.0 / grad.shape[1]
    mean_grad = row_sum(grad) * scale
    mean_both = row_sum(grad * xhat) * scale
    return rstd * (grad - mean_grad - xhat * mean_both)


def mish_forward(z, first, count, gain, shift, hidden, xhat_ref, slope, rstd_ref):
    for i in range(0, count, WIDE_GROUP):
        rows = pl.ds(first + i, WIDE_GROUP)
        xhat, rstd = norm(z[pl.ds(i, WIDE_GROUP), :])
        v = xhat * gain + shift
        e = jnp.exp(jnp.minimum(v, 30.0))
        n = e * (e + 2.0)
        r = pl.reciprocal(n + 2.0, approx=True)
        t = n * r
        xhat_ref[rows, :] = xhat.astype(xhat_ref.dtype)
        slope[rows, :] = (t + (4.0 * v) * ((e * r) * ((e + 1.0) * r))).astype(slope.dtype)
        rstd_ref[0][rows, rstd_ref[1] : rstd_ref[1] + 1] = rstd
        hidden[rows, :] = (v * t).astype(BF16)


def mish_backward(upstream, first, count, gain, xhat_ref, slope, rstd_ref, low, both_sums):
    width = upstream.shape[1]
    for i in range(0, count, GROUP):
        rows = pl.ds(first + i, GROUP)
        xhat = xhat_ref[rows, :].astype(F32)
        g = upstream[pl.ds(i, GROUP), :] * slope[rows, :]
        low[rows, :] = norm_back(g * gain, xhat, rstd_ref[0][rows, rstd_ref[1] : rstd_ref[1] + 1]).astype(BF16)
        both_sums[0] = both_sums[0] + (g * xhat).reshape(GROUP // 8, 8, width).sum(0)
        both_sums[1] = both_sums[1] + g.reshape(GROUP // 8, 8, width).sum(0)


def group_matrix(width):
    return (
        lax.broadcasted_iota(jnp.int32, (width, width), 0) // SIMNORM
        == lax.broadcasted_iota(jnp.int32, (width, width), 1) // SIMNORM
    ).astype(BF16)


def group_sums(values, groups):
    parts = []
    for k in range(values.shape[1] // 128):
        part = values[:, k * 128 : (k + 1) * 128]
        high = part.astype(BF16)
        rest = (part - high.astype(F32)).astype(BF16)
        parts.append(dot(high, groups) + dot(rest, groups))
    return jnp.concatenate(parts, 1)


def simnorm_forward(z, gain, shift, xhat_ref, chance, rstd_ref, groups):
    def body(i):
        xhat, rstd = norm(z[at(i, 32), :])
        e = jnp.exp(xhat * gain + shift)
        xhat_ref[at(i, 32), :] = xhat.astype(xhat_ref.dtype)
        chance[at(i, 32), :] = e / group_sums(e, groups)
        rstd_ref[0][at(i, 32), rstd_ref[1] : rstd_ref[1] + 1] = rstd

    loop(z.shape[0] // 32, body, 4)


def simnorm_backward(upstream, gain, xhat_ref, chance, rstd_ref, groups, low):
    width = gain.shape[1]

    def body(i, carry):
        gain_sum, shift_sum = carry
        xhat = xhat_ref[at(i, 32), :].astype(F32)
        p = chance[at(i, 32), :]
        w = upstream[at(i, 32), :] * p
        g = w - p * group_sums(w, groups)
        gx = g * xhat
        low[at(i, 32), :] = norm_back(g * gain, xhat, rstd_ref[0][at(i, 32), rstd_ref[1] : rstd_ref[1] + 1]).astype(BF16)
        return (
            gain_sum + gx.reshape(4, 8, width).sum(0),
            shift_sum + g.reshape(4, 8, width).sum(0),
        )

    zero = jnp.zeros((8, width), F32)
    gain_sum, shift_sum = lax.fori_loop(0, upstream.shape[0] // 32, body, (zero, zero), unroll=4)
    return col_sum(gain_sum), col_sum(shift_sum)


ORDERS = {
    "As": ("c", "z0", "y", "x", "z1"),
    "Bs": ("c", "x", "z0", "z1", "y"),
    "A0": ("c", "y", "z0", "z1"),
    "B0": ("c", "z0", "y", "z1"),
    "A1": ("c", "y", "z0", "z1"),
    "B1": ("c", "z0", "y", "z1"),
    "D2": ("c", "x", "y", "z0", "z1"),
    "F2": ("c", "y", "x", "z0", "z1"),
    "D1": ("c", "y", "z0", "z1", "x"),
    "G1": ("c", "z0", "y", "x", "z1"),
    "D3": ("c", "x", "y", "z0", "z1"),
    "E2": ("c", "z0", "y", "x", "z1"),
    "E1": ("c", "y", "z0", "x", "z1"),
}
SCHEDULE = {
    ("c", 0): [("L0", -1)],
    ("c", 1): [("L1", -1)],
    ("c", 2): [("L2", -1)],
    ("h", 0, 1): [("L0", 0), ("L1", 0)],
    ("h", 0, 4): [("As", -1), ("L2", 0)],
    ("h", 0, 7): [("Bs", -1), ("As", 0)],
    ("h", 1, 3): [("Bs", 0)],
    ("h", 2, 4): [("A0", -1), ("As", 1), ("Bs", 1)],
    ("h", 2, 7): [("Bs", 2), ("B0", -1), ("A0", 0)],
    ("h", 3, 1): [("As", 2)],
    ("h", 3, 2): [("B0", 0)],
    ("h", 3, 4): [("Bs", 3)],
    ("h", 3, 5): [("As", 3)],
    ("h", 4, 3): [("A0", 1), ("B0", 1), ("Bs", 4)],
    ("h", 4, 4): [("A1", -1), ("As", 4)],
    ("h", 4, 5): [("Bs", 5)],
    ("h", 4, 7): [("B0", 2), ("B1", -1), ("A1", 0), ("As", 5), ("Bs", 6), ("A0", 2)],
    ("t", 0): [("R2", -1), ("R1", -1), ("R0", -1), ("T", -1)],
    ("b", 0, 3): [("B1", 0), ("As", 6), ("T", 0), ("R2", 0)],
    ("b", 1, 1): [("B0", 3)],
    ("b", 1, 3): [("R1", 0)],
    ("b", 2, 3): [("R0", 0)],
    ("t", 10): [("D2", -1), ("F2", -1), ("A0", 3), ("T", 1), ("A1", 1)],
    ("t", 11): [("B1", 1), ("B1", 2), ("D1", -1), ("G1", -1), ("B0", 4), ("D2", 0), ("F2", 0), ("T", 2), ("A0", 4), ("A1", 2)],
    ("t", 12): [("D3", -1), ("D1", 0)],
    ("t", 13): [("G1", 0), ("B0", 5), ("A0", 5), ("T", 3), ("D3", 0), ("B1", 3)],
    ("t", 14): [("E2", -1)],
    ("t", 15): [("E1", -1), ("D2", 1)],
    ("t", 16): [("S", -1), ("F2", 1)],
    ("t", 17): [("E2", 0), ("E1", 0), ("A1", 3), ("S", 0), ("G1", 1), ("D1", 1), ("D3", 1), ("T", 4), ("D2", 2), ("B1", 4), ("E1", 1), ("B1", 5), ("F2", 2), ("E2", 1), ("G1", 2), ("D1", 2), ("A1", 4), ("D3", 2), ("S", 1), ("D2", 3), ("E1", 2), ("T", 5), ("A1", 5), ("G1", 3), ("E2", 2), ("F2", 3), ("S", 2), ("D1", 3), ("E1", 3), ("T", 6), ("D3", 3), ("D2", 4), ("G1", 4), ("E2", 3), ("D1", 4), ("F2", 4), ("S", 3), ("E1", 4), ("D2", 5), ("D3", 4), ("G1", 5), ("D1", 5), ("F2", 5), ("E2", 4), ("E1", 5), ("D2", 6), ("G1", 6), ("S", 4), ("D3", 5), ("D1", 6), ("F2", 6), ("E1", 6), ("E2", 5), ("D3", 6), ("S", 5), ("E2", 6), ("S", 6)],
}


class Piece:
    def __init__(self, index, order, buffers, gathered, credit=None, gives=False):
        self.index, self.order, self.buffers, self.gathered = index, order, buffers, gathered
        self.credit, self.gives = credit, gives
        self.stages = len(order) + 2


class Exchange:
    def __init__(self, send_sem, recv_sem, free_sem):
        self.send_sem, self.recv_sem, self.free_sem = send_sem, recv_sem, free_sem
        section, dp = lax.axis_index("section"), lax.axis_index("dp")
        self.bit = {
            "c": section % 2,
            "x": section // 2,
            "y": dp % 2,
            "z0": (dp // 2) % 2,
            "z1": dp // 4,
        }
        self.partner = {
            "c": {"section": section + 1 - 2 * self.bit["c"]},
            "x": {"section": section + 2 - 4 * self.bit["x"]},
            "y": {"dp": dp + 1 - 2 * self.bit["y"]},
            "z0": {"dp": dp + 2 - 4 * self.bit["z0"]},
            "z1": {"dp": dp + 4 - 8 * self.bit["z1"]},
        }

    def greet(self):
        barrier = pltpu.get_barrier_semaphore()
        for axis in self.partner:
            self.signal(barrier, axis)
        pl.semaphore_wait(barrier, len(self.partner))

    def signal(self, sem, axis):
        pl.semaphore_signal(
            sem, inc=1, device_id=self.partner[axis], device_id_type=pl.DeviceIdType.MESH
        )

    def remote(self, source, target, index, stage, axis):
        return pltpu.make_async_remote_copy(
            src_ref=source,
            dst_ref=target,
            send_sem=self.send_sem.at[index, stage],
            recv_sem=self.recv_sem.at[index, stage],
            device_id=self.partner[axis],
            device_id_type=pl.DeviceIdType.MESH,
        )

    def place(self, order, rank, quarter):
        bits = {
            "c": quarter // 2,
            "x": quarter % 2,
            "y": rank % 2,
            "z0": (rank // 2) % 2,
            "z1": rank // 4,
        }
        index = 0
        for axis in order if len(order) == 5 else order + ("x",):
            index = index * 2 + bits[axis]
        return index

    def copy(self, piece, stage):
        c, x = self.bit["c"], self.bit["x"]
        count = len(piece.order)
        if stage < count:
            axis = piece.order[stage]
            half = 32 >> (stage + 1)
            source = piece.buffers[stage].at[pl.ds((1 - self.bit[axis]) * half, half)]
            target = piece.buffers[stage + 1]
        elif stage == count:
            axis = "x"
            source = target = piece.gathered.at[c, x]
        else:
            axis = "c"
            source = target = piece.gathered.at[c]
        return self.remote(source, target, piece.index, stage, axis)

    def begin(self, piece):
        if piece.credit is not None:
            pl.semaphore_wait(self.free_sem.at[piece.credit], 1)
        self.copy(piece, 0).start()

    def advance(self, piece, stage):
        last = stage + 1 == piece.stages
        self.copy(piece, stage).wait_recv()
        if stage == 0 or last:
            self.copy(piece, stage).wait_send()
        if stage > 1:
            self.copy(piece, stage - 1).wait_send()
        if stage == 2 and piece.gives is not False:
            self.signal(self.free_sem.at[piece.gives], "c")
        count = len(piece.order)
        if stage < count:
            half = 32 >> (stage + 1)
            first = self.bit[piece.order[stage]] * half
            kept, total = piece.buffers[stage], piece.buffers[stage + 1]
            if stage < count - 1:

                def add(i):
                    total[i] = total[i] + kept[first + i]

                loop(half, add, min(half, 4))
            else:
                for i in range(half):
                    piece.gathered[self.bit["c"], self.bit["x"], i] = total[i] + kept[first + i]
        if not last:
            self.copy(piece, stage + 1).start()


class Sums:
    def __init__(self, index, parts, gathered, exchange):
        self.index, self.parts, self.gathered, self.exchange = index, parts, gathered, exchange
        self.stages = 7

    def copy(self, stage):
        parts = self.parts
        c, x = self.exchange.bit["c"], self.exchange.bit["x"]
        if stage == 0:
            axis, source, target = "c", parts[0].at[pl.ds((1 - c) * 2, 2)], parts[1]
        elif stage == 1:
            axis, source, target = "x", parts[1].at[1 - x], parts[2]
        elif stage < 5:
            axis, source, target = ("y", "z0", "z1")[stage - 2], parts[stage], parts[stage + 1]
        elif stage == 5:
            axis = "x"
            source = target = self.gathered.at[c * 2 + x]
        else:
            axis = "c"
            source = target = self.gathered.at[pl.ds(c * 2, 2)]
        return self.exchange.remote(source, target, self.index, stage, axis)

    def begin(self):
        self.copy(0).start()

    def advance(self, stage):
        parts = self.parts
        c, x = self.exchange.bit["c"], self.exchange.bit["x"]
        self.copy(stage).wait()
        if stage == 0:
            parts[1][...] = parts[1][...] + parts[0][pl.ds(c * 2, 2)]
        elif stage == 1:
            parts[2][...] = parts[2][...] + parts[1][x]
        elif stage < 4:
            parts[stage + 1][...] = parts[stage + 1][...] + parts[stage][...]
        elif stage == 4:
            self.gathered[c * 2 + x] = parts[5][...] + parts[4][...]
        if stage + 1 < self.stages:
            self.copy(stage + 1).start()


def step_kernel(
    sizes,
    obs_ref,
    act_ref,
    ids_ref,
    low_ref,
    frac_ref,
    mask_ref,
    task_ref,
    enc_one_gain,
    enc_one_shift,
    enc_two_gain,
    enc_two_shift,
    dyn_one_gain,
    dyn_one_shift,
    dyn_two_gain,
    dyn_two_shift,
    dyn_three_gain,
    dyn_three_shift,
    value_one_gain,
    value_one_shift,
    value_two_gain,
    value_two_shift,
    value_bias,
    goals_ref,
    we1_ref,
    we2_ref,
    wd1_ref,
    wd2_ref,
    wd3_ref,
    wv1_ref,
    wv2_ref,
    wv3_ref,
    ga_ref,
    ga_pair_ref,
    gb_ref,
    gb_pair_ref,
    ge_ref,
    small_ref,
    heads_ref,
    obs_grad_ref,
    goals,
    we1_raw,
    we1,
    we2,
    wd1,
    wd1_rest,
    wd2,
    wd3,
    wv1,
    wv1_rest,
    wv2,
    wv3_raw,
    wv3,
    x_enc,
    x_all,
    x_now,
    turned,
    onehot,
    target,
    param_ref,
    z_chain,
    slope_chain,
    rstd_chain,
    hid_chain,
    z_lat,
    lat,
    rstd_lat,
    dz_lat,
    z1,
    s1,
    r_both,
    h1,
    z2,
    s2,
    h2,
    up_a,
    up_b,
    up,
    carry,
    both_sums,
    dz,
    dlog,
    dx,
    lat_in,
    dx_in,
    pa,
    pb,
    pe,
    half_a,
    half_b,
    half_e,
    last_a,
    last_b,
    last_e,
    all_a,
    all_a_pair,
    all_b,
    all_b_pair,
    all_e,
    small,
    small_parts,
    small_all,
    heads_small,
    heads_parts,
    heads_all,
    chain_sem,
    goal_sem,
    value_sem,
    out_sem,
    send_sem,
    recv_sem,
    free_sem,
):
    micro_total, observed, moves, task_width, bins, heads = sizes
    horizon, _, rows, latent_width = goals_ref.shape
    tasks = task_ref.shape[0]
    hidden = wv2_ref.shape[1]
    inputs = wv1_ref.shape[1]
    rest = inputs - latent_width
    total = horizon * rows
    ranks = hidden // 128
    part_rows, rest_rows = pb.shape[1], pa.shape[1]
    section = lax.axis_index("section")
    exchange = Exchange(send_sem, recv_sem, free_sem)
    x_bit = exchange.bit["x"]
    micros = (section, section + 2 - 4 * x_bit)
    own_heads = heads // 2
    shared = heads - 1

    pieces = {}

    def piece(name, own, half, last, gathered, credit=None, gives=False):
        order = ORDERS[name]
        buffers = [own, half] + last
        pieces[name] = Piece(len(pieces), order, buffers, gathered, credit, gives)

    def lasts(refs, k, lanes=None):
        views = [ref.at[k] for ref in refs]
        return views if lanes is None else [view.at[:, :, lanes] for view in views]

    left, right = pl.ds(0, latent_width), pl.ds(latent_width, latent_width)
    piece("As", pa, half_a.at[0], lasts(last_a, 0), all_a.at[0], None, 0)
    piece("A0", pa, half_a.at[1], lasts(last_a, 1), all_a_pair.at[0], None, 1)
    whole = slice(None)
    for name, lanes, k, slot, final, credit, gives in (
        ("A1", left if "C1" in ORDERS else whole, 2, 0, all_a_pair.at[1], 0, 0),
        ("C1", right, 2, 0, all_a_pair.at[1], None, 2),
        ("D2", left if "F2" in ORDERS else whole, 3, 1, all_a.at[1], 1, False),
        ("F2", right, 3, 1, all_a.at[1], None, False),
        ("D3", left, 4, 0, all_a.at[2], 0, False),
        ("E2", right, 4, 0, all_a.at[2], 2 if "C1" in ORDERS else None, False),
    ):
        if name in ORDERS:
            piece(
                name,
                pa.at[:, :, lanes],
                half_a.at[slot, :, :, lanes],
                lasts(last_a, k, lanes),
                final.at[:, :, :, :, lanes],
                credit,
                gives,
            )
    piece("Bs", pb, half_b, lasts(last_b, 0), all_b.at[0], None, 4)
    piece("B0", pb, half_b, lasts(last_b, 1), all_b_pair.at[0], 4, 4)
    half_rows = part_rows // 2
    first_half, second_half = pl.ds(0, half_rows), pl.ds(half_rows, half_rows)
    for name, those, k, final, credit, gives in (
        ("B1", first_half if "H1" in ORDERS else whole, 2, all_b_pair.at[1], 4, 4),
        ("H1", second_half, 2, all_b_pair.at[1], None, 3),
        ("D1", first_half if "G1" in ORDERS else whole, 3, all_b.at[1], 4, False),
        ("G1", second_half, 3, all_b.at[1], 3 if "H1" in ORDERS else None, False),
    ):
        if name in ORDERS:
            piece(
                name,
                pb.at[:, those],
                half_b.at[:, those],
                [ref.at[k, :, those] for ref in last_b],
                final.at[:, :, :, those],
                credit,
                gives,
            )
    piece("E1", pe, half_e, list(last_e), all_e)
    sums = {
        "S": Sums(len(pieces), [small, *small_parts], small_all, exchange),
        "T": Sums(len(pieces) + 1, [heads_small, *heads_parts], heads_all, exchange),
    }
    swaps = len(pieces) + 2

    def swap(name):
        t = int(name[1])
        if name[0] == "L":
            source, target_ref, stage = x_all.at[pl.ds(t * rows, rows), pl.ds(0, latent_width)], lat_in.at[t], t
        else:
            source, target_ref, stage = lat_in.at[t], dx_in.at[t], horizon + t
        return exchange.remote(source, target_ref, swaps, stage, "x")

    def act(name, stage):
        if name[0] in "LR":
            if stage < 0:
                swap(name).start()
            else:
                swap(name).wait()
        elif name in sums:
            if stage < 0:
                sums[name].begin()
            else:
                sums[name].advance(stage)
        elif stage < 0:
            exchange.begin(pieces[name])
        else:
            exchange.advance(pieces[name], stage)

    def tick(*key):
        for name, stage in SCHEDULE.get(key, ()):
            act(name, stage)

    def loop_tick(group, index, point=None):
        for key in SCHEDULE:
            if key[0] == group and key[2:] == (() if point is None else (point,)):
                pl.when(index == key[1])(functools.partial(tick, *key))

    def chain_copies():
        return [
            pltpu.make_async_copy(source, place, chain_sem.at[k])
            for k, (source, place) in enumerate(
                (
                    (we1_ref, we1_raw),
                    (we2_ref, we2),
                    (wd1_ref, wd1),
                    (wd2_ref, wd2),
                    (wd3_ref, wd3),
                )
            )
        ]

    def value_copy(q, index):
        source, place = ((wv1_ref, wv1), (wv2_ref, wv2), (wv3_ref, wv3_raw))[index]
        return pltpu.make_async_copy(source.at[q], place, value_sem.at[index])

    for copy in chain_copies():
        copy.start()
    goal_copies = [
        pltpu.make_async_copy(goals_ref.at[t, section], goals.at[t], goal_sem.at[t]) for t in range(horizon)
    ]
    for copy in goal_copies:
        copy.start()

    small[...] = jnp.zeros_like(small)
    heads_small[...] = jnp.zeros_like(heads_small)
    dx[...] = jnp.zeros_like(dx)
    param_ref[...] = jnp.zeros_like(param_ref)
    we1[...] = jnp.zeros_like(we1)
    wd1_rest[...] = jnp.zeros_like(wd1_rest)
    wv1_rest[...] = jnp.zeros_like(wv1_rest)
    wv3[...] = jnp.zeros_like(wv3)
    turned[...] = jnp.zeros_like(turned)
    groups = group_matrix(128)

    def pick(ref, micro):
        out = jnp.zeros((1, rows), ref.dtype)
        for m in range(micro_total):
            out = out + jnp.where(micro == m, ref[m : m + 1, :], jnp.zeros((1, rows), ref.dtype))
        return out

    def line(ref):
        return ref[...].astype(F32).reshape(1, ref.shape[0])

    for index, vector in enumerate(
        (
            line(enc_one_gain),
            line(enc_one_shift),
            jnp.concatenate([line(enc_two_gain), line(enc_two_shift)], 1),
            line(dyn_one_gain),
            line(dyn_one_shift),
            line(dyn_two_gain),
            line(dyn_two_shift),
            jnp.concatenate([line(dyn_three_gain), line(dyn_three_shift)], 1),
        )
    ):
        param_ref[index : index + 1, :] = vector
    for index, ref in enumerate((value_one_gain, value_one_shift, value_two_gain, value_two_shift, value_bias)):
        for q in range(heads):
            at_row = 8 * (q + 1) + index
            param_ref[at_row : at_row + 1, : ref.shape[1]] = ref[q : q + 1, :].astype(F32)

    def pick_micro(values, micro):
        out = None
        for m in range(micro_total):
            part = jnp.where(micro == m, values[..., m, :], 0.0)
            out = part if out is None else out + part
        return out

    mask = mask_ref[...].astype(F32).astype(BF16)
    all_obs, all_act = obs_ref[...].astype(F32), act_ref[...].astype(F32)
    for j, micro in enumerate(micros):
        hot = (lax.broadcasted_iota(jnp.int32, (tasks, rows), 0) == pick(ids_ref, micro)).astype(BF16)
        onehot[j] = hot
        embedded = dot_left(task_ref[...], hot)
        allowed = dot(mask, hot)
        acts = pick_micro(all_act, micro)
        turned[moves:rest, :] = embedded
        for t in range(horizon):
            turned[0:moves, :] = acts[t] * allowed
            at_rows = slice((j * horizon + t) * rows, (j * horizon + t + 1) * rows)
            x_all[at_rows, latent_width:] = turned[:128, :].T.astype(BF16)
            bin_at = lax.broadcasted_iota(jnp.int32, (128, rows), 0)
            lower, upper_part = pick(low_ref.at[t], micro), pick(frac_ref.at[t], micro)
            target[at_rows, :] = (
                jnp.where(bin_at == lower, 1.0 - upper_part, 0.0) + jnp.where(bin_at == lower + 1, upper_part, 0.0)
            ).T
        if j == 0:
            turned[0:observed, :] = pick_micro(all_obs, micro)
            turned[observed : observed + task_width, :] = embedded
            x_enc[:, :128] = turned[:128, :].T.astype(BF16)
            x_enc[:, 128:] = turned[128:, :].T.astype(BF16)
            turned[...] = jnp.zeros_like(turned)

    def vec(index):
        return param_ref[index : index + 1, :]

    ups = (up_a, up_b)
    wide_up = up_a.at[pl.ds(0, rows), :]
    carry_up = up_a.at[pl.ds(0, rows), pl.ds(0, latent_width)]
    lat_up = up_b.at[pl.ds(0, rows), pl.ds(0, latent_width)]

    def in_blocks(count, product, after):
        size = up_a.shape[0] if count % up_a.shape[0] == 0 else rows
        blocks = [pl.ds(k * size, size) for k in range(count // size)]
        ups[0][:size, :] = product(blocks[0])
        for k, block in enumerate(blocks):
            if k + 1 < len(blocks):
                ups[(k + 1) % 2][:size, :] = product(blocks[k + 1])
            after(ups[k % 2], k * size, size)

    def forward_blocks(count, product, gain, shift, hidden_ref, xhat_ref, slope, rstd_ref):
        def after(z, first, size):
            mish_forward(z, first, size, gain, shift, hidden_ref, xhat_ref, slope, rstd_ref)

        in_blocks(count, product, after)

    def backward_blocks(count, product, gain, xhat_ref, slope, rstd_ref, low):
        both_sums[...] = jnp.zeros_like(both_sums)

        def after(upstream, first, size):
            mish_backward(upstream, first, size, gain, xhat_ref, slope, rstd_ref, low, both_sums)

        in_blocks(count, product, after)
        return col_sum(both_sums[0]), col_sum(both_sums[1])


    def mish_layer(product, index, slot):
        forward_blocks(
            rows,
            product,
            vec(index),
            vec(index + 1),
            hid_chain.at[at(slot, rows), :],
            z_chain.at[slot],
            slope_chain.at[slot],
            (rstd_chain.at[slot], 0),
        )

    def latent_layer(weight, hidden_slot, index, slot):
        carry_up[...] = dot(hid_chain[at(hidden_slot, rows), :], weight[...])
        simnorm_forward(
            carry_up,
            vec(index)[:, :latent_width],
            vec(index)[:, latent_width:],
            z_lat.at[slot],
            lat.at[slot],
            (rstd_lat.at[slot], 0),
            groups,
        )

    copies = chain_copies()
    copies[0].wait()
    we1[: observed + task_width, :] = we1_raw[...]
    mish_layer(lambda block: dot(x_enc[block, :], we1[...]), 0, 0)
    copies[1].wait()
    latent_layer(we2, 0, 2, 0)
    copies[2].wait()
    copies[3].wait()
    copies[4].wait()
    for index in range(3):
        value_copy(shared, index).start()
    wd1_rest[:rest, :] = wd1[latent_width:, :]
    exchange.greet()
    def dynamics_step(t):
        own = at(t, rows)
        x_all[own, :latent_width] = lat[t].astype(BF16)
        loop_tick("c", t)
        mish_layer(
            lambda block: dot(x_all[own, :latent_width], wd1[:latent_width, :])
            + dot(x_all[own, latent_width:], wd1_rest[...]),
            3,
            1 + t,
        )
        mish_layer(lambda block: dot(hid_chain[at(1 + t, rows), :], wd2[...]), 5, 1 + horizon + t)
        latent_layer(wd3, 1 + horizon + t, 7, t + 1)

    loop(horizon, dynamics_step)

    def placed(name):
        return lambda rank, quarter: exchange.place(ORDERS[name], rank, quarter)

    def put_rows(place_of, own, rank, block, lanes=slice(None), more=None):
        low = block.astype(BF16)
        for k in range(low.shape[0] // rest_rows):
            place = place_of(rank + k // 4, k % 4)
            part = low[k * rest_rows : (k + 1) * rest_rows]
            own[place, :, lanes] = part if more is None else jnp.where(more, part + own[place, :, lanes], part)

    def put_lanes(places, own, rank, block, begin=0, more=None):
        low = block.astype(BF16)
        quarter_rows = own.shape[1]
        part_size = quarter_rows // len(places)
        for k in range(low.shape[1] // 128):
            done = 0
            while done < low.shape[0]:
                quarter, offset = divmod(begin + done, quarter_rows)
                which, inside = divmod(offset, part_size)
                count = min(part_size - inside, low.shape[0] - done)
                place = places[which](rank + k, quarter)
                part = low[done : done + count, k * 128 : (k + 1) * 128]
                own[place, offset : offset + count, :] = (
                    part if more is None else jnp.where(more, part + own[place, offset : offset + count, :], part)
                )
                done += count

    def head_pass(j):
        fifth = 1 - (j + 2 * own_heads) // (2 * own_heads + 1)
        q = fifth * shared + (1 - fifth) * (x_bit * own_heads + (j - 1) // 2)
        others = (1 - fifth) * (1 - j % 2)

        def mixed(first_name, other_name):
            def place_of(rank, quarter):
                first = exchange.place(ORDERS[first_name], rank, quarter)
                other = exchange.place(ORDERS[other_name], rank, quarter)
                return other + fifth * (first - other)

            return place_of

        more = others == 1
        block = param_ref[pl.ds(pl.multiple_of(8 * (q + 1), 8), 8), :]
        first_gain, first_shift, second_gain, second_shift, bias = (block[k : k + 1, :] for k in range(5))
        offset = others * total

        def arrived(index):
            pl.when(others == 0)(lambda: value_copy(q, index).wait())

        def prefetch(index):
            nxt = x_bit * own_heads + j // 2
            pl.when((j % 2 == 0) & (j < 2 * own_heads))(lambda: value_copy(nxt, index).start())

        @pl.when(j == 2)
        def _():
            for t in range(horizon):
                x_all[total + t * rows : total + (t + 1) * rows, :latent_width] = lat_in[t]

        x_now[...] = x_all[pl.ds(pl.multiple_of(offset, total), total), :]
        arrived(0)

        @pl.when(others == 0)
        def _():
            wv1_rest[:rest, :] = wv1[latent_width:, :]

        forward_blocks(
            total,
            lambda block: dot(x_now[block, :latent_width], wv1[:latent_width, :])
            + dot(x_now[block, latent_width:], wv1_rest[...]),
            first_gain,
            first_shift,
            h1,
            z1,
            s1,
            (r_both, 0),
        )
        loop_tick("h", j, 1)
        arrived(1)
        forward_blocks(total, lambda block: dot(h1[block, :], wv2[...]), second_gain, second_shift, h2, z2, s2, (r_both, 1))
        loop_tick("h", j, 2)
        arrived(2)

        @pl.when(others == 0)
        def _():
            wv3[:bins, :] = wv3_raw[...]

        prefetch(2)
        valid = lax.broadcasted_iota(jnp.int32, (1, 128), 1) < bins
        bias_sum = jnp.zeros((1, 128), F32)
        for t in range(horizon):
            factor = value_weight * discount**t / (heads * micro_total)
            own = slice(t * rows, (t + 1) * rows)
            logits = jnp.where(valid, dot_right(h2[own, :], wv3[...]) + bias[:, :128], -1e30)
            e = jnp.exp(logits - jnp.max(logits, -1, keepdims=True))
            goal = target[pl.ds(pl.multiple_of(offset + t * rows, rows), rows), :]
            delta = factor * (e / row_sum(e) - goal)
            dlog[own, :] = delta.astype(BF16)
            bias_sum = bias_sum + col_sum(delta)
        second_sums = backward_blocks(
            total, lambda block: dot(dlog[block, :], wv3[...]), second_gain, z2, s2, (r_both, 1), dz
        )
        loop_tick("h", j, 3)
        for part in range(2):
            columns = pl.ds(part * (hidden // 2), hidden // 2)
            product = dot_left(h1[:, columns], dz[...])
            put_rows(mixed("As", "A0"), pa, part * (ranks // 2), product, slice(None), more)
        loop_tick("h", j, 4)
        both_sums[...] = jnp.zeros_like(both_sums)
        up[...] = dot_right(dz[...], wv2[...])
        mish_backward(up, 0, total, first_gain, z1, s1, (r_both, 0), dz, both_sums)
        prefetch(1)
        loop_tick("h", j, 5)
        here = pl.ds(pl.multiple_of(offset, total), total)
        dx[here, :latent_width] = dx[here, :latent_width] + dot_right(dz[...], wv1[:latent_width, :])
        dx[here, latent_width:] = dx[here, latent_width:] + dot_right(dz[...], wv1_rest[...])
        prefetch(0)
        loop_tick("h", j, 6)
        for part in range(2):
            columns = pl.ds(part * (hidden // 2), hidden // 2)
            put_lanes([mixed("Bs", "B0")], pb, part * (ranks // 2), dot_left(x_now[...], dz[:, columns]), 0, more)
        put_lanes([mixed("Bs", "B0")], pb, 0, dot_left(dlog[...], h2[...]), latent_width + 128, more)
        pad = jnp.zeros((1, hidden - 128), F32)
        place = pl.ds(pl.multiple_of(q % 2 * 8, 8), 8)
        heads_small[q // 2, place, :] = heads_small[q // 2, place, :] + jnp.concatenate(
            [
                col_sum(both_sums[0]),
                col_sum(both_sums[1]),
                *second_sums,
                jnp.concatenate([bias_sum, pad], 1),
                jnp.zeros((3, hidden), F32),
            ],
            0,
        )
        loop_tick("h", j, 7)

    loop(1 + 2 * own_heads, head_pass)

    for t in range(horizon):
        lat_in[t] = dx[total + t * rows : total + (t + 1) * rows, :latent_width].astype(BF16)
    tick("t", 0)
    for copy in goal_copies:
        copy.wait()
    embed_sums = []
    for j in range(2):
        parts = [dx[(j * horizon + t) * rows : (j * horizon + t + 1) * rows, latent_width:] for t in range(horizon)]
        embed_sums.append(sum(parts[1:], parts[0]))
    dz_one, dz_two = h1, dz
    gain_lat = vec(7)[:, :latent_width]
    carry[...] = jnp.zeros_like(carry)

    def step_backward(i, sums):
        t = horizon - 1 - i
        factor = 0.0
        for k in range(horizon):
            factor = jnp.where(t == k, 2.0 * consistency_weight * discount**k / (micro_total * latent_width), factor)
        lat_up[...] = factor * (lat[t + 1] - goals[t].astype(F32)) + carry[...]
        own = at(t, rows)
        one, two = 1 + t, 1 + horizon + t
        lat_sums = simnorm_backward(
            lat_up, gain_lat, z_lat.at[t + 1], lat.at[t + 1], (rstd_lat.at[t + 1], 0), groups, dz_lat.at[own, :]
        )
        two_sums = backward_blocks(
            rows,
            lambda block: dot_right(dz_lat[own, :], wd3[...]),
            vec(5),
            z_chain.at[two],
            slope_chain.at[two],
            (rstd_chain.at[two], 0),
            dz_two.at[own, :],
        )
        loop_tick("b", i, 1)
        one_sums = backward_blocks(
            rows,
            lambda block: dot_right(dz_two[own, :], wd2[...]),
            vec(3),
            z_chain.at[one],
            slope_chain.at[one],
            (rstd_chain.at[one], 0),
            dz_one.at[own, :],
        )
        loop_tick("b", i, 2)
        latent_delta = dot_right(dz_one[own, :], wd1[:latent_width, :])
        rest_delta = dot_right(dz_one[own, :], wd1_rest[...])
        loop_tick("b", i, 3)
        carry[...] = latent_delta.astype(BF16).astype(F32) + dx[own, :latent_width] + dx_in[t].astype(F32)
        return tuple(a + b for a, b in zip(sums, (rest_delta, *one_sums, *two_sums, *lat_sums)))

    zero, zero_lat = jnp.zeros((1, hidden), F32), jnp.zeros((1, latent_width), F32)
    totals = lax.fori_loop(
        0, horizon, step_backward, (embed_sums[0], zero, zero, zero, zero, zero_lat, zero_lat)
    )
    embed_sums[0] = totals[0]
    small[0, 3:8, :] = jnp.concatenate([*totals[1:5], jnp.concatenate(totals[5:], 1)], 0)

    def put_chain(name, grad, first, lanes=slice(None), second_name=None):
        for part in range(2):
            columns = pl.ds(part * (hidden // 2), hidden // 2)
            block = dot_left(hid_chain[first * rows : (first + horizon) * rows, columns], grad[...])
            if second_name is None:
                put_rows(placed(name), pa, part * (ranks // 2), block, lanes)
            else:
                put_rows(placed(name), pa, part * (ranks // 2), block[:, :latent_width], slice(0, latent_width))
                put_rows(
                    placed(second_name),
                    pa,
                    part * (ranks // 2),
                    block[:, latent_width:],
                    slice(latent_width, 2 * latent_width),
                )

    put_chain("D2", dz_two, 1, second_name="F2" if "F2" in ORDERS else None)
    tick("t", 10)
    for part in range(2):
        columns = pl.ds(part * (hidden // 2), hidden // 2)
        put_lanes([placed(name) for name in ("D1", "G1") if name in ORDERS], pb, part * (ranks // 2), dot_left(x_all[:total, :], dz_one[:, columns]))
    tick("t", 11)
    put_chain("D3", dz_lat, 1 + horizon, slice(0, latent_width))
    tick("t", 12)

    lat_up[...] = carry[...]
    low_lat = dz_lat.at[pl.ds(0, rows), :]
    encoder_lat = simnorm_backward(
        lat_up, vec(2)[:, :latent_width], z_lat.at[0], lat.at[0], (rstd_lat.at[0], 0), groups, low_lat
    )
    low_one = dz_one.at[pl.ds(0, rows), :]
    encoder_one = backward_blocks(
        rows,
        lambda block: dot_right(low_lat[...], we2[...]),
        vec(0),
        z_chain.at[0],
        slope_chain.at[0],
        (rstd_chain.at[0], 0),
        low_one,
    )
    small[0, 0:3, :] = jnp.concatenate([*encoder_one, jnp.concatenate(encoder_lat, 1)], 0)
    tick("t", 13)
    put_rows(
        placed("E2"), pa, 0, dot_left(hid_chain[:rows, :], low_lat[...]), slice(latent_width, 2 * latent_width)
    )
    tick("t", 14)
    put_lanes([placed("E1")], pe, 0, dot_left(x_enc[...], low_one[...])[: 4 * pe.shape[1]])
    tick("t", 15)
    enc_up = dot_right(low_one[...], we1[...])
    obs_grad_ref[...] = enc_up[:, :128].T[:observed, :]
    embed_sums[0] = embed_sums[0] + pltpu.roll(enc_up, x_enc.shape[1] - observed + moves, 1)[:, :128]
    table = None
    for j in range(2):
        high = embed_sums[j].astype(BF16)
        low = (embed_sums[j] - high.astype(F32)).astype(BF16)
        part = dot(onehot[j], high) + dot(onehot[j], low)
        table = part if table is None else table + part
    for k in range(tasks // 8):
        small[1 + k // 8, :, (k % 8) * 128 : (k % 8) * 128 + 128] = table[k * 8 : k * 8 + 8]
    tick("t", 16)
    outs = [
        pltpu.make_async_copy(source, place, out_sem.at[k])
        for k, (source, place) in enumerate(
            (
                (all_a, ga_ref),
                (all_a_pair, ga_pair_ref),
                (all_b, gb_ref),
                (all_b_pair, gb_pair_ref),
                (all_e, ge_ref),
            )
        )
    ]
    rest_steps = SCHEDULE[("t", 17)]
    members = (("As", "D2", "F2", "D3", "E2"), ("A0", "A1", "C1"), ("Bs", "D1", "G1"), ("B0", "B1", "H1"), ("E1",))
    done_at = [-1] * len(members)
    for index, (name, stage) in enumerate(rest_steps):
        for group, names in enumerate(members):
            if name in names and stage + 1 == pieces[name].stages:
                done_at[group] = index
    for group, index in enumerate(done_at):
        if index < 0:
            outs[group].start()
    for index, (name, stage) in enumerate(rest_steps):
        act(name, stage)
        for group, last in enumerate(done_at):
            if last == index:
                outs[group].start()
    small_ref[...] = small_all[...]
    heads_ref[...] = heads_all[...]
    for copy in outs:
        copy.wait()


def finish_kernel(
    sizes,
    ga_from,
    ga_pair_from,
    gb_from,
    gb_pair_from,
    ge_from,
    small_from,
    heads_from,
    obs_from,
    obs_out,
    table_ref,
    encoder_first,
    encoder_first_gain,
    encoder_first_shift,
    encoder_second,
    encoder_second_gain,
    encoder_second_shift,
    dynamics_first,
    dynamics_first_gain,
    dynamics_first_shift,
    dynamics_second,
    dynamics_second_gain,
    dynamics_second_shift,
    dynamics_third,
    dynamics_third_gain,
    dynamics_third_shift,
    value_first,
    value_first_gain,
    value_first_shift,
    value_second,
    value_second_gain,
    value_second_shift,
    value_third,
    value_bias,
    ga_ref,
    ga_pair_ref,
    gb_ref,
    gb_pair_ref,
    ge_ref,
    small_ref,
    heads_ref,
    obs_ref,
    sem,
):
    copies = [
        pltpu.make_async_copy(source, place, sem.at[k])
        for k, (source, place) in enumerate(
            (
                (ga_from, ga_ref),
                (ga_pair_from, ga_pair_ref),
                (gb_from, gb_ref),
                (gb_pair_from, gb_pair_ref),
                (ge_from, ge_ref),
                (small_from, small_ref),
                (heads_from, heads_ref),
                (obs_from, obs_ref),
            )
        )
    ]
    for copy in copies:
        copy.start()
    for copy in copies[5:]:
        copy.wait()
    _, _, moves, task_width, bins, heads = sizes
    rest_rows, part_rows = ga_ref.shape[4], gb_ref.shape[4]
    obs_out[:, 0, :] = obs_ref[...]
    inputs = dynamics_first.shape[0]
    latent_width = dynamics_third.shape[1]
    encoder_rows = encoder_first.shape[0]
    third_at = 4 * part_rows - 128
    own_heads = heads // 2

    def move(target, first_row, block):
        count = min(target.shape[0] - first_row, block.shape[0])
        if count > 0:
            target[first_row : first_row + count, :] = block[:count].astype(F32)

    def row(index):
        return small_ref[0, index : index + 1, :]

    def head_row(q, k):
        return heads_ref[q // 2, q % 2 * 8 + k : q % 2 * 8 + k + 1, :]

    encoder_first_gain[...] = row(0)
    encoder_first_shift[...] = row(1)
    encoder_second_gain[...] = row(2)[:, :latent_width]
    encoder_second_shift[...] = row(2)[:, latent_width:]
    dynamics_first_gain[...] = row(3)
    dynamics_first_shift[...] = row(4)
    dynamics_second_gain[...] = row(5)
    dynamics_second_shift[...] = row(6)
    dynamics_third_gain[...] = row(7)[:, :latent_width]
    dynamics_third_shift[...] = row(7)[:, latent_width:]
    for q in range(heads):
        for k, target in enumerate((value_first_gain, value_first_shift, value_second_gain, value_second_shift)):
            target[q : q + 1, :] = head_row(q, k)
        value_bias[q : q + 1, :] = head_row(q, 4)[:, :bins]
    for k in range(table_ref.shape[0] // 8):
        block = small_ref[1 + k // 8, :, (k % 8) * 128 : (k % 8) * 128 + 128]
        table_ref[k * 8 : k * 8 + 8, :] = block[:, moves : moves + task_width]
    for copy in copies[:5]:
        copy.wait()
    for c in range(2):
        for x in range(2):
            quarter = c * 2 + x
            move(value_second.at[heads - 1], quarter * rest_rows, ga_ref[0, c, x, 0])
            move(dynamics_second, quarter * rest_rows, ga_ref[1, c, x, 0])
            move(dynamics_third, quarter * rest_rows, ga_ref[2, c, x, 0, :, :latent_width])
            move(encoder_second, quarter * rest_rows, ga_ref[2, c, x, 0, :, latent_width:])
            move(encoder_first, quarter * ge_ref.shape[3], ge_ref[c, x, 0])
            move(dynamics_first, quarter * part_rows, gb_ref[1, c, x, 0])
            for k in range(own_heads):
                for i in range(2):
                    move(value_second.at[x * own_heads + k], (c * 2 + i) * rest_rows, ga_pair_ref[k, c, x, i])

    def lanes(head, quarter, block):
        first = quarter * part_rows
        move(value_first.at[head], first, block)
        if first + part_rows > third_at:
            move(value_third.at[head], 0, block[third_at - first :])

    for quarter in range(4):
        lanes(heads - 1, quarter, gb_ref[0, quarter // 2, quarter % 2, 0])
        for x in range(2):
            for k in range(own_heads):
                lanes(x * own_heads + k, quarter, gb_pair_ref[k, quarter // 2, x, quarter % 2])


def mish_curve(values):
    return values * jnp.tanh(jax.nn.softplus(values))


def layer_norm(before, gain_vec, shift_vec):
    center = before - jnp.mean(before, -1, keepdims=True)
    spread = jnp.mean(center * center, -1, keepdims=True)
    return center * lax.rsqrt(spread + epsilon) * gain_vec + shift_vec


def sim_norm(values):
    groups = values.reshape(values.shape[:-1] + (values.shape[-1] // SIMNORM, SIMNORM))
    return jax.nn.softmax(groups, -1).reshape(values.shape)


def post_mish(before, gain_vec, shift_vec):
    return mish_curve(layer_norm(before, gain_vec, shift_vec))


def post_simnorm(before, gain_vec, shift_vec):
    return sim_norm(layer_norm(before, gain_vec, shift_vec))


def head_mish(before, gain_vec, shift_vec):
    return post_mish(before, gain_vec[:, None, :], shift_vec[:, None, :])


def matmul(left_side, right_side):
    return jnp.dot(left_side, right_side, preferred_element_type=jnp.float32)


def left_transposed(left_side, right_side):
    return lax.dot_general(
        left_side, right_side, (((0,), (0,)), ((), ())), preferred_element_type=jnp.float32
    )


def right_transposed(left_side, right_side):
    return lax.dot_general(
        left_side, right_side, (((1,), (1,)), ((), ())), preferred_element_type=jnp.float32
    )


def dense_forward(inputs, weight, gain_vec, shift_vec, after_fn):
    before = matmul(inputs, weight)
    return jax.vjp(after_fn, before, gain_vec.astype(jnp.float32), shift_vec.astype(jnp.float32))


def dense_backward(inputs, weight, puller, upstream):
    delta_before, delta_gain, delta_shift = puller(upstream)
    rounded = delta_before.astype(jnp.bfloat16)
    return (
        right_transposed(rounded, weight),
        left_transposed(inputs, rounded),
        delta_gain,
        delta_shift,
    )


def encoder_forward(encoder_params, observed, embedded):
    inputs = jnp.concatenate([observed, embedded], 1)
    hidden, first_pull = dense_forward(
        inputs, encoder_params[0], encoder_params[1], encoder_params[2], post_mish
    )
    hidden_low = hidden.astype(jnp.bfloat16)
    latent, second_pull = dense_forward(
        hidden_low, encoder_params[3], encoder_params[4], encoder_params[5], post_simnorm
    )
    return (latent, (inputs, hidden_low, first_pull, second_pull))


def encoder_backward(encoder_params, retained, upstream):
    inputs, hidden_low, first_pull, second_pull = retained
    delta_hidden, delta_second, second_gain, second_shift = dense_backward(
        hidden_low, encoder_params[3], second_pull, upstream
    )
    delta_inputs, delta_first, first_gain, first_shift = dense_backward(
        inputs, encoder_params[0], first_pull, delta_hidden
    )
    return (
        delta_inputs,
        (delta_first, first_gain, first_shift, delta_second, second_gain, second_shift),
    )


def dynamics_forward(dynamics_params, latent_in, action_low, embedded):
    inputs = jnp.concatenate([latent_in, action_low, embedded], 1)
    layer_one, first_pull = dense_forward(
        inputs, dynamics_params[0], dynamics_params[1], dynamics_params[2], post_mish
    )
    one_low = layer_one.astype(jnp.bfloat16)
    layer_two, second_pull = dense_forward(
        one_low, dynamics_params[3], dynamics_params[4], dynamics_params[5], post_mish
    )
    two_low = layer_two.astype(jnp.bfloat16)
    latent, third_pull = dense_forward(
        two_low, dynamics_params[6], dynamics_params[7], dynamics_params[8], post_simnorm
    )
    return (latent, (inputs, one_low, two_low, first_pull, second_pull, third_pull))


def dynamics_backward(dynamics_params, retained, upstream):
    inputs, one_low, two_low, first_pull, second_pull, third_pull = retained
    delta_two, delta_third, third_gain, third_shift = dense_backward(
        two_low, dynamics_params[6], third_pull, upstream
    )
    delta_one, delta_second, second_gain, second_shift = dense_backward(
        one_low, dynamics_params[3], second_pull, delta_two
    )
    delta_inputs, delta_first, first_gain, first_shift = dense_backward(
        inputs, dynamics_params[0], first_pull, delta_one
    )
    return (
        delta_inputs,
        (
            delta_first,
            first_gain,
            first_shift,
            delta_second,
            second_gain,
            second_shift,
            delta_third,
            third_gain,
            third_shift,
        ),
    )


def value_backward(value_params, inputs, bin_rows, fraction_rows, factor):
    first_before = jnp.einsum(
        "rk,qkn->qrn", inputs, value_params[0], preferred_element_type=jnp.float32
    )
    layer_one, first_pull = jax.vjp(
        head_mish,
        first_before,
        value_params[1].astype(jnp.float32),
        value_params[2].astype(jnp.float32),
    )
    one_low = layer_one.astype(jnp.bfloat16)
    second_before = jnp.einsum(
        "qrk,qkn->qrn", one_low, value_params[3], preferred_element_type=jnp.float32
    )
    layer_two, second_pull = jax.vjp(
        head_mish,
        second_before,
        value_params[4].astype(jnp.float32),
        value_params[5].astype(jnp.float32),
    )
    two_low = layer_two.astype(jnp.bfloat16)
    logits = (
        jnp.einsum("qrk,qkn->qrn", two_low, value_params[6], preferred_element_type=jnp.float32)
        + value_params[7].astype(jnp.float32)[:, None, :]
    )
    chances = jax.nn.softmax(logits, -1)
    columns = lax.broadcasted_iota(jnp.int32, (1, logits.shape[2]), 1)
    lower_bin = bin_rows[:, None]
    target = (1.0 - fraction_rows)[:, None] * (columns == lower_bin).astype(
        jnp.float32
    ) + fraction_rows[:, None] * (columns == lower_bin + 1).astype(jnp.float32)
    delta_logits = factor[None, :, None] * (chances - target[None])
    logit_low = delta_logits.astype(jnp.bfloat16)
    delta_bias = jnp.sum(delta_logits, 1)
    delta_third = jnp.einsum("qrk,qrn->qkn", two_low, logit_low, preferred_element_type=jnp.float32)
    delta_two = jnp.einsum(
        "qrn,qkn->qrk", logit_low, value_params[6], preferred_element_type=jnp.float32
    )
    before_two, second_gain, second_shift = second_pull(delta_two)
    two_round = before_two.astype(jnp.bfloat16)
    delta_second = jnp.einsum(
        "qrk,qrn->qkn", one_low, two_round, preferred_element_type=jnp.float32
    )
    delta_one = jnp.einsum(
        "qrn,qkn->qrk", two_round, value_params[3], preferred_element_type=jnp.float32
    )
    before_one, first_gain, first_shift = first_pull(delta_one)
    one_round = before_one.astype(jnp.bfloat16)
    delta_first = jnp.einsum("rk,qrn->qkn", inputs, one_round, preferred_element_type=jnp.float32)
    delta_inputs = jnp.einsum(
        "qrn,qkn->rk", one_round, value_params[0], preferred_element_type=jnp.float32
    )
    return (
        delta_inputs,
        (
            delta_first,
            first_gain,
            first_shift,
            delta_second,
            second_gain,
            second_shift,
            delta_third,
            delta_bias,
        ),
    )


def reduce_end(gradients):
    def reduced(index, axis):
        shard = lax.psum_scatter(
            gradients[index].astype(jnp.bfloat16), "dp", scatter_dimension=axis, tiled=True
        )
        return lax.psum(shard, "section").astype(jnp.float32)

    return tuple(
        reduced(index, axis)
        for index, axis in ((0, 1), (3, 0), (6, 1), (9, 0), (12, 0), (15, 2), (18, 1), (21, 1))
    )


def plain_device(
    observations,
    actions,
    action_mask,
    task_ids,
    targets,
    bin_low,
    bin_frac,
    task_table,
    encoder_first,
    encoder_first_gain,
    encoder_first_shift,
    encoder_second,
    encoder_second_gain,
    encoder_second_shift,
    dynamics_first,
    dynamics_first_gain,
    dynamics_first_shift,
    dynamics_second,
    dynamics_second_gain,
    dynamics_second_shift,
    dynamics_third,
    dynamics_third_gain,
    dynamics_third_shift,
    value_first,
    value_first_gain,
    value_first_shift,
    value_second,
    value_second_gain,
    value_second_shift,
    value_third,
    value_bias,
):
    encoder_params = (
        encoder_first,
        encoder_first_gain,
        encoder_first_shift,
        encoder_second,
        encoder_second_gain,
        encoder_second_shift,
    )
    dynamics_params = (
        dynamics_first,
        dynamics_first_gain,
        dynamics_first_shift,
        dynamics_second,
        dynamics_second_gain,
        dynamics_second_shift,
        dynamics_third,
        dynamics_third_gain,
        dynamics_third_shift,
    )
    value_params = (
        value_first,
        value_first_gain,
        value_first_shift,
        value_second,
        value_second_gain,
        value_second_shift,
        value_third,
        value_bias,
    )
    sections = lax.axis_size("section")
    level_now = lax.axis_index("section")
    micro_total = observations.shape[0]
    share = micro_total // sections
    latent_width = dynamics_third.shape[1]
    action_width = actions.shape[3]
    observed_width = observations.shape[2]
    horizon = actions.shape[0]
    heads = value_first.shape[0]
    task_count = task_table.shape[0]

    def mine(array, axis):
        part = lax.dynamic_slice_in_dim(array, level_now * share, share, axis)
        shape = part.shape
        return part.reshape(shape[:axis] + (shape[axis] * shape[axis + 1],) + shape[axis + 2 :])

    observed = mine(observations, 0)
    movement = mine(actions, 1)
    task_rows = mine(task_ids, 0)
    goals = mine(targets, 1)
    low_bins = mine(bin_low, 1)
    fractions = mine(bin_frac, 1)
    rows = observed.shape[0]
    onehot = (task_rows[:, None] == lax.broadcasted_iota(jnp.int32, (1, task_count), 1)).astype(
        jnp.bfloat16
    )
    embedded = matmul(onehot, task_table).astype(jnp.bfloat16)
    allowed = matmul(onehot, action_mask.astype(jnp.bfloat16))
    chosen = (movement.astype(jnp.float32) * allowed[None]).astype(jnp.bfloat16)

    latent, encoder_kept = encoder_forward(encoder_params, observed, embedded)
    latents = [latent]
    dynamics_kept = []
    for step in range(horizon):
        latent, kept = dynamics_forward(
            dynamics_params, latents[step].astype(jnp.bfloat16), chosen[step], embedded
        )
        latents.append(latent)
        dynamics_kept.append(kept)
    inputs = jnp.concatenate([kept[0] for kept in dynamics_kept], 0)
    step_weight = jnp.asarray(
        [value_weight * discount**step / (heads * micro_total) for step in range(horizon)],
        jnp.float32,
    )
    value_delta, value_grads = value_backward(
        value_params,
        inputs,
        low_bins.reshape(-1),
        fractions.reshape(-1),
        jnp.repeat(step_weight, rows),
    )
    value_delta = value_delta.reshape(horizon, rows, -1)
    upstream = jnp.zeros((rows, latent_width), jnp.float32)
    embed_delta = jnp.sum(value_delta[:, :, latent_width + action_width :], 0)
    dynamics_grads = None
    for step in reversed(range(horizon)):
        factor = 2.0 * consistency_weight * discount**step / (micro_total * latent_width)
        upstream = upstream + factor * (latents[step + 1] - goals[step].astype(jnp.float32))
        inputs_delta, step_grads = dynamics_backward(dynamics_params, dynamics_kept[step], upstream)
        dynamics_grads = (
            step_grads
            if dynamics_grads is None
            else tuple(a + b for a, b in zip(dynamics_grads, step_grads))
        )
        embed_delta = embed_delta + inputs_delta[:, latent_width + action_width :]
        upstream = (
            inputs_delta[:, :latent_width].astype(jnp.bfloat16).astype(jnp.float32)
            + value_delta[step, :, :latent_width]
        )
    inputs_delta, encoder_grads = encoder_backward(encoder_params, encoder_kept, upstream)
    observed_delta = inputs_delta[:, :observed_width]
    embed_delta = embed_delta + inputs_delta[:, observed_width:]
    table_sum = left_transposed(onehot.astype(jnp.float32), embed_delta)
    totals = encoder_grads + dynamics_grads + value_grads
    matrices = reduce_end(totals)
    small_sums = lax.psum(
        tuple(totals[i] for i in (1, 2, 4, 5, 7, 8, 10, 11, 13, 14, 16, 17, 19, 20, 22))
        + (table_sum,),
        ("section", "dp"),
    )
    return (
        observed_delta.reshape(share, rows // share, observed_width),
        small_sums[15],
        matrices[0],
        small_sums[0],
        small_sums[1],
        matrices[1],
        small_sums[2],
        small_sums[3],
        matrices[2],
        small_sums[4],
        small_sums[5],
        matrices[3],
        small_sums[6],
        small_sums[7],
        matrices[4],
        small_sums[8],
        small_sums[9],
        matrices[5],
        small_sums[10],
        small_sums[11],
        matrices[6],
        small_sums[12],
        small_sums[13],
        matrices[7],
        small_sums[14],
    )


def step_device(
    observations,
    actions,
    action_mask,
    task_ids,
    targets,
    bin_low,
    bin_frac,
    task_table,
    encoder_first,
    encoder_first_gain,
    encoder_first_shift,
    encoder_second,
    encoder_second_gain,
    encoder_second_shift,
    dynamics_first,
    dynamics_first_gain,
    dynamics_first_shift,
    dynamics_second,
    dynamics_second_gain,
    dynamics_second_shift,
    dynamics_third,
    dynamics_third_gain,
    dynamics_third_shift,
    value_first,
    value_first_gain,
    value_first_shift,
    value_second,
    value_second_gain,
    value_second_shift,
    value_third,
    value_bias,
):
    horizon, micro_total, rows, moves = actions.shape
    tasks, task_width = task_table.shape
    heads, inputs, hidden = value_first.shape
    latent_width = dynamics_third.shape[1]
    observed = observations.shape[2]
    bins = value_third.shape[2]
    enc_rows = ceil_to(observed + task_width, 256)
    in_rows = latent_width + 128
    total = horizon * rows
    ranks = hidden // 128
    sizes = (micro_total, observed, moves, task_width, bins, heads)
    part_rows = (in_rows + 128) // 4
    rest_rows = hidden // (ranks * 4)
    enc_part = ceil_to(observed + task_width, 64) // 4
    chain = 1 + 2 * horizon
    pair = heads // 2
    vmem, anywhere = pl.BlockSpec(memory_space=pltpu.VMEM), pl.BlockSpec(memory_space=pl.ANY)
    names = len(ORDERS) + 3

    def gathered(count, blocks, block_rows, width):
        return (count, 2, 2, blocks, block_rows, width)

    shapes = (
        gathered(3, 1, rest_rows, hidden),
        gathered(pair, 2, rest_rows, hidden),
        gathered(2, 1, part_rows, 128),
        gathered(pair, 2, part_rows, 128),
        gathered(1, 1, enc_part, 128)[1:],
    )
    f32, bf16 = (lambda *shape: pltpu.VMEM(shape, F32)), (lambda *shape: pltpu.VMEM(shape, BF16))
    outs = pl.pallas_call(
        functools.partial(step_kernel, sizes),
        out_shape=tuple(jax.ShapeDtypeStruct(shape, BF16) for shape in shapes)
        + (
            jax.ShapeDtypeStruct((4, 8, hidden), F32),
            jax.ShapeDtypeStruct((4, 16, hidden), F32),
            jax.ShapeDtypeStruct((observed, rows), F32),
        ),
        in_specs=[vmem] * 22 + [anywhere] * 9,
        out_specs=[anywhere] * 5 + [vmem] * 3,
        scratch_shapes=[
            bf16(horizon, rows, latent_width),
            bf16(observed + task_width, hidden),
            bf16(enc_rows, hidden),
            bf16(hidden, latent_width),
            bf16(inputs, hidden),
            bf16(128, hidden),
            bf16(hidden, hidden),
            bf16(hidden, latent_width),
            bf16(inputs, hidden),
            bf16(128, hidden),
            bf16(hidden, hidden),
            bf16(bins, hidden),
            bf16(128, hidden),
            bf16(rows, enc_rows),
            bf16(2 * total, in_rows),
            bf16(total, in_rows),
            f32(enc_rows, rows),
            bf16(2, tasks, rows),
            f32(2 * total, 128),
            f32(8 * (heads + 1), hidden),
            bf16(chain, rows, hidden),
            bf16(chain, rows, hidden),
            f32(chain, rows, 128),
            bf16(chain * rows, hidden),
            bf16(horizon + 1, rows, latent_width),
            f32(horizon + 1, rows, latent_width),
            f32(horizon + 1, rows, 128),
            bf16(total, latent_width),
        ]
        + [bf16(total, hidden), bf16(total, hidden), f32(total, 128)]
        + [bf16(total, hidden)] * 4
        + [
            f32(rows, hidden),
            f32(rows, hidden),
            f32(total, hidden),
            f32(rows, latent_width),
            f32(2, 8, hidden),
            bf16(total, hidden),
            bf16(total, 128),
            f32(2 * total, in_rows),
            bf16(horizon, rows, latent_width),
            bf16(horizon, rows, latent_width),
            bf16(32, rest_rows, hidden),
            bf16(32, part_rows, 128),
            bf16(32, enc_part, 128),
            bf16(2, 16, rest_rows, hidden),
            bf16(16, part_rows, 128),
            bf16(16, enc_part, 128),
            [bf16(5, 8 >> k, rest_rows, hidden) for k in range(4)],
            [bf16(4, 8 >> k, part_rows, 128) for k in range(4)],
            [bf16(8 >> k, enc_part, 128) for k in range(4)],
            *(bf16(*shape) for shape in shapes),
            f32(4, 8, hidden),
            [f32(2, 8, hidden)] + [f32(8, hidden)] * 4,
            f32(4, 8, hidden),
            f32(4, 16, hidden),
            [f32(2, 16, hidden)] + [f32(16, hidden)] * 4,
            f32(4, 16, hidden),
            pltpu.SemaphoreType.DMA((5,)),
            pltpu.SemaphoreType.DMA((horizon,)),
            pltpu.SemaphoreType.DMA((3,)),
            pltpu.SemaphoreType.DMA((5,)),
            pltpu.SemaphoreType.DMA((names, 7)),
            pltpu.SemaphoreType.DMA((names, 7)),
            pltpu.SemaphoreType.REGULAR((5,)),
        ],
        compiler_params=pltpu.CompilerParams(
            collective_id=0, has_side_effects=True, vmem_limit_bytes=KERNEL_VMEM
        ),
    )(
        observations.transpose(2, 0, 1),
        actions.transpose(0, 3, 1, 2),
        task_ids,
        bin_low,
        bin_frac,
        action_mask.T,
        task_table,
        encoder_first_gain,
        encoder_first_shift,
        encoder_second_gain,
        encoder_second_shift,
        dynamics_first_gain,
        dynamics_first_shift,
        dynamics_second_gain,
        dynamics_second_shift,
        dynamics_third_gain,
        dynamics_third_shift,
        value_first_gain,
        value_first_shift,
        value_second_gain,
        value_second_shift,
        value_bias,
        targets,
        encoder_first,
        encoder_second,
        dynamics_first,
        dynamics_second,
        dynamics_third,
        value_first,
        value_second,
        value_third.transpose(0, 2, 1),
    )

    def like(*shape):
        return jax.ShapeDtypeStruct(shape, F32)

    done = pl.pallas_call(
        functools.partial(finish_kernel, sizes),
        out_shape=(
            like(observed, 1, rows),
            like(tasks, task_width),
            like(observed + task_width, 128),
            like(1, hidden),
            like(1, hidden),
            like(128, latent_width),
            like(1, latent_width),
            like(1, latent_width),
            like(inputs, 128),
            like(1, hidden),
            like(1, hidden),
            like(128, hidden),
            like(1, hidden),
            like(1, hidden),
            like(128, latent_width),
            like(1, latent_width),
            like(1, latent_width),
            like(heads, inputs, 128),
            like(heads, hidden),
            like(heads, hidden),
            like(heads, 128, hidden),
            like(heads, hidden),
            like(heads, hidden),
            like(heads, bins, 128),
            like(heads, bins),
        ),
        in_specs=[anywhere] * 8,
        out_specs=[vmem] * 25,
        scratch_shapes=[
            *(bf16(*shape) for shape in shapes),
            f32(4, 8, hidden),
            f32(4, 16, hidden),
            f32(observed, rows),
            pltpu.SemaphoreType.DMA((8,)),
        ],
        compiler_params=pltpu.CompilerParams(vmem_limit_bytes=FINISH_VMEM),
    )(*outs)
    done = [item.reshape(-1) if item.shape[0] == 1 else item for item in done]
    done[0] = done[0].transpose(1, 2, 0)
    done[23] = done[23].transpose(0, 2, 1)
    return tuple(done)


def solution(mesh):
    in_specs = (
        P(None, "dp", None),
        P(None, None, "dp", None),
        P(),
        P(None, "dp"),
        P(None, None, "dp", None),
        P(None, None, "dp"),
        P(None, None, "dp"),
    ) + (P(),) * 24
    out_specs = (
        P("section", "dp", None),
        P(),
        P(None, "dp"),
        P(),
        P(),
        P("dp", None),
        P(),
        P(),
        P(None, "dp"),
        P(),
        P(),
        P("dp", None),
        P(),
        P(),
        P("dp", None),
        P(),
        P(),
        P(None, None, "dp"),
        P(),
        P(),
        P(None, "dp", None),
        P(),
        P(),
        P(None, "dp", None),
        P(),
    )
    paired = (mesh.shape["section"], mesh.shape["dp"]) == (4, 8)
    return jax.shard_map(
        step_device if paired else plain_device,
        mesh=mesh,
        in_specs=in_specs,
        out_specs=out_specs,
        check_vma=False,
    )
```

```python
import functools

import jax
import jax.numpy as jnp
from jax import lax
from jax.experimental import pallas as pl
from jax.experimental.pallas import tpu as pltpu
from jax.sharding import PartitionSpec as P

SIMNORM = 8
epsilon = 1e-05
discount = 0.5
consistency_weight = 20.0
value_weight = 0.1

F32, BF16 = jnp.float32, jnp.bfloat16
WIDE_GROUP = 16
GROUP = 16
KERNEL_VMEM = 63 << 20
FINISH_VMEM = 63 << 20


def ceil_to(value, unit):
    return -(-value // unit) * unit


def row_sum(values):
    return jnp.sum(values, -1, keepdims=True)


def col_sum(values):
    return jnp.sum(values, 0, keepdims=True)


def dot(a, b):
    return lax.dot_general(a, b, (((1,), (0,)), ((), ())), preferred_element_type=F32)


def dot_left(a, b):
    return lax.dot_general(a, b, (((0,), (0,)), ((), ())), preferred_element_type=F32)


def dot_right(a, b):
    return lax.dot_general(a, b, (((1,), (1,)), ((), ())), preferred_element_type=F32)


def loop(count, body, unroll=1):
    def step(i, carry):
        body(i)
        return carry

    lax.fori_loop(0, count, step, 0, unroll=unroll)


def at(i, size):
    return pl.ds(pl.multiple_of(i * size, size), size)


def norm(values):
    scale = 1.0 / values.shape[1]
    center = values - row_sum(values) * scale
    rstd = lax.rsqrt(row_sum(center * center) * scale + epsilon)
    return center * rstd, rstd


def norm_back(grad, xhat, rstd):
    scale = 1.0 / grad.shape[1]
    mean_grad = row_sum(grad) * scale
    mean_both = row_sum(grad * xhat) * scale
    return rstd * (grad - mean_grad - xhat * mean_both)


def mish_forward(z, first, count, gain, shift, hidden, xhat_ref, slope, rstd_ref):
    for i in range(0, count, WIDE_GROUP):
        rows = pl.ds(first + i, WIDE_GROUP)
        xhat, rstd = norm(z[pl.ds(i, WIDE_GROUP), :])
        v = xhat * gain + shift
        e = jnp.exp(jnp.minimum(v, 30.0))
        n = e * (e + 2.0)
        r = pl.reciprocal(n + 2.0, approx=True)
        t = n * r
        xhat_ref[rows, :] = xhat.astype(xhat_ref.dtype)
        slope[rows, :] = (t + (4.0 * v) * ((e * r) * ((e + 1.0) * r))).astype(slope.dtype)
        rstd_ref[0][rows, rstd_ref[1] : rstd_ref[1] + 1] = rstd
        hidden[rows, :] = (v * t).astype(BF16)


def mish_backward(upstream, first, count, gain, xhat_ref, slope, rstd_ref, low, both_sums):
    width = upstream.shape[1]
    for i in range(0, count, GROUP):
        rows = pl.ds(first + i, GROUP)
        xhat = xhat_ref[rows, :].astype(F32)
        g = upstream[pl.ds(i, GROUP), :] * slope[rows, :]
        low[rows, :] = norm_back(g * gain, xhat, rstd_ref[0][rows, rstd_ref[1] : rstd_ref[1] + 1]).astype(BF16)
        both_sums[0] = both_sums[0] + (g * xhat).reshape(GROUP // 8, 8, width).sum(0)
        both_sums[1] = both_sums[1] + g.reshape(GROUP // 8, 8, width).sum(0)


def group_matrix(width):
    return (
        lax.broadcasted_iota(jnp.int32, (width, width), 0) // SIMNORM
        == lax.broadcasted_iota(jnp.int32, (width, width), 1) // SIMNORM
    ).astype(BF16)


def group_sums(values, groups):
    parts = []
    for k in range(values.shape[1] // 128):
        part = values[:, k * 128 : (k + 1) * 128]
        high = part.astype(BF16)
        rest = (part - high.astype(F32)).astype(BF16)
        parts.append(dot(high, groups) + dot(rest, groups))
    return jnp.concatenate(parts, 1)


def simnorm_forward(z, gain, shift, xhat_ref, chance, rstd_ref, groups):
    def body(i):
        xhat, rstd = norm(z[at(i, 32), :])
        e = jnp.exp(xhat * gain + shift)
        xhat_ref[at(i, 32), :] = xhat.astype(xhat_ref.dtype)
        chance[at(i, 32), :] = e / group_sums(e, groups)
        rstd_ref[0][at(i, 32), rstd_ref[1] : rstd_ref[1] + 1] = rstd

    loop(z.shape[0] // 32, body, 4)


def simnorm_backward(upstream, gain, xhat_ref, chance, rstd_ref, groups, low):
    width = gain.shape[1]

    def body(i, carry):
        gain_sum, shift_sum = carry
        xhat = xhat_ref[at(i, 32), :].astype(F32)
        p = chance[at(i, 32), :]
        w = upstream[at(i, 32), :] * p
        g = w - p * group_sums(w, groups)
        gx = g * xhat
        low[at(i, 32), :] = norm_back(g * gain, xhat, rstd_ref[0][at(i, 32), rstd_ref[1] : rstd_ref[1] + 1]).astype(BF16)
        return (
            gain_sum + gx.reshape(4, 8, width).sum(0),
            shift_sum + g.reshape(4, 8, width).sum(0),
        )

    zero = jnp.zeros((8, width), F32)
    gain_sum, shift_sum = lax.fori_loop(0, upstream.shape[0] // 32, body, (zero, zero), unroll=4)
    return col_sum(gain_sum), col_sum(shift_sum)


ORDERS = {
    "As": ("c", "z0", "y", "x", "z1"),
    "Bs": ("c", "x", "z0", "z1", "y"),
    "A0": ("c", "y", "z0", "z1"),
    "B0": ("c", "z0", "y", "z1"),
    "A1": ("c", "y", "z0", "z1"),
    "B1": ("c", "z0", "y", "z1"),
    "D2": ("c", "x", "y", "z0", "z1"),
    "F2": ("c", "y", "x", "z0", "z1"),
    "D1": ("c", "y", "z0", "z1", "x"),
    "G1": ("c", "z0", "y", "x", "z1"),
    "D3": ("c", "x", "y", "z0", "z1"),
    "E2": ("c", "z0", "y", "x", "z1"),
    "E1": ("c", "y", "z0", "x", "z1"),
}
SCHEDULE = {
    ("c", 0): [("L0", -1)],
    ("c", 1): [("L1", -1)],
    ("c", 2): [("L2", -1)],
    ("h", 0, 1): [("L0", 0), ("L1", 0)],
    ("h", 0, 4): [("As", -1), ("L2", 0)],
    ("h", 0, 7): [("Bs", -1), ("As", 0)],
    ("h", 1, 3): [("Bs", 0)],
    ("h", 2, 4): [("A0", -1), ("As", 1), ("Bs", 1)],
    ("h", 2, 7): [("Bs", 2), ("B0", -1), ("A0", 0)],
    ("h", 3, 1): [("As", 2)],
    ("h", 3, 2): [("B0", 0)],
    ("h", 3, 4): [("Bs", 3)],
    ("h", 3, 5): [("As", 3)],
    ("h", 4, 3): [("A0", 1), ("B0", 1), ("Bs", 4)],
    ("h", 4, 4): [("A1", -1), ("As", 4)],
    ("h", 4, 5): [("Bs", 5)],
    ("h", 4, 7): [("B0", 2), ("B1", -1), ("A1", 0), ("As", 5), ("Bs", 6), ("A0", 2)],
    ("t", 0): [("R2", -1), ("R1", -1), ("R0", -1), ("T", -1)],
    ("b", 0, 3): [("B1", 0), ("As", 6), ("T", 0), ("R2", 0)],
    ("b", 1, 1): [("B0", 3)],
    ("b", 1, 3): [("R1", 0)],
    ("b", 2, 3): [("R0", 0)],
    ("t", 10): [("D2", -1), ("F2", -1), ("A0", 3), ("T", 1), ("A1", 1)],
    ("t", 11): [("B1", 1), ("B1", 2), ("D1", -1), ("G1", -1), ("B0", 4), ("D2", 0), ("F2", 0), ("T", 2), ("A0", 4), ("A1", 2)],
    ("t", 12): [("D3", -1), ("D1", 0)],
    ("t", 13): [("G1", 0), ("B0", 5), ("A0", 5), ("T", 3), ("D3", 0), ("B1", 3)],
    ("t", 14): [("E2", -1)],
    ("t", 15): [("E1", -1), ("D2", 1)],
    ("t", 16): [("S", -1), ("F2", 1)],
    ("t", 17): [("E2", 0), ("E1", 0), ("A1", 3), ("S", 0), ("G1", 1), ("D1", 1), ("D3", 1), ("T", 4), ("D2", 2), ("B1", 4), ("E1", 1), ("B1", 5), ("F2", 2), ("E2", 1), ("G1", 2), ("D1", 2), ("A1", 4), ("D3", 2), ("S", 1), ("D2", 3), ("E1", 2), ("T", 5), ("A1", 5), ("G1", 3), ("E2", 2), ("F2", 3), ("S", 2), ("D1", 3), ("E1", 3), ("T", 6), ("D3", 3), ("D2", 4), ("G1", 4), ("E2", 3), ("D1", 4), ("F2", 4), ("S", 3), ("E1", 4), ("D2", 5), ("D3", 4), ("G1", 5), ("D1", 5), ("F2", 5), ("E2", 4), ("E1", 5), ("D2", 6), ("G1", 6), ("S", 4), ("D3", 5), ("D1", 6), ("F2", 6), ("E1", 6), ("E2", 5), ("D3", 6), ("S", 5), ("E2", 6), ("S", 6)],
}


class Piece:
    def __init__(self, index, order, buffers, gathered, credit=None, gives=False):
        self.index, self.order, self.buffers, self.gathered = index, order, buffers, gathered
        self.credit, self.gives = credit, gives
        self.stages = len(order) + 2


class Exchange:
    def __init__(self, send_sem, recv_sem, free_sem):
        self.send_sem, self.recv_sem, self.free_sem = send_sem, recv_sem, free_sem
        section, dp = lax.axis_index("section"), lax.axis_index("dp")
        self.bit = {
            "c": section % 2,
            "x": section // 2,
            "y": dp % 2,
            "z0": (dp // 2) % 2,
            "z1": dp // 4,
        }
        self.partner = {
            "c": {"section": section + 1 - 2 * self.bit["c"]},
            "x": {"section": section + 2 - 4 * self.bit["x"]},
            "y": {"dp": dp + 1 - 2 * self.bit["y"]},
            "z0": {"dp": dp + 2 - 4 * self.bit["z0"]},
            "z1": {"dp": dp + 4 - 8 * self.bit["z1"]},
        }

    def greet(self):
        barrier = pltpu.get_barrier_semaphore()
        for axis in self.partner:
            self.signal(barrier, axis)
        pl.semaphore_wait(barrier, len(self.partner))

    def signal(self, sem, axis):
        pl.semaphore_signal(
            sem, inc=1, device_id=self.partner[axis], device_id_type=pl.DeviceIdType.MESH
        )

    def remote(self, source, target, index, stage, axis):
        return pltpu.make_async_remote_copy(
            src_ref=source,
            dst_ref=target,
            send_sem=self.send_sem.at[index, stage],
            recv_sem=self.recv_sem.at[index, stage],
            device_id=self.partner[axis],
            device_id_type=pl.DeviceIdType.MESH,
        )

    def place(self, order, rank, quarter):
        bits = {
            "c": quarter // 2,
            "x": quarter % 2,
            "y": rank % 2,
            "z0": (rank // 2) % 2,
            "z1": rank // 4,
        }
        index = 0
        for axis in order if len(order) == 5 else order + ("x",):
            index = index * 2 + bits[axis]
        return index

    def copy(self, piece, stage):
        c, x = self.bit["c"], self.bit["x"]
        count = len(piece.order)
        if stage < count:
            axis = piece.order[stage]
            half = 32 >> (stage + 1)
            source = piece.buffers[stage].at[pl.ds((1 - self.bit[axis]) * half, half)]
            target = piece.buffers[stage + 1]
        elif stage == count:
            axis = "x"
            source = target = piece.gathered.at[c, x]
        else:
            axis = "c"
            source = target = piece.gathered.at[c]
        return self.remote(source, target, piece.index, stage, axis)

    def begin(self, piece):
        if piece.credit is not None:
            pl.semaphore_wait(self.free_sem.at[piece.credit], 1)
        self.copy(piece, 0).start()

    def advance(self, piece, stage):
        last = stage + 1 == piece.stages
        self.copy(piece, stage).wait_recv()
        if stage == 0 or last:
            self.copy(piece, stage).wait_send()
        if stage > 1:
            self.copy(piece, stage - 1).wait_send()
        if stage == 2 and piece.gives is not False:
            self.signal(self.free_sem.at[piece.gives], "c")
        count = len(piece.order)
        if stage < count:
            half = 32 >> (stage + 1)
            first = self.bit[piece.order[stage]] * half
            kept, total = piece.buffers[stage], piece.buffers[stage + 1]
            if stage < count - 1:

                def add(i):
                    total[i] = total[i] + kept[first + i]

                loop(half, add, min(half, 8))
            else:
                for i in range(half):
                    piece.gathered[self.bit["c"], self.bit["x"], i] = total[i] + kept[first + i]
        if not last:
            self.copy(piece, stage + 1).start()


class Sums:
    def __init__(self, index, parts, gathered, exchange):
        self.index, self.parts, self.gathered, self.exchange = index, parts, gathered, exchange
        self.stages = 7

    def copy(self, stage):
        parts = self.parts
        c, x = self.exchange.bit["c"], self.exchange.bit["x"]
        if stage == 0:
            axis, source, target = "c", parts[0].at[pl.ds((1 - c) * 2, 2)], parts[1]
        elif stage == 1:
            axis, source, target = "x", parts[1].at[1 - x], parts[2]
        elif stage < 5:
            axis, source, target = ("y", "z0", "z1")[stage - 2], parts[stage], parts[stage + 1]
        elif stage == 5:
            axis = "x"
            source = target = self.gathered.at[c * 2 + x]
        else:
            axis = "c"
            source = target = self.gathered.at[pl.ds(c * 2, 2)]
        return self.exchange.remote(source, target, self.index, stage, axis)

    def begin(self):
        self.copy(0).start()

    def advance(self, stage):
        parts = self.parts
        c, x = self.exchange.bit["c"], self.exchange.bit["x"]
        self.copy(stage).wait()
        if stage == 0:
            parts[1][...] = parts[1][...] + parts[0][pl.ds(c * 2, 2)]
        elif stage == 1:
            parts[2][...] = parts[2][...] + parts[1][x]
        elif stage < 4:
            parts[stage + 1][...] = parts[stage + 1][...] + parts[stage][...]
        elif stage == 4:
            self.gathered[c * 2 + x] = parts[5][...] + parts[4][...]
        if stage + 1 < self.stages:
            self.copy(stage + 1).start()


def step_kernel(
    sizes,
    obs_ref,
    act_ref,
    ids_ref,
    low_ref,
    frac_ref,
    mask_ref,
    task_ref,
    enc_one_gain,
    enc_one_shift,
    enc_two_gain,
    enc_two_shift,
    dyn_one_gain,
    dyn_one_shift,
    dyn_two_gain,
    dyn_two_shift,
    dyn_three_gain,
    dyn_three_shift,
    value_one_gain,
    value_one_shift,
    value_two_gain,
    value_two_shift,
    value_bias,
    goals_ref,
    we1_ref,
    we2_ref,
    wd1_ref,
    wd2_ref,
    wd3_ref,
    wv1_ref,
    wv2_ref,
    wv3_ref,
    ga_ref,
    ga_pair_ref,
    gb_ref,
    gb_pair_ref,
    ge_ref,
    small_ref,
    heads_ref,
    obs_grad_ref,
    goals,
    we1_raw,
    we1,
    we2,
    wd1,
    wd1_rest,
    wd2,
    wd3,
    wv1,
    wv1_rest,
    wv2,
    wv3_raw,
    wv3,
    x_enc,
    x_all,
    x_now,
    turned,
    onehot,
    target,
    param_ref,
    z_chain,
    slope_chain,
    rstd_chain,
    hid_chain,
    z_lat,
    lat,
    rstd_lat,
    dz_lat,
    z1,
    s1,
    r_both,
    h1,
    z2,
    s2,
    h2,
    up_a,
    up_b,
    up,
    carry,
    both_sums,
    dz,
    dlog,
    dx,
    lat_in,
    dx_in,
    pa,
    pb,
    pe,
    half_a,
    half_b,
    half_e,
    last_a,
    last_b,
    last_e,
    all_a,
    all_a_pair,
    all_b,
    all_b_pair,
    all_e,
    small,
    small_parts,
    small_all,
    heads_small,
    heads_parts,
    heads_all,
    chain_sem,
    goal_sem,
    value_sem,
    out_sem,
    send_sem,
    recv_sem,
    free_sem,
):
    micro_total, observed, moves, task_width, bins, heads = sizes
    horizon, _, rows, latent_width = goals_ref.shape
    tasks = task_ref.shape[0]
    hidden = wv2_ref.shape[1]
    inputs = wv1_ref.shape[1]
    rest = inputs - latent_width
    total = horizon * rows
    ranks = hidden // 128
    part_rows, rest_rows = pb.shape[1], pa.shape[1]
    section = lax.axis_index("section")
    exchange = Exchange(send_sem, recv_sem, free_sem)
    x_bit = exchange.bit["x"]
    micros = (section, section + 2 - 4 * x_bit)
    own_heads = heads // 2
    shared = heads - 1

    pieces = {}

    def piece(name, own, half, last, gathered, credit=None, gives=False):
        order = ORDERS[name]
        buffers = [own, half] + last
        pieces[name] = Piece(len(pieces), order, buffers, gathered, credit, gives)

    def lasts(refs, k, lanes=None):
        views = [ref.at[k] for ref in refs]
        return views if lanes is None else [view.at[:, :, lanes] for view in views]

    left, right = pl.ds(0, latent_width), pl.ds(latent_width, latent_width)
    piece("As", pa, half_a.at[0], lasts(last_a, 0), all_a.at[0], None, 0)
    piece("A0", pa, half_a.at[1], lasts(last_a, 1), all_a_pair.at[0], None, 1)
    whole = slice(None)
    for name, lanes, k, slot, final, credit, gives in (
        ("A1", left if "C1" in ORDERS else whole, 2, 0, all_a_pair.at[1], 0, 0),
        ("C1", right, 2, 0, all_a_pair.at[1], None, 2),
        ("D2", left if "F2" in ORDERS else whole, 3, 1, all_a.at[1], 1, False),
        ("F2", right, 3, 1, all_a.at[1], None, False),
        ("D3", left, 4, 0, all_a.at[2], 0, False),
        ("E2", right, 4, 0, all_a.at[2], 2 if "C1" in ORDERS else None, False),
    ):
        if name in ORDERS:
            piece(
                name,
                pa.at[:, :, lanes],
                half_a.at[slot, :, :, lanes],
                lasts(last_a, k, lanes),
                final.at[:, :, :, :, lanes],
                credit,
                gives,
            )
    piece("Bs", pb, half_b, lasts(last_b, 0), all_b.at[0], None, 4)
    piece("B0", pb, half_b, lasts(last_b, 1), all_b_pair.at[0], 4, 4)
    half_rows = part_rows // 2
    first_half, second_half = pl.ds(0, half_rows), pl.ds(half_rows, half_rows)
    for name, those, k, final, credit, gives in (
        ("B1", first_half if "H1" in ORDERS else whole, 2, all_b_pair.at[1], 4, 4),
        ("H1", second_half, 2, all_b_pair.at[1], None, 3),
        ("D1", first_half if "G1" in ORDERS else whole, 3, all_b.at[1], 4, False),
        ("G1", second_half, 3, all_b.at[1], 3 if "H1" in ORDERS else None, False),
    ):
        if name in ORDERS:
            piece(
                name,
                pb.at[:, those],
                half_b.at[:, those],
                [ref.at[k, :, those] for ref in last_b],
                final.at[:, :, :, those],
                credit,
                gives,
            )
    piece("E1", pe, half_e, list(last_e), all_e)
    sums = {
        "S": Sums(len(pieces), [small, *small_parts], small_all, exchange),
        "T": Sums(len(pieces) + 1, [heads_small, *heads_parts], heads_all, exchange),
    }
    swaps = len(pieces) + 2

    def swap(name):
        t = int(name[1])
        if name[0] == "L":
            source, target_ref, stage = x_all.at[pl.ds(t * rows, rows), pl.ds(0, latent_width)], lat_in.at[t], t
        else:
            source, target_ref, stage = lat_in.at[t], dx_in.at[t], horizon + t
        return exchange.remote(source, target_ref, swaps, stage, "x")

    def act(name, stage):
        if name[0] in "LR":
            if stage < 0:
                swap(name).start()
            else:
                swap(name).wait()
        elif name in sums:
            if stage < 0:
                sums[name].begin()
            else:
                sums[name].advance(stage)
        elif stage < 0:
            exchange.begin(pieces[name])
        else:
            exchange.advance(pieces[name], stage)

    def tick(*key):
        for name, stage in SCHEDULE.get(key, ()):
            act(name, stage)

    def loop_tick(group, index, point=None):
        for key in SCHEDULE:
            if key[0] == group and key[2:] == (() if point is None else (point,)):
                pl.when(index == key[1])(functools.partial(tick, *key))

    def chain_copies():
        return [
            pltpu.make_async_copy(source, place, chain_sem.at[k])
            for k, (source, place) in enumerate(
                (
                    (we1_ref, we1_raw),
                    (we2_ref, we2),
                    (wd1_ref, wd1),
                    (wd2_ref, wd2),
                    (wd3_ref, wd3),
                )
            )
        ]

    def value_copy(q, index):
        source, place = ((wv1_ref, wv1), (wv2_ref, wv2), (wv3_ref, wv3_raw))[index]
        return pltpu.make_async_copy(source.at[q], place, value_sem.at[index])

    for copy in chain_copies():
        copy.start()
    goal_copies = [
        pltpu.make_async_copy(goals_ref.at[t, section], goals.at[t], goal_sem.at[t]) for t in range(horizon)
    ]
    for copy in goal_copies:
        copy.start()

    small[...] = jnp.zeros_like(small)
    heads_small[...] = jnp.zeros_like(heads_small)
    dx[...] = jnp.zeros_like(dx)
    param_ref[...] = jnp.zeros_like(param_ref)
    we1[...] = jnp.zeros_like(we1)
    wd1_rest[...] = jnp.zeros_like(wd1_rest)
    wv1_rest[...] = jnp.zeros_like(wv1_rest)
    wv3[...] = jnp.zeros_like(wv3)
    turned[...] = jnp.zeros_like(turned)
    groups = group_matrix(128)

    def pick(ref, micro):
        out = jnp.zeros((1, rows), ref.dtype)
        for m in range(micro_total):
            out = out + jnp.where(micro == m, ref[m : m + 1, :], jnp.zeros((1, rows), ref.dtype))
        return out

    def line(ref):
        return ref[...].astype(F32).reshape(1, ref.shape[0])

    for index, vector in enumerate(
        (
            line(enc_one_gain),
            line(enc_one_shift),
            jnp.concatenate([line(enc_two_gain), line(enc_two_shift)], 1),
            line(dyn_one_gain),
            line(dyn_one_shift),
            line(dyn_two_gain),
            line(dyn_two_shift),
            jnp.concatenate([line(dyn_three_gain), line(dyn_three_shift)], 1),
        )
    ):
        param_ref[index : index + 1, :] = vector
    for index, ref in enumerate((value_one_gain, value_one_shift, value_two_gain, value_two_shift, value_bias)):
        for q in range(heads):
            at_row = 8 * (q + 1) + index
            param_ref[at_row : at_row + 1, : ref.shape[1]] = ref[q : q + 1, :].astype(F32)

    def pick_micro(values, micro):
        out = None
        for m in range(micro_total):
            part = jnp.where(micro == m, values[..., m, :], 0.0)
            out = part if out is None else out + part
        return out

    mask = mask_ref[...].astype(F32).astype(BF16)
    all_obs, all_act = obs_ref[...].astype(F32), act_ref[...].astype(F32)
    for j, micro in enumerate(micros):
        hot = (lax.broadcasted_iota(jnp.int32, (tasks, rows), 0) == pick(ids_ref, micro)).astype(BF16)
        onehot[j] = hot
        embedded = dot_left(task_ref[...], hot)
        allowed = dot(mask, hot)
        acts = pick_micro(all_act, micro)
        turned[moves:rest, :] = embedded
        for t in range(horizon):
            turned[0:moves, :] = acts[t] * allowed
            at_rows = slice((j * horizon + t) * rows, (j * horizon + t + 1) * rows)
            x_all[at_rows, latent_width:] = turned[:128, :].T.astype(BF16)
            bin_at = lax.broadcasted_iota(jnp.int32, (128, rows), 0)
            lower, upper_part = pick(low_ref.at[t], micro), pick(frac_ref.at[t], micro)
            target[at_rows, :] = (
                jnp.where(bin_at == lower, 1.0 - upper_part, 0.0) + jnp.where(bin_at == lower + 1, upper_part, 0.0)
            ).T
        if j == 0:
            turned[0:observed, :] = pick_micro(all_obs, micro)
            turned[observed : observed + task_width, :] = embedded
            x_enc[:, :128] = turned[:128, :].T.astype(BF16)
            x_enc[:, 128:] = turned[128:, :].T.astype(BF16)
            turned[...] = jnp.zeros_like(turned)

    def vec(index):
        return param_ref[index : index + 1, :]

    ups = (up_a, up_b)
    wide_up = up_a.at[pl.ds(0, rows), :]
    carry_up = up_a.at[pl.ds(0, rows), pl.ds(0, latent_width)]
    lat_up = up_b.at[pl.ds(0, rows), pl.ds(0, latent_width)]

    def in_blocks(count, product, after):
        size = up_a.shape[0] if count % up_a.shape[0] == 0 else rows
        blocks = [pl.ds(k * size, size) for k in range(count // size)]
        ups[0][:size, :] = product(blocks[0])
        for k, block in enumerate(blocks):
            if k + 1 < len(blocks):
                ups[(k + 1) % 2][:size, :] = product(blocks[k + 1])
            after(ups[k % 2], k * size, size)

    def forward_blocks(count, product, gain, shift, hidden_ref, xhat_ref, slope, rstd_ref):
        def after(z, first, size):
            mish_forward(z, first, size, gain, shift, hidden_ref, xhat_ref, slope, rstd_ref)

        in_blocks(count, product, after)

    def backward_blocks(count, product, gain, xhat_ref, slope, rstd_ref, low):
        both_sums[...] = jnp.zeros_like(both_sums)

        def after(upstream, first, size):
            mish_backward(upstream, first, size, gain, xhat_ref, slope, rstd_ref, low, both_sums)

        in_blocks(count, product, after)
        return col_sum(both_sums[0]), col_sum(both_sums[1])


    def mish_layer(product, index, slot):
        forward_blocks(
            rows,
            product,
            vec(index),
            vec(index + 1),
            hid_chain.at[at(slot, rows), :],
            z_chain.at[slot],
            slope_chain.at[slot],
            (rstd_chain.at[slot], 0),
        )

    def latent_layer(weight, hidden_slot, index, slot):
        carry_up[...] = dot(hid_chain[at(hidden_slot, rows), :], weight[...])
        simnorm_forward(
            carry_up,
            vec(index)[:, :latent_width],
            vec(index)[:, latent_width:],
            z_lat.at[slot],
            lat.at[slot],
            (rstd_lat.at[slot], 0),
            groups,
        )

    copies = chain_copies()
    copies[0].wait()
    we1[: observed + task_width, :] = we1_raw[...]
    mish_layer(lambda block: dot(x_enc[block, :], we1[...]), 0, 0)
    copies[1].wait()
    latent_layer(we2, 0, 2, 0)
    copies[2].wait()
    copies[3].wait()
    copies[4].wait()
    for index in range(3):
        value_copy(shared, index).start()
    wd1_rest[:rest, :] = wd1[latent_width:, :]
    exchange.greet()
    def dynamics_step(t):
        own = at(t, rows)
        x_all[own, :latent_width] = lat[t].astype(BF16)
        loop_tick("c", t)
        mish_layer(
            lambda block: dot(x_all[own, :latent_width], wd1[:latent_width, :])
            + dot(x_all[own, latent_width:], wd1_rest[...]),
            3,
            1 + t,
        )
        mish_layer(lambda block: dot(hid_chain[at(1 + t, rows), :], wd2[...]), 5, 1 + horizon + t)
        latent_layer(wd3, 1 + horizon + t, 7, t + 1)

    loop(horizon, dynamics_step)

    def placed(name):
        return lambda rank, quarter: exchange.place(ORDERS[name], rank, quarter)

    def put_rows(place_of, own, rank, block, lanes=slice(None), more=None):
        low = block.astype(BF16)
        for k in range(low.shape[0] // rest_rows):
            place = place_of(rank + k // 4, k % 4)
            part = low[k * rest_rows : (k + 1) * rest_rows]
            own[place, :, lanes] = part if more is None else jnp.where(more, part + own[place, :, lanes], part)

    def put_lanes(places, own, rank, block, begin=0, more=None):
        low = block.astype(BF16)
        quarter_rows = own.shape[1]
        part_size = quarter_rows // len(places)
        for k in range(low.shape[1] // 128):
            done = 0
            while done < low.shape[0]:
                quarter, offset = divmod(begin + done, quarter_rows)
                which, inside = divmod(offset, part_size)
                count = min(part_size - inside, low.shape[0] - done)
                place = places[which](rank + k, quarter)
                part = low[done : done + count, k * 128 : (k + 1) * 128]
                own[place, offset : offset + count, :] = (
                    part if more is None else jnp.where(more, part + own[place, offset : offset + count, :], part)
                )
                done += count

    def head_pass(j):
        fifth = 1 - (j + 2 * own_heads) // (2 * own_heads + 1)
        q = fifth * shared + (1 - fifth) * (x_bit * own_heads + (j - 1) // 2)
        others = (1 - fifth) * (1 - j % 2)

        def mixed(first_name, other_name):
            def place_of(rank, quarter):
                first = exchange.place(ORDERS[first_name], rank, quarter)
                other = exchange.place(ORDERS[other_name], rank, quarter)
                return other + fifth * (first - other)

            return place_of

        more = others == 1
        block = param_ref[pl.ds(pl.multiple_of(8 * (q + 1), 8), 8), :]
        first_gain, first_shift, second_gain, second_shift, bias = (block[k : k + 1, :] for k in range(5))
        offset = others * total

        def arrived(index):
            pl.when(others == 0)(lambda: value_copy(q, index).wait())

        def prefetch(index):
            nxt = x_bit * own_heads + j // 2
            pl.when((j % 2 == 0) & (j < 2 * own_heads))(lambda: value_copy(nxt, index).start())

        @pl.when(j == 2)
        def _():
            for t in range(horizon):
                x_all[total + t * rows : total + (t + 1) * rows, :latent_width] = lat_in[t]

        x_now[...] = x_all[pl.ds(pl.multiple_of(offset, total), total), :]
        arrived(0)

        @pl.when(others == 0)
        def _():
            wv1_rest[:rest, :] = wv1[latent_width:, :]

        forward_blocks(
            total,
            lambda block: dot(x_now[block, :latent_width], wv1[:latent_width, :])
            + dot(x_now[block, latent_width:], wv1_rest[...]),
            first_gain,
            first_shift,
            h1,
            z1,
            s1,
            (r_both, 0),
        )
        loop_tick("h", j, 1)
        arrived(1)
        forward_blocks(total, lambda block: dot(h1[block, :], wv2[...]), second_gain, second_shift, h2, z2, s2, (r_both, 1))
        loop_tick("h", j, 2)
        arrived(2)

        @pl.when(others == 0)
        def _():
            wv3[:bins, :] = wv3_raw[...]

        prefetch(2)
        valid = lax.broadcasted_iota(jnp.int32, (1, 128), 1) < bins
        bias_sum = jnp.zeros((1, 128), F32)
        for t in range(horizon):
            factor = value_weight * discount**t / (heads * micro_total)
            own = slice(t * rows, (t + 1) * rows)
            logits = jnp.where(valid, dot_right(h2[own, :], wv3[...]) + bias[:, :128], -1e30)
            e = jnp.exp(logits - jnp.max(logits, -1, keepdims=True))
            goal = target[pl.ds(pl.multiple_of(offset + t * rows, rows), rows), :]
            delta = factor * (e / row_sum(e) - goal)
            dlog[own, :] = delta.astype(BF16)
            bias_sum = bias_sum + col_sum(delta)
        second_sums = backward_blocks(
            total, lambda block: dot(dlog[block, :], wv3[...]), second_gain, z2, s2, (r_both, 1), dz
        )
        loop_tick("h", j, 3)
        for part in range(2):
            columns = pl.ds(part * (hidden // 2), hidden // 2)
            product = dot_left(h1[:, columns], dz[...])
            put_rows(mixed("As", "A0"), pa, part * (ranks // 2), product, slice(None), more)
        loop_tick("h", j, 4)
        both_sums[...] = jnp.zeros_like(both_sums)
        up[...] = dot_right(dz[...], wv2[...])
        mish_backward(up, 0, total, first_gain, z1, s1, (r_both, 0), dz, both_sums)
        prefetch(1)
        loop_tick("h", j, 5)
        here = pl.ds(pl.multiple_of(offset, total), total)
        dx[here, :latent_width] = dx[here, :latent_width] + dot_right(dz[...], wv1[:latent_width, :])
        dx[here, latent_width:] = dx[here, latent_width:] + dot_right(dz[...], wv1_rest[...])
        prefetch(0)
        loop_tick("h", j, 6)
        for part in range(2):
            columns = pl.ds(part * (hidden // 2), hidden // 2)
            put_lanes([mixed("Bs", "B0")], pb, part * (ranks // 2), dot_left(x_now[...], dz[:, columns]), 0, more)
        put_lanes([mixed("Bs", "B0")], pb, 0, dot_left(dlog[...], h2[...]), latent_width + 128, more)
        pad = jnp.zeros((1, hidden - 128), F32)
        place = pl.ds(pl.multiple_of(q % 2 * 8, 8), 8)
        heads_small[q // 2, place, :] = heads_small[q // 2, place, :] + jnp.concatenate(
            [
                col_sum(both_sums[0]),
                col_sum(both_sums[1]),
                *second_sums,
                jnp.concatenate([bias_sum, pad], 1),
                jnp.zeros((3, hidden), F32),
            ],
            0,
        )
        loop_tick("h", j, 7)

    loop(1 + 2 * own_heads, head_pass)

    for t in range(horizon):
        lat_in[t] = dx[total + t * rows : total + (t + 1) * rows, :latent_width].astype(BF16)
    tick("t", 0)
    for copy in goal_copies:
        copy.wait()
    embed_sums = []
    for j in range(2):
        parts = [dx[(j * horizon + t) * rows : (j * horizon + t + 1) * rows, latent_width:] for t in range(horizon)]
        embed_sums.append(sum(parts[1:], parts[0]))
    dz_one, dz_two = h1, dz
    gain_lat = vec(7)[:, :latent_width]
    carry[...] = jnp.zeros_like(carry)

    def step_backward(i, sums):
        t = horizon - 1 - i
        factor = 0.0
        for k in range(horizon):
            factor = jnp.where(t == k, 2.0 * consistency_weight * discount**k / (micro_total * latent_width), factor)
        lat_up[...] = factor * (lat[t + 1] - goals[t].astype(F32)) + carry[...]
        own = at(t, rows)
        one, two = 1 + t, 1 + horizon + t
        lat_sums = simnorm_backward(
            lat_up, gain_lat, z_lat.at[t + 1], lat.at[t + 1], (rstd_lat.at[t + 1], 0), groups, dz_lat.at[own, :]
        )
        two_sums = backward_blocks(
            rows,
            lambda block: dot_right(dz_lat[own, :], wd3[...]),
            vec(5),
            z_chain.at[two],
            slope_chain.at[two],
            (rstd_chain.at[two], 0),
            dz_two.at[own, :],
        )
        loop_tick("b", i, 1)
        one_sums = backward_blocks(
            rows,
            lambda block: dot_right(dz_two[own, :], wd2[...]),
            vec(3),
            z_chain.at[one],
            slope_chain.at[one],
            (rstd_chain.at[one], 0),
            dz_one.at[own, :],
        )
        loop_tick("b", i, 2)
        latent_delta = dot_right(dz_one[own, :], wd1[:latent_width, :])
        rest_delta = dot_right(dz_one[own, :], wd1_rest[...])
        loop_tick("b", i, 3)
        carry[...] = latent_delta.astype(BF16).astype(F32) + dx[own, :latent_width] + dx_in[t].astype(F32)
        return tuple(a + b for a, b in zip(sums, (rest_delta, *one_sums, *two_sums, *lat_sums)))

    zero, zero_lat = jnp.zeros((1, hidden), F32), jnp.zeros((1, latent_width), F32)
    totals = lax.fori_loop(
        0, horizon, step_backward, (embed_sums[0], zero, zero, zero, zero, zero_lat, zero_lat)
    )
    embed_sums[0] = totals[0]
    small[0, 3:8, :] = jnp.concatenate([*totals[1:5], jnp.concatenate(totals[5:], 1)], 0)

    def put_chain(name, grad, first, lanes=slice(None), second_name=None):
        for part in range(2):
            columns = pl.ds(part * (hidden // 2), hidden // 2)
            block = dot_left(hid_chain[first * rows : (first + horizon) * rows, columns], grad[...])
            if second_name is None:
                put_rows(placed(name), pa, part * (ranks // 2), block, lanes)
            else:
                put_rows(placed(name), pa, part * (ranks // 2), block[:, :latent_width], slice(0, latent_width))
                put_rows(
                    placed(second_name),
                    pa,
                    part * (ranks // 2),
                    block[:, latent_width:],
                    slice(latent_width, 2 * latent_width),
                )

    put_chain("D2", dz_two, 1, second_name="F2" if "F2" in ORDERS else None)
    tick("t", 10)
    for part in range(2):
        columns = pl.ds(part * (hidden // 2), hidden // 2)
        put_lanes([placed(name) for name in ("D1", "G1") if name in ORDERS], pb, part * (ranks // 2), dot_left(x_all[:total, :], dz_one[:, columns]))
    tick("t", 11)
    put_chain("D3", dz_lat, 1 + horizon, slice(0, latent_width))
    tick("t", 12)

    lat_up[...] = carry[...]
    low_lat = dz_lat.at[pl.ds(0, rows), :]
    encoder_lat = simnorm_backward(
        lat_up, vec(2)[:, :latent_width], z_lat.at[0], lat.at[0], (rstd_lat.at[0], 0), groups, low_lat
    )
    low_one = dz_one.at[pl.ds(0, rows), :]
    encoder_one = backward_blocks(
        rows,
        lambda block: dot_right(low_lat[...], we2[...]),
        vec(0),
        z_chain.at[0],
        slope_chain.at[0],
        (rstd_chain.at[0], 0),
        low_one,
    )
    small[0, 0:3, :] = jnp.concatenate([*encoder_one, jnp.concatenate(encoder_lat, 1)], 0)
    tick("t", 13)
    put_rows(
        placed("E2"), pa, 0, dot_left(hid_chain[:rows, :], low_lat[...]), slice(latent_width, 2 * latent_width)
    )
    tick("t", 14)
    put_lanes([placed("E1")], pe, 0, dot_left(x_enc[...], low_one[...])[: 4 * pe.shape[1]])
    tick("t", 15)
    enc_up = dot_right(low_one[...], we1[...])
    obs_grad_ref[...] = enc_up[:, :128].T[:observed, :]
    embed_sums[0] = embed_sums[0] + pltpu.roll(enc_up, x_enc.shape[1] - observed + moves, 1)[:, :128]
    table = None
    for j in range(2):
        high = embed_sums[j].astype(BF16)
        low = (embed_sums[j] - high.astype(F32)).astype(BF16)
        part = dot(onehot[j], high) + dot(onehot[j], low)
        table = part if table is None else table + part
    for k in range(tasks // 8):
        small[1 + k // 8, :, (k % 8) * 128 : (k % 8) * 128 + 128] = table[k * 8 : k * 8 + 8]
    tick("t", 16)
    outs = [
        pltpu.make_async_copy(source, place, out_sem.at[k])
        for k, (source, place) in enumerate(
            (
                (all_a, ga_ref),
                (all_a_pair, ga_pair_ref),
                (all_b, gb_ref),
                (all_b_pair, gb_pair_ref),
                (all_e, ge_ref),
            )
        )
    ]
    rest_steps = SCHEDULE[("t", 17)]
    members = (("As", "D2", "F2", "D3", "E2"), ("A0", "A1", "C1"), ("Bs", "D1", "G1"), ("B0", "B1", "H1"), ("E1",))
    done_at = [-1] * len(members)
    for index, (name, stage) in enumerate(rest_steps):
        for group, names in enumerate(members):
            if name in names and stage + 1 == pieces[name].stages:
                done_at[group] = index
    for group, index in enumerate(done_at):
        if index < 0:
            outs[group].start()
    for index, (name, stage) in enumerate(rest_steps):
        act(name, stage)
        for group, last in enumerate(done_at):
            if last == index:
                outs[group].start()
    small_ref[...] = small_all[...]
    heads_ref[...] = heads_all[...]
    for copy in outs:
        copy.wait()


def finish_kernel(
    sizes,
    ga_from,
    ga_pair_from,
    gb_from,
    gb_pair_from,
    ge_from,
    small_from,
    heads_from,
    obs_from,
    obs_out,
    table_ref,
    encoder_first,
    encoder_first_gain,
    encoder_first_shift,
    encoder_second,
    encoder_second_gain,
    encoder_second_shift,
    dynamics_first,
    dynamics_first_gain,
    dynamics_first_shift,
    dynamics_second,
    dynamics_second_gain,
    dynamics_second_shift,
    dynamics_third,
    dynamics_third_gain,
    dynamics_third_shift,
    value_first,
    value_first_gain,
    value_first_shift,
    value_second,
    value_second_gain,
    value_second_shift,
    value_third,
    value_bias,
    ga_ref,
    ga_pair_ref,
    gb_ref,
    gb_pair_ref,
    ge_ref,
    small_ref,
    heads_ref,
    obs_ref,
    sem,
):
    copies = [
        pltpu.make_async_copy(source, place, sem.at[k])
        for k, (source, place) in enumerate(
            (
                (ga_from, ga_ref),
                (ga_pair_from, ga_pair_ref),
                (gb_from, gb_ref),
                (gb_pair_from, gb_pair_ref),
                (ge_from, ge_ref),
                (small_from, small_ref),
                (heads_from, heads_ref),
                (obs_from, obs_ref),
            )
        )
    ]
    for copy in copies:
        copy.start()
    for copy in copies[5:]:
        copy.wait()
    _, _, moves, task_width, bins, heads = sizes
    rest_rows, part_rows = ga_ref.shape[4], gb_ref.shape[4]
    obs_out[:, 0, :] = obs_ref[...]
    inputs = dynamics_first.shape[0]
    latent_width = dynamics_third.shape[1]
    encoder_rows = encoder_first.shape[0]
    third_at = 4 * part_rows - 128
    own_heads = heads // 2

    def move(target, first_row, block):
        count = min(target.shape[0] - first_row, block.shape[0])
        if count > 0:
            target[first_row : first_row + count, :] = block[:count].astype(F32)

    def row(index):
        return small_ref[0, index : index + 1, :]

    def head_row(q, k):
        return heads_ref[q // 2, q % 2 * 8 + k : q % 2 * 8 + k + 1, :]

    encoder_first_gain[...] = row(0)
    encoder_first_shift[...] = row(1)
    encoder_second_gain[...] = row(2)[:, :latent_width]
    encoder_second_shift[...] = row(2)[:, latent_width:]
    dynamics_first_gain[...] = row(3)
    dynamics_first_shift[...] = row(4)
    dynamics_second_gain[...] = row(5)
    dynamics_second_shift[...] = row(6)
    dynamics_third_gain[...] = row(7)[:, :latent_width]
    dynamics_third_shift[...] = row(7)[:, latent_width:]
    for q in range(heads):
        for k, target in enumerate((value_first_gain, value_first_shift, value_second_gain, value_second_shift)):
            target[q : q + 1, :] = head_row(q, k)
        value_bias[q : q + 1, :] = head_row(q, 4)[:, :bins]
    for k in range(table_ref.shape[0] // 8):
        block = small_ref[1 + k // 8, :, (k % 8) * 128 : (k % 8) * 128 + 128]
        table_ref[k * 8 : k * 8 + 8, :] = block[:, moves : moves + task_width]
    for copy in copies[:5]:
        copy.wait()
    for c in range(2):
        for x in range(2):
            quarter = c * 2 + x
            move(value_second.at[heads - 1], quarter * rest_rows, ga_ref[0, c, x, 0])
            move(dynamics_second, quarter * rest_rows, ga_ref[1, c, x, 0])
            move(dynamics_third, quarter * rest_rows, ga_ref[2, c, x, 0, :, :latent_width])
            move(encoder_second, quarter * rest_rows, ga_ref[2, c, x, 0, :, latent_width:])
            move(encoder_first, quarter * ge_ref.shape[3], ge_ref[c, x, 0])
            move(dynamics_first, quarter * part_rows, gb_ref[1, c, x, 0])
            for k in range(own_heads):
                for i in range(2):
                    move(value_second.at[x * own_heads + k], (c * 2 + i) * rest_rows, ga_pair_ref[k, c, x, i])

    def lanes(head, quarter, block):
        first = quarter * part_rows
        move(value_first.at[head], first, block)
        if first + part_rows > third_at:
            move(value_third.at[head], 0, block[third_at - first :])

    for quarter in range(4):
        lanes(heads - 1, quarter, gb_ref[0, quarter // 2, quarter % 2, 0])
        for x in range(2):
            for k in range(own_heads):
                lanes(x * own_heads + k, quarter, gb_pair_ref[k, quarter // 2, x, quarter % 2])


def mish_curve(values):
    return values * jnp.tanh(jax.nn.softplus(values))


def layer_norm(before, gain_vec, shift_vec):
    center = before - jnp.mean(before, -1, keepdims=True)
    spread = jnp.mean(center * center, -1, keepdims=True)
    return center * lax.rsqrt(spread + epsilon) * gain_vec + shift_vec


def sim_norm(values):
    groups = values.reshape(values.shape[:-1] + (values.shape[-1] // SIMNORM, SIMNORM))
    return jax.nn.softmax(groups, -1).reshape(values.shape)


def post_mish(before, gain_vec, shift_vec):
    return mish_curve(layer_norm(before, gain_vec, shift_vec))


def post_simnorm(before, gain_vec, shift_vec):
    return sim_norm(layer_norm(before, gain_vec, shift_vec))


def head_mish(before, gain_vec, shift_vec):
    return post_mish(before, gain_vec[:, None, :], shift_vec[:, None, :])


def matmul(left_side, right_side):
    return jnp.dot(left_side, right_side, preferred_element_type=jnp.float32)


def left_transposed(left_side, right_side):
    return lax.dot_general(
        left_side, right_side, (((0,), (0,)), ((), ())), preferred_element_type=jnp.float32
    )


def right_transposed(left_side, right_side):
    return lax.dot_general(
        left_side, right_side, (((1,), (1,)), ((), ())), preferred_element_type=jnp.float32
    )


def dense_forward(inputs, weight, gain_vec, shift_vec, after_fn):
    before = matmul(inputs, weight)
    return jax.vjp(after_fn, before, gain_vec.astype(jnp.float32), shift_vec.astype(jnp.float32))


def dense_backward(inputs, weight, puller, upstream):
    delta_before, delta_gain, delta_shift = puller(upstream)
    rounded = delta_before.astype(jnp.bfloat16)
    return (
        right_transposed(rounded, weight),
        left_transposed(inputs, rounded),
        delta_gain,
        delta_shift,
    )


def encoder_forward(encoder_params, observed, embedded):
    inputs = jnp.concatenate([observed, embedded], 1)
    hidden, first_pull = dense_forward(
        inputs, encoder_params[0], encoder_params[1], encoder_params[2], post_mish
    )
    hidden_low = hidden.astype(jnp.bfloat16)
    latent, second_pull = dense_forward(
        hidden_low, encoder_params[3], encoder_params[4], encoder_params[5], post_simnorm
    )
    return (latent, (inputs, hidden_low, first_pull, second_pull))


def encoder_backward(encoder_params, retained, upstream):
    inputs, hidden_low, first_pull, second_pull = retained
    delta_hidden, delta_second, second_gain, second_shift = dense_backward(
        hidden_low, encoder_params[3], second_pull, upstream
    )
    delta_inputs, delta_first, first_gain, first_shift = dense_backward(
        inputs, encoder_params[0], first_pull, delta_hidden
    )
    return (
        delta_inputs,
        (delta_first, first_gain, first_shift, delta_second, second_gain, second_shift),
    )


def dynamics_forward(dynamics_params, latent_in, action_low, embedded):
    inputs = jnp.concatenate([latent_in, action_low, embedded], 1)
    layer_one, first_pull = dense_forward(
        inputs, dynamics_params[0], dynamics_params[1], dynamics_params[2], post_mish
    )
    one_low = layer_one.astype(jnp.bfloat16)
    layer_two, second_pull = dense_forward(
        one_low, dynamics_params[3], dynamics_params[4], dynamics_params[5], post_mish
    )
    two_low = layer_two.astype(jnp.bfloat16)
    latent, third_pull = dense_forward(
        two_low, dynamics_params[6], dynamics_params[7], dynamics_params[8], post_simnorm
    )
    return (latent, (inputs, one_low, two_low, first_pull, second_pull, third_pull))


def dynamics_backward(dynamics_params, retained, upstream):
    inputs, one_low, two_low, first_pull, second_pull, third_pull = retained
    delta_two, delta_third, third_gain, third_shift = dense_backward(
        two_low, dynamics_params[6], third_pull, upstream
    )
    delta_one, delta_second, second_gain, second_shift = dense_backward(
        one_low, dynamics_params[3], second_pull, delta_two
    )
    delta_inputs, delta_first, first_gain, first_shift = dense_backward(
        inputs, dynamics_params[0], first_pull, delta_one
    )
    return (
        delta_inputs,
        (
            delta_first,
            first_gain,
            first_shift,
            delta_second,
            second_gain,
            second_shift,
            delta_third,
            third_gain,
            third_shift,
        ),
    )


def value_backward(value_params, inputs, bin_rows, fraction_rows, factor):
    first_before = jnp.einsum(
        "rk,qkn->qrn", inputs, value_params[0], preferred_element_type=jnp.float32
    )
    layer_one, first_pull = jax.vjp(
        head_mish,
        first_before,
        value_params[1].astype(jnp.float32),
        value_params[2].astype(jnp.float32),
    )
    one_low = layer_one.astype(jnp.bfloat16)
    second_before = jnp.einsum(
        "qrk,qkn->qrn", one_low, value_params[3], preferred_element_type=jnp.float32
    )
    layer_two, second_pull = jax.vjp(
        head_mish,
        second_before,
        value_params[4].astype(jnp.float32),
        value_params[5].astype(jnp.float32),
    )
    two_low = layer_two.astype(jnp.bfloat16)
    logits = (
        jnp.einsum("qrk,qkn->qrn", two_low, value_params[6], preferred_element_type=jnp.float32)
        + value_params[7].astype(jnp.float32)[:, None, :]
    )
    chances = jax.nn.softmax(logits, -1)
    columns = lax.broadcasted_iota(jnp.int32, (1, logits.shape[2]), 1)
    lower_bin = bin_rows[:, None]
    target = (1.0 - fraction_rows)[:, None] * (columns == lower_bin).astype(
        jnp.float32
    ) + fraction_rows[:, None] * (columns == lower_bin + 1).astype(jnp.float32)
    delta_logits = factor[None, :, None] * (chances - target[None])
    logit_low = delta_logits.astype(jnp.bfloat16)
    delta_bias = jnp.sum(delta_logits, 1)
    delta_third = jnp.einsum("qrk,qrn->qkn", two_low, logit_low, preferred_element_type=jnp.float32)
    delta_two = jnp.einsum(
        "qrn,qkn->qrk", logit_low, value_params[6], preferred_element_type=jnp.float32
    )
    before_two, second_gain, second_shift = second_pull(delta_two)
    two_round = before_two.astype(jnp.bfloat16)
    delta_second = jnp.einsum(
        "qrk,qrn->qkn", one_low, two_round, preferred_element_type=jnp.float32
    )
    delta_one = jnp.einsum(
        "qrn,qkn->qrk", two_round, value_params[3], preferred_element_type=jnp.float32
    )
    before_one, first_gain, first_shift = first_pull(delta_one)
    one_round = before_one.astype(jnp.bfloat16)
    delta_first = jnp.einsum("rk,qrn->qkn", inputs, one_round, preferred_element_type=jnp.float32)
    delta_inputs = jnp.einsum(
        "qrn,qkn->rk", one_round, value_params[0], preferred_element_type=jnp.float32
    )
    return (
        delta_inputs,
        (
            delta_first,
            first_gain,
            first_shift,
            delta_second,
            second_gain,
            second_shift,
            delta_third,
            delta_bias,
        ),
    )


def reduce_end(gradients):
    def reduced(index, axis):
        shard = lax.psum_scatter(
            gradients[index].astype(jnp.bfloat16), "dp", scatter_dimension=axis, tiled=True
        )
        return lax.psum(shard, "section").astype(jnp.float32)

    return tuple(
        reduced(index, axis)
        for index, axis in ((0, 1), (3, 0), (6, 1), (9, 0), (12, 0), (15, 2), (18, 1), (21, 1))
    )


def plain_device(
    observations,
    actions,
    action_mask,
    task_ids,
    targets,
    bin_low,
    bin_frac,
    task_table,
    encoder_first,
    encoder_first_gain,
    encoder_first_shift,
    encoder_second,
    encoder_second_gain,
    encoder_second_shift,
    dynamics_first,
    dynamics_first_gain,
    dynamics_first_shift,
    dynamics_second,
    dynamics_second_gain,
    dynamics_second_shift,
    dynamics_third,
    dynamics_third_gain,
    dynamics_third_shift,
    value_first,
    value_first_gain,
    value_first_shift,
    value_second,
    value_second_gain,
    value_second_shift,
    value_third,
    value_bias,
):
    encoder_params = (
        encoder_first,
        encoder_first_gain,
        encoder_first_shift,
        encoder_second,
        encoder_second_gain,
        encoder_second_shift,
    )
    dynamics_params = (
        dynamics_first,
        dynamics_first_gain,
        dynamics_first_shift,
        dynamics_second,
        dynamics_second_gain,
        dynamics_second_shift,
        dynamics_third,
        dynamics_third_gain,
        dynamics_third_shift,
    )
    value_params = (
        value_first,
        value_first_gain,
        value_first_shift,
        value_second,
        value_second_gain,
        value_second_shift,
        value_third,
        value_bias,
    )
    sections = lax.axis_size("section")
    level_now = lax.axis_index("section")
    micro_total = observations.shape[0]
    share = micro_total // sections
    latent_width = dynamics_third.shape[1]
    action_width = actions.shape[3]
    observed_width = observations.shape[2]
    horizon = actions.shape[0]
    heads = value_first.shape[0]
    task_count = task_table.shape[0]

    def mine(array, axis):
        part = lax.dynamic_slice_in_dim(array, level_now * share, share, axis)
        shape = part.shape
        return part.reshape(shape[:axis] + (shape[axis] * shape[axis + 1],) + shape[axis + 2 :])

    observed = mine(observations, 0)
    movement = mine(actions, 1)
    task_rows = mine(task_ids, 0)
    goals = mine(targets, 1)
    low_bins = mine(bin_low, 1)
    fractions = mine(bin_frac, 1)
    rows = observed.shape[0]
    onehot = (task_rows[:, None] == lax.broadcasted_iota(jnp.int32, (1, task_count), 1)).astype(
        jnp.bfloat16
    )
    embedded = matmul(onehot, task_table).astype(jnp.bfloat16)
    allowed = matmul(onehot, action_mask.astype(jnp.bfloat16))
    chosen = (movement.astype(jnp.float32) * allowed[None]).astype(jnp.bfloat16)

    latent, encoder_kept = encoder_forward(encoder_params, observed, embedded)
    latents = [latent]
    dynamics_kept = []
    for step in range(horizon):
        latent, kept = dynamics_forward(
            dynamics_params, latents[step].astype(jnp.bfloat16), chosen[step], embedded
        )
        latents.append(latent)
        dynamics_kept.append(kept)
    inputs = jnp.concatenate([kept[0] for kept in dynamics_kept], 0)
    step_weight = jnp.asarray(
        [value_weight * discount**step / (heads * micro_total) for step in range(horizon)],
        jnp.float32,
    )
    value_delta, value_grads = value_backward(
        value_params,
        inputs,
        low_bins.reshape(-1),
        fractions.reshape(-1),
        jnp.repeat(step_weight, rows),
    )
    value_delta = value_delta.reshape(horizon, rows, -1)
    upstream = jnp.zeros((rows, latent_width), jnp.float32)
    embed_delta = jnp.sum(value_delta[:, :, latent_width + action_width :], 0)
    dynamics_grads = None
    for step in reversed(range(horizon)):
        factor = 2.0 * consistency_weight * discount**step / (micro_total * latent_width)
        upstream = upstream + factor * (latents[step + 1] - goals[step].astype(jnp.float32))
        inputs_delta, step_grads = dynamics_backward(dynamics_params, dynamics_kept[step], upstream)
        dynamics_grads = (
            step_grads
            if dynamics_grads is None
            else tuple(a + b for a, b in zip(dynamics_grads, step_grads))
        )
        embed_delta = embed_delta + inputs_delta[:, latent_width + action_width :]
        upstream = (
            inputs_delta[:, :latent_width].astype(jnp.bfloat16).astype(jnp.float32)
            + value_delta[step, :, :latent_width]
        )
    inputs_delta, encoder_grads = encoder_backward(encoder_params, encoder_kept, upstream)
    observed_delta = inputs_delta[:, :observed_width]
    embed_delta = embed_delta + inputs_delta[:, observed_width:]
    table_sum = left_transposed(onehot.astype(jnp.float32), embed_delta)
    totals = encoder_grads + dynamics_grads + value_grads
    matrices = reduce_end(totals)
    small_sums = lax.psum(
        tuple(totals[i] for i in (1, 2, 4, 5, 7, 8, 10, 11, 13, 14, 16, 17, 19, 20, 22))
        + (table_sum,),
        ("section", "dp"),
    )
    return (
        observed_delta.reshape(share, rows // share, observed_width),
        small_sums[15],
        matrices[0],
        small_sums[0],
        small_sums[1],
        matrices[1],
        small_sums[2],
        small_sums[3],
        matrices[2],
        small_sums[4],
        small_sums[5],
        matrices[3],
        small_sums[6],
        small_sums[7],
        matrices[4],
        small_sums[8],
        small_sums[9],
        matrices[5],
        small_sums[10],
        small_sums[11],
        matrices[6],
        small_sums[12],
        small_sums[13],
        matrices[7],
        small_sums[14],
    )


def step_device(
    observations,
    actions,
    action_mask,
    task_ids,
    targets,
    bin_low,
    bin_frac,
    task_table,
    encoder_first,
    encoder_first_gain,
    encoder_first_shift,
    encoder_second,
    encoder_second_gain,
    encoder_second_shift,
    dynamics_first,
    dynamics_first_gain,
    dynamics_first_shift,
    dynamics_second,
    dynamics_second_gain,
    dynamics_second_shift,
    dynamics_third,
    dynamics_third_gain,
    dynamics_third_shift,
    value_first,
    value_first_gain,
    value_first_shift,
    value_second,
    value_second_gain,
    value_second_shift,
    value_third,
    value_bias,
):
    horizon, micro_total, rows, moves = actions.shape
    tasks, task_width = task_table.shape
    heads, inputs, hidden = value_first.shape
    latent_width = dynamics_third.shape[1]
    observed = observations.shape[2]
    bins = value_third.shape[2]
    enc_rows = ceil_to(observed + task_width, 256)
    in_rows = latent_width + 128
    total = horizon * rows
    ranks = hidden // 128
    sizes = (micro_total, observed, moves, task_width, bins, heads)
    part_rows = (in_rows + 128) // 4
    rest_rows = hidden // (ranks * 4)
    enc_part = ceil_to(observed + task_width, 64) // 4
    chain = 1 + 2 * horizon
    pair = heads // 2
    vmem, anywhere = pl.BlockSpec(memory_space=pltpu.VMEM), pl.BlockSpec(memory_space=pl.ANY)
    names = len(ORDERS) + 3

    def gathered(count, blocks, block_rows, width):
        return (count, 2, 2, blocks, block_rows, width)

    shapes = (
        gathered(3, 1, rest_rows, hidden),
        gathered(pair, 2, rest_rows, hidden),
        gathered(2, 1, part_rows, 128),
        gathered(pair, 2, part_rows, 128),
        gathered(1, 1, enc_part, 128)[1:],
    )
    f32, bf16 = (lambda *shape: pltpu.VMEM(shape, F32)), (lambda *shape: pltpu.VMEM(shape, BF16))
    outs = pl.pallas_call(
        functools.partial(step_kernel, sizes),
        out_shape=tuple(jax.ShapeDtypeStruct(shape, BF16) for shape in shapes)
        + (
            jax.ShapeDtypeStruct((4, 8, hidden), F32),
            jax.ShapeDtypeStruct((4, 16, hidden), F32),
            jax.ShapeDtypeStruct((observed, rows), F32),
        ),
        in_specs=[vmem] * 22 + [anywhere] * 9,
        out_specs=[anywhere] * 5 + [vmem] * 3,
        scratch_shapes=[
            bf16(horizon, rows, latent_width),
            bf16(observed + task_width, hidden),
            bf16(enc_rows, hidden),
            bf16(hidden, latent_width),
            bf16(inputs, hidden),
            bf16(128, hidden),
            bf16(hidden, hidden),
            bf16(hidden, latent_width),
            bf16(inputs, hidden),
            bf16(128, hidden),
            bf16(hidden, hidden),
            bf16(bins, hidden),
            bf16(128, hidden),
            bf16(rows, enc_rows),
            bf16(2 * total, in_rows),
            bf16(total, in_rows),
            f32(enc_rows, rows),
            bf16(2, tasks, rows),
            f32(2 * total, 128),
            f32(8 * (heads + 1), hidden),
            bf16(chain, rows, hidden),
            bf16(chain, rows, hidden),
            f32(chain, rows, 128),
            bf16(chain * rows, hidden),
            bf16(horizon + 1, rows, latent_width),
            f32(horizon + 1, rows, latent_width),
            f32(horizon + 1, rows, 128),
            bf16(total, latent_width),
        ]
        + [bf16(total, hidden), bf16(total, hidden), f32(total, 128)]
        + [bf16(total, hidden)] * 4
        + [
            f32(rows, hidden),
            f32(rows, hidden),
            f32(total, hidden),
            f32(rows, latent_width),
            f32(2, 8, hidden),
            bf16(total, hidden),
            bf16(total, 128),
            f32(2 * total, in_rows),
            bf16(horizon, rows, latent_width),
            bf16(horizon, rows, latent_width),
            bf16(32, rest_rows, hidden),
            bf16(32, part_rows, 128),
            bf16(32, enc_part, 128),
            bf16(2, 16, rest_rows, hidden),
            bf16(16, part_rows, 128),
            bf16(16, enc_part, 128),
            [bf16(5, 8 >> k, rest_rows, hidden) for k in range(4)],
            [bf16(4, 8 >> k, part_rows, 128) for k in range(4)],
            [bf16(8 >> k, enc_part, 128) for k in range(4)],
            *(bf16(*shape) for shape in shapes),
            f32(4, 8, hidden),
            [f32(2, 8, hidden)] + [f32(8, hidden)] * 4,
            f32(4, 8, hidden),
            f32(4, 16, hidden),
            [f32(2, 16, hidden)] + [f32(16, hidden)] * 4,
            f32(4, 16, hidden),
            pltpu.SemaphoreType.DMA((5,)),
            pltpu.SemaphoreType.DMA((horizon,)),
            pltpu.SemaphoreType.DMA((3,)),
            pltpu.SemaphoreType.DMA((5,)),
            pltpu.SemaphoreType.DMA((names, 7)),
            pltpu.SemaphoreType.DMA((names, 7)),
            pltpu.SemaphoreType.REGULAR((5,)),
        ],
        compiler_params=pltpu.CompilerParams(
            collective_id=0, has_side_effects=True, vmem_limit_bytes=KERNEL_VMEM
        ),
    )(
        observations.transpose(2, 0, 1),
        actions.transpose(0, 3, 1, 2),
        task_ids,
        bin_low,
        bin_frac,
        action_mask.T,
        task_table,
        encoder_first_gain,
        encoder_first_shift,
        encoder_second_gain,
        encoder_second_shift,
        dynamics_first_gain,
        dynamics_first_shift,
        dynamics_second_gain,
        dynamics_second_shift,
        dynamics_third_gain,
        dynamics_third_shift,
        value_first_gain,
        value_first_shift,
        value_second_gain,
        value_second_shift,
        value_bias,
        targets,
        encoder_first,
        encoder_second,
        dynamics_first,
        dynamics_second,
        dynamics_third,
        value_first,
        value_second,
        value_third.transpose(0, 2, 1),
    )

    def like(*shape):
        return jax.ShapeDtypeStruct(shape, F32)

    done = pl.pallas_call(
        functools.partial(finish_kernel, sizes),
        out_shape=(
            like(observed, 1, rows),
            like(tasks, task_width),
            like(observed + task_width, 128),
            like(1, hidden),
            like(1, hidden),
            like(128, latent_width),
            like(1, latent_width),
            like(1, latent_width),
            like(inputs, 128),
            like(1, hidden),
            like(1, hidden),
            like(128, hidden),
            like(1, hidden),
            like(1, hidden),
            like(128, latent_width),
            like(1, latent_width),
            like(1, latent_width),
            like(heads, inputs, 128),
            like(heads, hidden),
            like(heads, hidden),
            like(heads, 128, hidden),
            like(heads, hidden),
            like(heads, hidden),
            like(heads, bins, 128),
            like(heads, bins),
        ),
        in_specs=[anywhere] * 8,
        out_specs=[vmem] * 25,
        scratch_shapes=[
            *(bf16(*shape) for shape in shapes),
            f32(4, 8, hidden),
            f32(4, 16, hidden),
            f32(observed, rows),
            pltpu.SemaphoreType.DMA((8,)),
        ],
        compiler_params=pltpu.CompilerParams(vmem_limit_bytes=FINISH_VMEM),
    )(*outs)
    done = [item.reshape(-1) if item.shape[0] == 1 else item for item in done]
    done[0] = done[0].transpose(1, 2, 0)
    done[23] = done[23].transpose(0, 2, 1)
    return tuple(done)


def solution(mesh):
    in_specs = (
        P(None, "dp", None),
        P(None, None, "dp", None),
        P(),
        P(None, "dp"),
        P(None, None, "dp", None),
        P(None, None, "dp"),
        P(None, None, "dp"),
    ) + (P(),) * 24
    out_specs = (
        P("section", "dp", None),
        P(),
        P(None, "dp"),
        P(),
        P(),
        P("dp", None),
        P(),
        P(),
        P(None, "dp"),
        P(),
        P(),
        P("dp", None),
        P(),
        P(),
        P("dp", None),
        P(),
        P(),
        P(None, None, "dp"),
        P(),
        P(),
        P(None, "dp", None),
        P(),
        P(),
        P(None, "dp", None),
        P(),
    )
    paired = (mesh.shape["section"], mesh.shape["dp"]) == (4, 8)
    return jax.shard_map(
        step_device if paired else plain_device,
        mesh=mesh,
        in_specs=in_specs,
        out_specs=out_specs,
        check_vma=False,
    )
```
